256 devices in a mesh: grp: 8 (over z_hi, core), dev: 32 (over y, z_lo, x).
Axes of the slice: x: 4, y: 4, z: 8 (z_hi: 4, z_lo: 2; z = z_hi * 2 + z_lo), core: 2. Of those that a mesh axis runs over, the one named last changes fastest.
Arguments:
- forcing: float32 [4, 32, 512, 256], P(None, 'grp', 'dev'), may hold values from -6 to 6
- viscosity: float32 [32, 512, 256], P('grp', 'dev'), may hold values from 0.0316 to 31.6
Outputs:
- solution: float32 [4, 32, 512, 256], P(None, 'grp', 'dev')
- final_residual: float32 [4, 32, 512, 256], P(None, 'grp', 'dev')
The draws below stay inside these ranges and needn't reach their ends.
All inputs are finite; a program needn't handle non-finite values.
Results may differ from the reference program's by a relative error of at most 0.00002.
Values sent between devices are 32-bit elements; how exact they have to be, the bound alone decides.
No kernel may reach another device: no remote copies, remote signals or barrier semaphores. Data moves between devices by JAX's collectives and lax.ppermute only.
A program may use at most 64 MiB of HBM per device.

```python
import math
import jax
import jax.numpy as jnp

NZ = 256
NU = 2
COARSE = 6
NX = 32
NY = 512


def shard_levels(own_key, shape, cuts, least, largest):
    def one(dim, blocks):
        steps = jax.random.uniform(jax.random.fold_in(jax.random.fold_in(own_key, 6), dim), (blocks,), jnp.float32, least / len(cuts), largest / len(cuts))
        return jnp.repeat(jnp.exp(steps), shape[dim] // blocks).reshape((-1,) + (1,) * (len(shape) - dim - 1))

    level = one(*cuts[0])
    for cut in cuts[1:]:
        level = level * one(*cut)
    return level


def gaussian(own_key, shape, deviation, most, shards=(), held_as=jnp.bfloat16):
    factor_of = shard_levels(own_key, shape, shards, -0.22, 0.18) if shards else 1.0
    drawn = jax.random.normal(own_key, shape, jnp.float32) * deviation * factor_of
    return jnp.minimum(jnp.maximum(drawn, -most), most).astype(held_as)


def setup_inputs(seed: int = 0) -> dict:
    arg_keys = jax.random.split(jax.random.key(seed), 3)
    forcing = gaussian(arg_keys[0], (4, NX, NY, NZ), 1.0, 6.0, ((1, 8), (2, 32)), jnp.float32)
    viscosity = jnp.clip(jnp.exp(math.log(31.6) - 6.9077553 * jax.random.uniform(arg_keys[1], (NX, NY, NZ), jnp.float32) ** shard_levels(arg_keys[1], (NX, NY, NZ), ((0, 8), (1, 32)), -0.2, 0.2)), 0.0316, 31.6)
    return dict(forcing=forcing, viscosity=viscosity)


OMEGA = 0.6
BETA = 0.25


def zero_pad(array):
    return jnp.pad(array, ((0, 0), (1, 1), (1, 1), (1, 1)))


def neighbours_of(padded):
    return [padded[:, 2:, 1:-1, 1:-1], padded[:, :-2, 1:-1, 1:-1],
            padded[:, 1:-1, 2:, 1:-1], padded[:, 1:-1, :-2, 1:-1],
            padded[:, 1:-1, 1:-1, 2:], padded[:, 1:-1, 1:-1, :-2]]


def prepare(viscous, spacing, pad_rule):
    neighbours = neighbours_of(pad_rule(viscous))
    faces = [(viscous + other) * 0.5 for other in neighbours]
    total = faces[0]
    for face in faces[1:]:
        total = total + face
    diagonal = total / (spacing * spacing)
    weight = jnp.concatenate([jnp.broadcast_to(OMEGA / diagonal, (3,) + diagonal.shape[1:]), BETA * viscous], axis=0)
    return faces, weight


def operate(field, faces, spacing, padded):
    neighbours = neighbours_of(padded)
    total = faces[0] * (field[:3] - neighbours[0][:3])
    for index in range(1, 6):
        total = total + faces[index] * (field[:3] - neighbours[index][:3])
    gradient = jnp.concatenate([neighbours[0][3:4] - neighbours[1][3:4],
                                neighbours[2][3:4] - neighbours[3][3:4],
                                neighbours[4][3:4] - neighbours[5][3:4]], axis=0)
    velocity = total / (spacing * spacing) + gradient / (2.0 * spacing)
    divergence = (neighbours[0][0:1] - neighbours[1][0:1]) + (neighbours[2][1:2] - neighbours[3][1:2]) + (neighbours[4][2:3] - neighbours[5][2:3])
    return jnp.concatenate([velocity, divergence / (2.0 * spacing)], axis=0)


def residual_of(source, field, faces, spacing, pad_rule):
    return source - operate(field, faces, spacing, pad_rule(field))


def smooth(source, field, faces, weight, spacing, pad_rule, count):
    for sweep in range(count):
        field = field + weight * residual_of(source, field, faces, spacing, pad_rule)
    return field


def restrict(array):
    comps, xsize, ysize, zsize = array.shape
    return array.reshape(comps, xsize // 2, 2, ysize // 2, 2, zsize // 2, 2).mean(axis=(2, 4, 6))


def prolong(array):
    return jnp.repeat(jnp.repeat(jnp.repeat(array, 2, axis=1), 2, axis=2), 2, axis=3)


def reference(forcing, viscosity):
    viscous = viscosity[None]
    faces_fine, weight_fine = prepare(viscous, 1.0, zero_pad)
    field = weight_fine * forcing
    field = smooth(forcing, field, faces_fine, weight_fine, 1.0, zero_pad, NU - 1)
    source_mid = restrict(residual_of(forcing, field, faces_fine, 1.0, zero_pad))
    viscous_mid = restrict(viscous)
    faces_mid, weight_mid = prepare(viscous_mid, 2.0, zero_pad)
    update_mid = weight_mid * source_mid
    update_mid = smooth(source_mid, update_mid, faces_mid, weight_mid, 2.0, zero_pad, NU - 1)
    source_low = restrict(residual_of(source_mid, update_mid, faces_mid, 2.0, zero_pad))
    viscous_low = restrict(viscous_mid)
    faces_low, weight_low = prepare(viscous_low, 4.0, zero_pad)
    update_low = weight_low * source_low
    update_low = smooth(source_low, update_low, faces_low, weight_low, 4.0, zero_pad, COARSE - 1)
    update_mid = update_mid + prolong(update_low)
    update_mid = smooth(source_mid, update_mid, faces_mid, weight_mid, 2.0, zero_pad, NU)
    field = field + prolong(update_mid)
    field = smooth(forcing, field, faces_fine, weight_fine, 1.0, zero_pad, NU)
    return field, residual_of(forcing, field, faces_fine, 1.0, zero_pad)
```

```python
import jax
import jax.numpy as jnp
from jax import lax
from jax.experimental import pallas as pl
from jax.experimental.pallas import tpu as pltpu
from jax.sharding import PartitionSpec as P

COARSE = 6
OMEGA = 0.6
BETA = 0.25
F32 = jnp.float32
VMEM_LIMIT = 48 * 1024 * 1024


def shifts(value, step):
    rows, lanes = value.shape
    lane = lax.broadcasted_iota(jnp.int32, (rows, 128), 1)
    if lanes == 256:
        low, high = value[:, :128], value[:, 128:]
        low_up, high_up = pltpu.roll(low, 127, 1), pltpu.roll(high, 127, 1)
        low_dn, high_dn = pltpu.roll(low, 1, 1), pltpu.roll(high, 1, 1)
        last, first = lane == 127, lane == 0
        plus = jnp.concatenate([jnp.where(last, high_up, low_up), jnp.where(last, 0.0, high_up)], 1)
        minus = jnp.concatenate([jnp.where(first, 0.0, low_dn), jnp.where(first, low_dn, high_dn)], 1)
        return plus, minus
    plus = jnp.where(lane >= 128 - step, 0.0, pltpu.roll(value, 128 - step, 1))
    minus = jnp.where(lane < step, 0.0, pltpu.roll(value, step, 1))
    return plus, minus


def around(load, layer, row, step):
    here = load(layer, row)
    return here, [load(layer + 1, row), load(layer - 1, row), load(layer, row + 1), load(layer, row - 1), *shifts(here, step)]


def sums_of(visc, layer, row, step):
    here, near = around(lambda i, r: visc[i, pl.ds(r, 8), :], layer, row, step)
    sums = [here + other for other in near]
    return here, sums, sum(sums[1:], sums[0])


def stencil(field, layer, row, step, sums):
    here, flux, grad, div = [], [], None, None
    for comp in range(4):
        centre, near = around(lambda i, r: field[comp, i, pl.ds(r, 8), :], layer, row, step)
        here.append(centre)
        if comp < 3:
            terms = [s * n for s, n in zip(sums, near)]
            flux.append(sum(terms[1:], terms[0]))
            diff = near[2 * comp] - near[2 * comp + 1]
            div = diff if div is None else div + diff
        else:
            grad = [near[2 * c] - near[2 * c + 1] for c in range(3)]
    return here, flux, grad, div


def sweep_chunk(out, field, out_layer, layer, row, step, spacing, visc, visc_layer, weight, weight_layer, source, source_layer):
    e_here, sums, _ = sums_of(visc, visc_layer, row, step)
    here, flux, grad, div = stencil(field, layer, row, step, sums)
    w = weight[weight_layer, pl.ds(row, 8), :]
    for c in range(3):
        b = source[c, source_layer, pl.ds(row, 8), :]
        out[c, out_layer, pl.ds(row, 8), :] = (1.0 - OMEGA) * here[c] + w * (
            b + (0.5 / (spacing * spacing)) * flux[c] - (0.5 / spacing) * grad[c]
        )
    b = source[3, source_layer, pl.ds(row, 8), :]
    out[3, out_layer, pl.ds(row, 8), :] = here[3] + (BETA * e_here) * (b - (0.5 / spacing) * div)


def residual_chunk(field, layer, row, step, spacing, visc, visc_layer, source, source_layer):
    _, sums, total = sums_of(visc, visc_layer, row, step)
    here, flux, grad, div = stencil(field, layer, row, step, sums)
    out = []
    for c in range(3):
        b = source[c, source_layer, pl.ds(row, 8), :]
        out.append(b - ((0.5 / (spacing * spacing)) * (total * here[c] - flux[c]) + (0.5 / spacing) * grad[c]))
    out.append(source[3, source_layer, pl.ds(row, 8), :] - (0.5 / spacing) * div)
    return out


def start_chunk(out, out_layer, row, step, spacing, visc, visc_layer, weight, weight_layer, source, source_layer, inside):
    e_here, _, total = sums_of(visc, visc_layer, row, step)
    w = jnp.where(inside, (2.0 * OMEGA * spacing * spacing) / total, 0.0)
    weight[weight_layer, pl.ds(row, 8), :] = w
    for c in range(3):
        out[c, out_layer, pl.ds(row, 8), :] = w * source[c, source_layer, pl.ds(row, 8), :]
    out[3, out_layer, pl.ds(row, 8), :] = (BETA * e_here) * source[3, source_layer, pl.ds(row, 8), :]


def rows_inside(row, first, count, lanes):
    at = lax.broadcasted_iota(jnp.int32, (8, lanes), 0) + (row + first)
    return (at >= 0) & (at < count)


def loop(count, body):
    lax.fori_loop(0, count, lambda i, carry: (body(i), carry)[1], 0)


def fold_matrix(fine, transpose=False):
    shape = (fine // 2, fine) if transpose else (fine, fine // 2)
    a = lax.broadcasted_iota(jnp.int32, shape, 1 if transpose else 0)
    b = lax.broadcasted_iota(jnp.int32, shape, 0 if transpose else 1)
    return jnp.where(a // 2 == b, 1.0, 0.0).astype(F32)


def exact_dot(a, b):
    return jnp.dot(a, b, precision=lax.Precision.HIGHEST, preferred_element_type=F32)


def fine_down(groups, devs, idx, f, e, xm, xp, ym, yp, pay_o, x1_o, ew_o, w_o, fw_o, fw, ew, wt, x0, x1, pair, half):
    g, d = idx[0], idx[1]
    zero8 = jnp.zeros((8, 256), F32)
    low_x, high_x = jnp.where(g > 0, 1.0, 0.0), jnp.where(g < groups - 1, 1.0, 0.0)
    low_y, high_y = jnp.where(d > 0, 1.0, 0.0), jnp.where(d < devs - 1, 1.0, 0.0)

    def scale_of(layer):
        return low_x if layer < 3 else high_x if layer > 6 else 1.0

    for layer in range(10):
        for row in (0, 40):
            ew[layer, row : row + 8, :] = zero8
        own = xm[8 + layer] if layer < 3 else xp[8 + layer - 7] if layer > 6 else e[layer - 3]
        s = scale_of(layer)
        ew[layer, 16:32, :] = own * s
        ew[layer, 8:16, :] = ym[192 + 8 * layer : 200 + 8 * layer, :] * (s * low_y)
        ew[layer, 32:40, :] = yp[192 + 8 * layer : 200 + 8 * layer, :] * (s * high_y)
    for layer in range(8):
        for c in range(4):
            own = xm[2 * c + layer] if layer < 2 else xp[2 * c + layer - 6] if layer > 5 else f[c, layer - 2]
            fw[c, layer, 16:32, :] = own
            fw[c, layer, 8:16, :] = zero8
            fw[c, layer, 32:40, :] = zero8
            at = 24 * layer + 6 * c
            fw[c, layer, 10:16, :] = ym[at : at + 6, :]
            fw[c, layer, 32:38, :] = yp[at : at + 6, :]
    for layer in range(8):
        for c in range(4):
            for row in (0, 40):
                x0[c, layer, row : row + 8, :] = zero8
                x1[c, layer, row : row + 8, :] = zero8

    def start(i):
        layer_in = (4 * g - 2 + i >= 0) & (4 * g - 2 + i < 4 * groups)
        for row in (8, 16, 24, 32):
            inside = rows_inside(row, 16 * d - 16, 16 * devs, 256) & layer_in
            start_chunk(x0, i, row, 1, 1.0, ew, i + 1, wt, i, fw, i, inside)

    loop(8, start)

    def sweep(i):
        for row in (8, 16, 24, 32):
            sweep_chunk(x1, x0, i + 1, i + 1, row, 1, 1.0, ew, i + 2, wt, i + 1, fw, i + 1)

    loop(6, sweep)

    def restrict(m):
        for row in (8, 16, 24, 32):
            a = residual_chunk(x1, 2 * m + 2, row, 1, 1.0, ew, 2 * m + 3, fw, 2 * m + 2)
            b = residual_chunk(x1, 2 * m + 3, row, 1, 1.0, ew, 2 * m + 4, fw, 2 * m + 3)
            for c in range(4):
                pair[2 * c + m, row - 8 : row, :] = a[c] + b[c]
            pair[8 + m, row - 8 : row, :] = ew[2 * m + 3, pl.ds(row, 8), :] + ew[2 * m + 4, pl.ds(row, 8), :]

    loop(2, restrict)
    half[...] = exact_dot(pair[...].reshape(320, 256), fold_matrix(256)) * 0.125
    coarse = half[pl.ds(0, 160, stride=2), :] + half[pl.ds(1, 160, stride=2), :]
    coarse = coarse.reshape(10, 16, 128)
    for m in range(2):
        lanes = slice(128 * m, 128 * m + 128)
        for c in range(4):
            pay_o[12 * c : 12 * c + 12, lanes] = coarse[2 * c + m, 2:14, :]
        pay_o[48:64, lanes] = coarse[8 + m]
    for c in range(4):
        for j in range(2):
            at = 64 + 18 * (2 * c + j)
            pay_o[at : at + 18, :] = x1[c, 3 + j, 15:33, :]
    x1_o[...] = x1[:, 1:7, 8:40, :]
    ew_o[...] = ew[:, 8:40, :]
    w_o[...] = wt[:, 8:40, :]
    fw_o[...] = fw[:, :, 8:40, :]


def mid_down(groups, devs, idx, own, partner, xr, c2, s3, up_o, dn_o, low_o, y_o, b_o, e_o, w_o, bw, ew, wt, y0, y1, pair, low):
    g, d = idx[0], idx[1]
    chips = groups // 2
    chip, core = g // 2, g % 2
    other = 1 - core
    beside = (chip + chips - 1 + 2 * core) % chips
    across = (chip + 1 + (chips - 2) * core) % chips
    far = (chip + 2) % chips
    zero8 = jnp.zeros((8, 128), F32)

    def clear(i):
        for row in (0, 8, 16, 24):
            ew[i, row : row + 8, :] = zero8
            wt[i, row : row + 8, :] = zero8
            for c in range(4):
                bw[c, i, row : row + 8, :] = zero8
                y0[c, i, row : row + 8, :] = zero8
                y1[c, i, row : row + 8, :] = zero8

    loop(2 * groups + 8, clear)

    def place(block, at, which, core_at):
        base = 4 + 4 * which + 2 * core_at
        for m in range(2):
            lanes = slice(128 * m, 128 * m + 128)
            for c in range(4):
                bw[c, base + m, 10:22, :] = block[at + 12 * c : at + 12 * c + 12, lanes]
            ew[base + m, 8:24, :] = block[at + 48 : at + 64, lanes]

    place(own, 0, chip, core)
    place(partner, 0, chip, other)
    place(xr, 0, beside, other)
    place(xr, 208, beside, core)
    place(s3, 0, across, core)
    place(s3, 64, across, other)
    place(c2, 0, far, core)
    place(s3, 128, far, other)

    def start(i):
        for row in (8, 16):
            inside = rows_inside(row, 8 * d - 12, 8 * devs, 128)
            start_chunk(y0, i + 4, row, 1, 2.0, ew, i + 4, wt, i + 4, bw, i + 4, inside)

    loop(2 * groups, start)

    def sweep(i):
        for row in (8, 16):
            sweep_chunk(y1, y0, i + 4, i + 4, row, 1, 2.0, ew, i + 4, wt, i + 4, bw, i + 4)

    loop(2 * groups, sweep)
    lane = lax.broadcasted_iota(jnp.int32, (4, 128), 1)

    def restrict(m):
        at = 2 * m + 4
        for row in (8, 16):
            a = residual_chunk(y1, at, row, 1, 2.0, ew, at, bw, at)
            b = residual_chunk(y1, at + 1, row, 1, 2.0, ew, at + 1, bw, at + 1)
            for c in range(4):
                pair[c, row - 8 : row, :] = a[c] + b[c]
            pair[4, row - 8 : row, :] = ew[at, pl.ds(row, 8), :] + ew[at + 1, pl.ds(row, 8), :]
        for c in range(5):
            rows = pair[c, pl.ds(4, 4, stride=2), :] + pair[c, pl.ds(5, 4, stride=2), :]
            mate = jnp.where(lane % 2 == 0, pltpu.roll(rows, 127, 1), pltpu.roll(rows, 1, 1))
            low[c, m, 0:4, :] = (rows + mate) * 0.125

    loop(groups, restrict)
    for c in range(5):
        for q in range(groups // 2):
            packed = jnp.where(lane % 2 == 0, low[c, 2 * q, 0:4, :], low[c, 2 * q + 1, 0:4, :])
            at = 4 * (c * (groups // 2) + q)
            for out in (up_o, dn_o, low_o):
                out[at : at + 4, :] = packed
    base = 20 * (groups // 2)
    for c in range(4):
        for j in range(6):
            at = base + 4 * (6 * c + j)
            up_o[at : at + 4, :] = y1[c, 2 * g + 2 + j, 16:20, :]
            dn_o[at : at + 4, :] = y1[c, 2 * g + 2 + j, 12:16, :]
        for j in range(2):
            at = base + 96 + 4 * (2 * c + j)
            up_o[at : at + 4, :] = bw[c, 2 * g + 4 + j, 16:20, :]
            dn_o[at : at + 4, :] = bw[c, 2 * g + 4 + j, 12:16, :]

    def keep(j):
        e_o[j] = ew[2 * g + j, 8:24, :]
        w_o[j] = wt[2 * g + j, 8:24, :]
        for c in range(4):
            y_o[c, j] = y1[c, 2 * g + j, 8:24, :]
            b_o[c, j] = bw[c, 2 * g + j, 8:24, :]

    loop(10, keep)


def up_all(groups, devs, idx, low, m1, p1, m2, p2, y_i, b_i, e_i, w_i, x1, fe, fwt, ff, own_edge, far_edge, sol_o, res_o,
           e2, w2, b2, z0, z1, e1, w1, b1, ya, yb, rep, half, va, vb, ew, wt, fw):
    g, d = idx[0], idx[1]
    core = g % 2
    zero8 = jnp.zeros((8, 128), F32)
    zero8w = jnp.zeros((8, 256), F32)
    lane = lax.broadcasted_iota(jnp.int32, (4, 128), 1)
    even = lane % 2 == 0

    def clear(i):
        for row in (0, 8, 16, 24, 32):
            e2[i, row : row + 8, :] = zero8
            for c in range(4):
                b2[c, i, row : row + 8, :] = zero8
                z0[c, i, row : row + 8, :] = zero8
                z1[c, i, row : row + 8, :] = zero8

    loop(groups + 4, clear)
    for source, away in ((m2, -2), (m1, -1), (low, 0), (p1, 1), (p2, 2)):
        row = 16 + 4 * away
        there = 1.0 if away == 0 else jnp.where((d + away >= 0) & (d + away < devs), 1.0, 0.0)
        for c in range(5):
            for q in range(groups // 2):
                at = 4 * (c * (groups // 2) + q)
                packed = source[at : at + 4, :]
                first = jnp.where(even, packed, pltpu.roll(packed, 1, 1))
                second = jnp.where(even, pltpu.roll(packed, 127, 1), packed)
                if c == 4:
                    e2[2 * q + 2, row : row + 4, :] = first * there
                    e2[2 * q + 3, row : row + 4, :] = second * there
                else:
                    b2[c, 2 * q + 2, row : row + 4, :] = first
                    b2[c, 2 * q + 3, row : row + 4, :] = second

    def start_low(i):
        for row in (8, 16, 24):
            inside = rows_inside(row, 4 * d - 16, 4 * devs, 128)
            start_chunk(z0, i + 2, row, 2, 4.0, e2, i + 2, w2, i + 2, b2, i + 2, inside)

    loop(groups, start_low)
    here, there_ = z0, z1
    for _ in range(COARSE - 1):

        def sweep_low(i, here=here, there_=there_):
            for row in (8, 16, 24):
                sweep_chunk(there_, here, i + 2, i + 2, row, 2, 4.0, e2, i + 2, w2, i + 2, b2, i + 2)

        loop(groups, sweep_low)
        here, there_ = there_, here
    z = here

    low_y, high_y = jnp.where(d > 0, 1.0, 0.0), jnp.where(d < devs - 1, 1.0, 0.0)
    base = 20 * (groups // 2)
    for j in range(10):
        e1[j, 0:8, :] = zero8
        e1[j, 24:32, :] = zero8
        e1[j, 8:24, :] = e_i[j]
        w1[j, 8:24, :] = w_i[j]
        for c in range(4):
            b1[c, j, 8:24, :] = b_i[c, j]
            for row in (0, 24):
                ya[c, j, row : row + 8, :] = zero8
                yb[c, j, row : row + 8, :] = zero8
            ya[c, j, 8:24, :] = y_i[c, j]
    for c in range(4):
        for j in range(2):
            at = base + 96 + 4 * (2 * c + j)
            b1[c, 4 + j, 8:12, :] = m1[at : at + 4, :]
            b1[c, 4 + j, 20:24, :] = p1[at : at + 4, :]
        for j in range(6):
            at = base + 4 * (6 * c + j)
            ya[c, 2 + j, 8:12, :] = m1[at : at + 4, :] * low_y
            ya[c, 2 + j, 20:24, :] = p1[at : at + 4, :] * high_y
    for k in range(5):
        for c in range(4):
            rows = z[c, g + k, 14:22, :]
            rep[pl.ds(0, 8, stride=2), :] = rows
            rep[pl.ds(1, 8, stride=2), :] = rows
            twice = rep[...]
            ya[c, 2 * k, 8:24, :] = ya[c, 2 * k, 8:24, :] + twice
            ya[c, 2 * k + 1, 8:24, :] = ya[c, 2 * k + 1, 8:24, :] + twice

    def sweep_mid(out, field, first):
        def body(i):
            for row in (8, 16):
                at = i + first
                sweep_chunk(out, field, at, at, row, 1, 2.0, e1, at, w1, at, b1, at)

        return body

    loop(8, sweep_mid(yb, ya, 1))
    loop(6, sweep_mid(ya, yb, 2))

    spread = fold_matrix(256, True)
    wide = exact_dot(ya[:, 2:8, 8:24, :].reshape(384, 128), spread)
    for n in range(2):
        for parity in range(2):
            half[n, pl.ds(parity, 384, stride=2), :] = wide[:, 128 * n : 128 * n + 128]
    for layer in range(10):
        ew[layer, 0:8, :] = zero8w
        ew[layer, 40:48, :] = zero8w
        ew[layer, 8:40, :] = fe[layer]
    wt[:, 8:40, :] = fwt[...]
    fw[:, :, 8:40, :] = ff[...]
    low_x, high_x = jnp.where(g > 0, 1.0, 0.0), jnp.where(g < groups - 1, 1.0, 0.0)
    on_chip = jnp.where(core == 0, 1.0, 0.0)
    for c in range(4):
        for layer in range(12):
            for row in (0, 40):
                va[c, layer, row : row + 8, :] = zero8w
                vb[c, layer, row : row + 8, :] = zero8w
            at = (6 * c + layer // 2) * 32
            rows = jnp.concatenate([half[0, at : at + 32, :], half[1, at : at + 32, :]], 1)
            va[c, layer, 8:40, :] = rows + x1[c, layer - 3] if 3 <= layer <= 8 else rows
        for j in range(2):
            at = 18 * (2 * c + j)
            own, far = own_edge[at : at + 18, :], far_edge[at : at + 18, :]
            before = jnp.where(core == 0, far, own) * low_x
            after = jnp.where(core == 0, own, far) * high_x
            va[c, 1 + j, 15:33, :] = va[c, 1 + j, 15:33, :] + before
            va[c, 9 + j, 15:33, :] = va[c, 9 + j, 15:33, :] + after

    def sweep_fine(out, field, first, rows):
        def body(i):
            for row in rows:
                at = i + first
                sweep_chunk(out, field, at, at, row, 1, 1.0, ew, at - 1, wt, at - 2, fw, at - 2)

        return body

    loop(8, sweep_fine(vb, va, 2, (8, 16, 24, 32)))
    loop(6, sweep_fine(va, vb, 3, (8, 16, 24, 32)))

    def last(i):
        for row in (16, 24):
            out = residual_chunk(va, i + 4, row, 1, 1.0, ew, i + 3, fw, i + 2)
            for c in range(4):
                sol_o[c, i, row - 16 : row - 8, :] = va[c, i + 4, row : row + 8, :]
                res_o[c, i, row - 16 : row - 8, :] = out[c]

    loop(4, last)


def call(kernel, outs, scratch, *args):
    specs = [pl.BlockSpec(memory_space=pltpu.SMEM)] + [pl.BlockSpec(memory_space=pltpu.VMEM)] * (len(args) - 1)
    return pl.pallas_call(
        kernel,
        out_shape=[jax.ShapeDtypeStruct(shape, F32) for shape in outs],
        in_specs=specs,
        out_specs=[pl.BlockSpec(memory_space=pltpu.VMEM)] * len(outs),
        scratch_shapes=[pltpu.VMEM(shape, F32) for shape in scratch],
        compiler_params=pltpu.CompilerParams(vmem_limit_bytes=VMEM_LIMIT),
    )(*args)


def shift(value, axis, by):
    peers = lax.axis_size(axis)
    return lax.ppermute(value, axis, [(i, (i + by) % peers) for i in range(peers)])


def local(forcing, viscosity):
    groups, devs = lax.axis_size("grp"), lax.axis_size("dev")
    idx = jnp.stack([lax.axis_index("grp"), lax.axis_index("dev")]).astype(jnp.int32)

    def x_pack(f, e):
        return jnp.concatenate([f.reshape(8, 16, 256), e], axis=0)

    xm = shift(x_pack(forcing[:, 2:4], viscosity[1:4]), "grp", 1)
    xp = shift(x_pack(forcing[:, 0:2], viscosity[0:3]), "grp", -1)
    f8 = jnp.concatenate([xm[:8].reshape(4, 2, 16, 256), forcing, xp[:8].reshape(4, 2, 16, 256)], axis=1)
    e10 = jnp.concatenate([xm[8:], viscosity, xp[8:]], axis=0)

    def y_pack(f, e):
        return jnp.concatenate([jnp.swapaxes(f, 0, 1).reshape(192, 256), e.reshape(80, 256)], axis=0)

    ym = shift(y_pack(f8[:, :, 10:16], e10[:, 8:16]), "dev", 1)
    yp = shift(y_pack(f8[:, :, 0:6], e10[:, 0:8]), "dev", -1)

    pay, x1, ew, wt, fw = call(
        lambda *refs: fine_down(groups, devs, *refs),
        [(208, 256), (4, 6, 32, 256), (10, 32, 256), (8, 32, 256), (4, 8, 32, 256)],
        [(4, 8, 48, 256), (10, 48, 256), (8, 48, 256), (4, 8, 48, 256), (4, 8, 48, 256), (10, 32, 256), (320, 128)],
        idx, forcing, viscosity, xm, xp, ym, yp,
    )

    swap = [(i, i ^ 1) for i in range(groups)]
    beside = [(i, (i + 1) % groups if i % 2 else (i - 1) % groups) for i in range(groups)]
    got = lax.ppermute(pay, "grp", swap)
    xr = lax.ppermute(jnp.concatenate([pay, got[:64]], axis=0), "grp", beside)
    c2 = shift(pay[:64], "grp", 4)
    s3 = lax.ppermute(jnp.concatenate([xr[:64], xr[208:], c2], axis=0), "grp", swap)

    layers = 2 * groups + 8
    tall = 20 * (groups // 2)
    up, dn, low, y_w, b_w, e_w, w_w = call(
        lambda *refs: mid_down(groups, devs, *refs),
        [(tall + 128, 128), (tall + 128, 128), (tall, 128), (4, 10, 16, 128), (4, 10, 16, 128), (10, 16, 128), (10, 16, 128)],
        [(4, layers, 32, 128), (layers, 32, 128), (layers, 32, 128), (4, layers, 32, 128), (4, layers, 32, 128), (5, 16, 128), (5, groups, 8, 128)],
        idx, pay[:64], got[:64], xr, c2, s3,
    )

    m1, p1 = shift(up, "dev", 1), shift(dn, "dev", -1)
    m2, p2 = shift(low, "dev", 2), shift(low, "dev", -2)
    deep = groups + 4
    return tuple(call(
        lambda *refs: up_all(groups, devs, *refs),
        [(4, 4, 16, 256), (4, 4, 16, 256)],
        [(deep, 40, 128), (deep, 40, 128), (4, deep, 40, 128), (4, deep, 40, 128), (4, deep, 40, 128),
         (10, 32, 128), (10, 32, 128), (4, 10, 32, 128), (4, 10, 32, 128), (4, 10, 32, 128), (16, 128), (2, 768, 128),
         (4, 12, 48, 256), (4, 12, 48, 256), (10, 48, 256), (8, 48, 256), (4, 8, 48, 256)],
        idx, low, m1, p1, m2, p2, y_w, b_w, e_w, w_w, x1, ew, wt, fw, got[64:], xr[64:208],
    ))


def solution(mesh):
    in_specs = (P(None, "grp", "dev", None), P("grp", "dev", None))
    out_specs = (P(None, "grp", "dev", None), P(None, "grp", "dev", None))
    return jax.shard_map(local, mesh=mesh, in_specs=in_specs, out_specs=out_specs, check_vma=False)
```

```python
import jax
import jax.numpy as jnp
from jax import lax
from jax.experimental import pallas as pl
from jax.experimental.pallas import tpu as pltpu
from jax.sharding import PartitionSpec as P

COARSE = 6
OMEGA = 0.6
BETA = 0.25
F32 = jnp.float32
VMEM_LIMIT = 48 * 1024 * 1024


def shifts(value, step):
    rows, lanes = value.shape
    lane = lax.broadcasted_iota(jnp.int32, (rows, 128), 1)
    if lanes == 256:
        low, high = value[:, :128], value[:, 128:]
        low_up, high_up = pltpu.roll(low, 127, 1), pltpu.roll(high, 127, 1)
        low_dn, high_dn = pltpu.roll(low, 1, 1), pltpu.roll(high, 1, 1)
        last, first = lane == 127, lane == 0
        plus = jnp.concatenate([jnp.where(last, high_up, low_up), jnp.where(last, 0.0, high_up)], 1)
        minus = jnp.concatenate([jnp.where(first, 0.0, low_dn), jnp.where(first, low_dn, high_dn)], 1)
        return plus, minus
    plus = jnp.where(lane >= 128 - step, 0.0, pltpu.roll(value, 128 - step, 1))
    minus = jnp.where(lane < step, 0.0, pltpu.roll(value, step, 1))
    return plus, minus


def get(ref, lead, row, count=8):
    if len(ref.shape) == len(lead) + 3:
        return jnp.concatenate([ref[(*lead, n, pl.ds(row, count))] for n in range(2)], 1)
    return ref[(*lead, pl.ds(row, count))]


def put(ref, lead, row, value):
    rows = pl.ds(row, value.shape[0])
    if len(ref.shape) == len(lead) + 3:
        for n in range(2):
            ref[(*lead, n, rows)] = value[:, 128 * n : 128 * n + 128]
    else:
        ref[(*lead, rows)] = value


def around(ref, lead, layer, row, step):
    rows = ref.shape[-2]
    here = get(ref, (*lead, layer), row)
    near = [get(ref, (*lead, layer + 1), row), get(ref, (*lead, layer - 1), row)]
    near.append(get(ref, (*lead, layer), row + 1) if row + 9 <= rows else pltpu.roll(here, 7, 0))
    near.append(get(ref, (*lead, layer), row - 1) if row >= 1 else pltpu.roll(here, 1, 0))
    return here, [*near, *shifts(here, step)]


def sums_of(visc, layer, row, step):
    here, near = around(visc, (), layer, row, step)
    sums = [here + other for other in near]
    return here, sums, sum(sums[1:], sums[0])


def stencil(field, layer, row, step, sums):
    here, flux, grad, div = [], [], None, None
    for comp in range(4):
        centre, near = around(field, (comp,), layer, row, step)
        here.append(centre)
        if comp < 3:
            terms = [s * n for s, n in zip(sums, near)]
            flux.append(sum(terms[1:], terms[0]))
            diff = near[2 * comp] - near[2 * comp + 1]
            div = diff if div is None else div + diff
        else:
            grad = [near[2 * c] - near[2 * c + 1] for c in range(3)]
    return here, flux, grad, div


def sweep_chunk(out, field, layer, row, step, spacing, visc, visc_layer, weight, weight_layer, source, source_layer):
    e_here, sums, _ = sums_of(visc, visc_layer, row, step)
    here, flux, grad, div = stencil(field, layer, row, step, sums)
    w = get(weight, (weight_layer,), row)
    for c in range(3):
        b = get(source, (c, source_layer), row)
        value = (1.0 - OMEGA) * here[c] + w * (b + (0.5 / (spacing * spacing)) * flux[c] - (0.5 / spacing) * grad[c])
        put(out, (c, layer), row, value)
    b = get(source, (3, source_layer), row)
    put(out, (3, layer), row, here[3] + (BETA * e_here) * (b - (0.5 / spacing) * div))


def residual_chunk(field, layer, row, step, spacing, visc, visc_layer, source, source_layer):
    _, sums, total = sums_of(visc, visc_layer, row, step)
    here, flux, grad, div = stencil(field, layer, row, step, sums)
    out = []
    for c in range(3):
        b = get(source, (c, source_layer), row)
        out.append(b - ((0.5 / (spacing * spacing)) * (total * here[c] - flux[c]) + (0.5 / spacing) * grad[c]))
    out.append(get(source, (3, source_layer), row) - (0.5 / spacing) * div)
    return out


def start_chunk(out, layer, row, step, spacing, visc, visc_layer, weight, weight_layer, source, source_layer, inside):
    e_here, _, total = sums_of(visc, visc_layer, row, step)
    w = jnp.where(inside, (2.0 * OMEGA * spacing * spacing) / total, 0.0)
    put(weight, (weight_layer,), row, w)
    for c in range(4):
        scale = w if c < 3 else BETA * e_here
        put(out, (c, layer), row, scale * get(source, (c, source_layer), row))


def rows_inside(row, first, count, lanes):
    at = lax.broadcasted_iota(jnp.int32, (8, lanes), 0) + (row + first)
    return (at >= 0) & (at < count)


def fold_matrix(fine, transpose=False):
    shape = (fine // 2, fine) if transpose else (fine, fine // 2)
    a = lax.broadcasted_iota(jnp.int32, shape, 1 if transpose else 0)
    b = lax.broadcasted_iota(jnp.int32, shape, 0 if transpose else 1)
    return jnp.where(a // 2 == b, 1.0, 0.0).astype(F32)


def exact_dot(a, b):
    return jnp.dot(a, b, precision=lax.Precision.HIGHEST, preferred_element_type=F32)


def fine_down(groups, devs, idx, f, e, xm, xp, ym, yp, pay_o, x1, ew, wt, fw, x0, pair, half):
    g, d = idx[0], idx[1]
    low_x, high_x = jnp.where(g > 0, 1.0, 0.0), jnp.where(g < groups - 1, 1.0, 0.0)
    low_y, high_y = jnp.where(d > 0, 1.0, 0.0), jnp.where(d < devs - 1, 1.0, 0.0)
    zero = jnp.zeros((2, 256), F32)
    for layer in range(10):
        own = xm[8 + layer] if layer < 3 else xp[8 + layer - 7] if layer > 6 else e[layer - 3]
        s = low_x if layer < 3 else high_x if layer > 6 else 1.0
        at = slice(192 + 8 * layer, 200 + 8 * layer)
        put(ew, (layer,), 0, ym[at, :] * (s * low_y))
        put(ew, (layer,), 8, own * s)
        put(ew, (layer,), 24, yp[at, :] * (s * high_y))
    for layer in range(8):
        for c in range(4):
            own = xm[2 * c + layer] if layer < 2 else xp[2 * c + layer - 6] if layer > 5 else f[c, layer - 2]
            at = slice(24 * layer + 6 * c, 24 * layer + 6 * c + 6)
            put(fw, (c, layer), 0, jnp.concatenate([zero, ym[at, :]], 0))
            put(fw, (c, layer), 8, own)
            put(fw, (c, layer), 24, jnp.concatenate([yp[at, :], zero], 0))
    for layer in range(8):
        layer_in = (4 * g - 2 + layer >= 0) & (4 * g - 2 + layer < 4 * groups)
        for row in (0, 8, 16, 24):
            inside = rows_inside(row, 16 * d - 8, 16 * devs, 256) & layer_in
            start_chunk(x0, layer, row, 1, 1.0, ew, layer + 1, wt, layer, fw, layer, inside)
    for layer in range(1, 7):
        for row in (0, 8, 16, 24):
            sweep_chunk(x1, x0, layer, row, 1, 1.0, ew, layer + 1, wt, layer, fw, layer)
    for m in range(2):
        for row in (4, 12, 20):
            a = residual_chunk(x1, 2 * m + 2, row, 1, 1.0, ew, 2 * m + 3, fw, 2 * m + 2)
            b = residual_chunk(x1, 2 * m + 3, row, 1, 1.0, ew, 2 * m + 4, fw, 2 * m + 3)
            for c in range(4):
                pair[2 * c + m, row : row + 8, :] = a[c] + b[c]
        for c in range(4):
            pair[2 * c + m, 0:4, :] = jnp.zeros((4, 256), F32)
            pair[2 * c + m, 28:32, :] = jnp.zeros((4, 256), F32)
        pair[8 + m] = get(ew, (2 * m + 3,), 0, 32) + get(ew, (2 * m + 4,), 0, 32)
    half[...] = exact_dot(pair[...].reshape(320, 256), fold_matrix(256)) * 0.125
    coarse = half[pl.ds(0, 160, stride=2), :] + half[pl.ds(1, 160, stride=2), :]
    coarse = coarse.reshape(10, 16, 128)
    for m in range(2):
        lanes = slice(128 * m, 128 * m + 128)
        for c in range(4):
            pay_o[12 * c : 12 * c + 12, lanes] = coarse[2 * c + m, 2:14, :]
        pay_o[48:64, lanes] = coarse[8 + m]
    for c in range(4):
        for j in range(2):
            at = 64 + 18 * (2 * c + j)
            pay_o[at : at + 18, :] = get(x1, (c, 3 + j), 7, 18)


def mid_down(groups, devs, idx, own, partner, xr, c2, s3, up_o, dn_o, low_o, y_o, b_o, e_o, w_o, bw, ew, wt, y0, y1, pair, low):
    g, d = idx[0], idx[1]
    chips = groups // 2
    chip, core = g // 2, g % 2
    other = 1 - core
    beside = (chip + chips - 1 + 2 * core) % chips
    across = (chip + 1 + (chips - 2) * core) % chips
    far = (chip + 2) % chips
    layers = 2 * groups
    zero = jnp.zeros((16, 128), F32)
    for i in (0, 1, 2, 3, layers + 4, layers + 5, layers + 6, layers + 7):
        ew[i] = zero
        wt[i] = zero
        for c in range(4):
            bw[c, i] = zero
            y0[c, i] = zero
            y1[c, i] = zero
    for i in range(layers):
        for c in range(4):
            bw[c, i + 4, 0:2, :] = zero[0:2]
            bw[c, i + 4, 14:16, :] = zero[0:2]

    def place(block, at, which, core_at):
        base = 4 + 4 * which + 2 * core_at
        for m in range(2):
            lanes = slice(128 * m, 128 * m + 128)
            for c in range(4):
                bw[c, base + m, 2:14, :] = block[at + 12 * c : at + 12 * c + 12, lanes]
            ew[base + m] = block[at + 48 : at + 64, lanes]

    place(own, 0, chip, core)
    place(partner, 0, chip, other)
    place(xr, 0, beside, other)
    place(xr, 208, beside, core)
    place(s3, 0, across, core)
    place(s3, 64, across, other)
    place(c2, 0, far, core)
    place(s3, 128, far, other)
    for i in range(4, layers + 4):
        for row in (0, 8):
            inside = rows_inside(row, 8 * d - 4, 8 * devs, 128)
            start_chunk(y0, i, row, 1, 2.0, ew, i, wt, i, bw, i, inside)
    for i in range(4, layers + 4):
        for row in (0, 8):
            sweep_chunk(y1, y0, i, row, 1, 2.0, ew, i, wt, i, bw, i)
    lane = lax.broadcasted_iota(jnp.int32, (4, 128), 1)
    for m in range(groups):
        at = 2 * m + 4
        a = residual_chunk(y1, at, 4, 1, 2.0, ew, at, bw, at)
        b = residual_chunk(y1, at + 1, 4, 1, 2.0, ew, at + 1, bw, at + 1)
        for c in range(5):
            pair[m, c] = a[c] + b[c] if c < 4 else get(ew, (at,), 4) + get(ew, (at + 1,), 4)
    for m in range(groups):
        for c in range(5):
            rows = pair[m, c, pl.ds(0, 4, stride=2), :] + pair[m, c, pl.ds(1, 4, stride=2), :]
            mate = jnp.where(lane % 2 == 0, pltpu.roll(rows, 127, 1), pltpu.roll(rows, 1, 1))
            low[c, m, 0:4, :] = (rows + mate) * 0.125
    for c in range(5):
        for q in range(groups // 2):
            packed = jnp.where(lane % 2 == 0, low[c, 2 * q, 0:4, :], low[c, 2 * q + 1, 0:4, :])
            at = 4 * (c * (groups // 2) + q)
            for out in (up_o, dn_o, low_o):
                out[at : at + 4, :] = packed
    base = 20 * (groups // 2)
    for c in range(4):
        for j in range(6):
            at = base + 4 * (6 * c + j)
            up_o[at : at + 4, :] = y1[c, 2 * g + 2 + j, 8:12, :]
            dn_o[at : at + 4, :] = y1[c, 2 * g + 2 + j, 4:8, :]
        for j in range(2):
            at = base + 96 + 4 * (2 * c + j)
            up_o[at : at + 4, :] = bw[c, 2 * g + 4 + j, 8:12, :]
            dn_o[at : at + 4, :] = bw[c, 2 * g + 4 + j, 4:8, :]
    for j in range(10):
        e_o[j] = ew[2 * g + j]
        w_o[j] = wt[2 * g + j]
        for c in range(4):
            y_o[c, j] = y1[c, 2 * g + j]
            b_o[c, j] = bw[c, 2 * g + j]


def up_all(groups, devs, idx, low, m1, p1, m2, p2, y_i, b_i, e1, w1, x1, ew, wt, fw, own_edge, far_edge, sol_o, res_o,
           e2, w2, b2, z0, z1, b1, ya, yb, rep, half, va, vb):
    g, d = idx[0], idx[1]
    core = g % 2
    zero = jnp.zeros((32, 128), F32)
    lane = lax.broadcasted_iota(jnp.int32, (4, 128), 1)
    even = lane % 2 == 0

    for i in (0, 1, groups + 2, groups + 3):
        e2[i] = zero
        for c in range(4):
            z0[c, i] = zero
            z1[c, i] = zero
    for i in range(2, groups + 2):
        e2[i, 0:8, :] = zero[0:8]
        e2[i, 16:32, :] = zero[0:16]
        for c in range(4):
            b2[c, i, 0:8, :] = zero[0:8]
            b2[c, i, 16:32, :] = zero[0:16]
    for source, away in ((m2, -2), (m1, -1), (low, 0), (p1, 1), (p2, 2)):
        row = 10 + 4 * away
        there = 1.0 if away == 0 else jnp.where((d + away >= 0) & (d + away < devs), 1.0, 0.0)
        for c in range(5):
            for q in range(groups // 2):
                at = 4 * (c * (groups // 2) + q)
                packed = source[at : at + 4, :]
                first = jnp.where(even, packed, pltpu.roll(packed, 1, 1))
                second = jnp.where(even, pltpu.roll(packed, 127, 1), packed)
                if c == 4:
                    e2[2 * q + 2, row : row + 4, :] = first * there
                    e2[2 * q + 3, row : row + 4, :] = second * there
                else:
                    b2[c, 2 * q + 2, row : row + 4, :] = first
                    b2[c, 2 * q + 3, row : row + 4, :] = second
    for i in range(2, groups + 2):
        for row in (0, 8, 16):
            inside = rows_inside(row, 4 * d - 10, 4 * devs, 128)
            start_chunk(z0, i, row, 2, 4.0, e2, i, w2, i, b2, i, inside)
    here, other = z0, z1
    for _ in range(COARSE - 1):
        for i in range(2, groups + 2):
            for row in (4, 12):
                sweep_chunk(other, here, i, row, 2, 4.0, e2, i, w2, i, b2, i)
        here, other = other, here
    z = here

    low_y, high_y = jnp.where(d > 0, 1.0, 0.0), jnp.where(d < devs - 1, 1.0, 0.0)
    base = 20 * (groups // 2)
    for c in range(4):
        for k in range(5):
            rows = z[c, g + k, 8:16, :]
            rep[c, k, pl.ds(0, 8, stride=2), :] = rows
            rep[c, k, pl.ds(1, 8, stride=2), :] = rows
    for c in range(4):
        for j in range(10):
            b1[c, j] = b_i[c, j]
            ya[c, j] = y_i[c, j]
        for j in range(2):
            at = base + 96 + 4 * (2 * c + j)
            b1[c, 4 + j, 0:4, :] = m1[at : at + 4, :]
            b1[c, 4 + j, 12:16, :] = p1[at : at + 4, :]
        for j in range(6):
            at = base + 4 * (6 * c + j)
            ya[c, 2 + j, 0:4, :] = m1[at : at + 4, :] * low_y
            ya[c, 2 + j, 12:16, :] = p1[at : at + 4, :] * high_y
        for j in range(10):
            ya[c, j] = ya[c, j] + rep[c, j // 2]
    for at in range(1, 9):
        for row in (0, 8):
            sweep_chunk(yb, ya, at, row, 1, 2.0, e1, at, w1, at, b1, at)
    for at in range(2, 8):
        for row in (0, 8):
            sweep_chunk(ya, yb, at, row, 1, 2.0, e1, at, w1, at, b1, at)

    spread = fold_matrix(256, True)
    wide = exact_dot(ya[:, 2:8].reshape(384, 128), spread)
    for n in range(2):
        for parity in range(2):
            half[n, pl.ds(parity, 384, stride=2), :] = wide[:, 128 * n : 128 * n + 128]
    low_x, high_x = jnp.where(g > 0, 1.0, 0.0), jnp.where(g < groups - 1, 1.0, 0.0)
    for c in range(4):
        for layer in range(1, 11):
            for n in range(2):
                at = (6 * c + layer // 2) * 32
                rows = half[n, at : at + 32, :]
                va[c, layer, n] = rows + x1[c, layer - 2, n] if 3 <= layer <= 8 else rows
        for j in range(2):
            at = 18 * (2 * c + j)
            own, far = own_edge[at : at + 18, :], far_edge[at : at + 18, :]
            before = jnp.where(core == 0, far, own) * low_x
            after = jnp.where(core == 0, own, far) * high_x
            put(va, (c, 1 + j), 7, get(va, (c, 1 + j), 7, 18) + before)
            put(va, (c, 9 + j), 7, get(va, (c, 9 + j), 7, 18) + after)
    for at in range(2, 10):
        for row in (4, 12, 20):
            sweep_chunk(vb, va, at, row, 1, 1.0, ew, at - 1, wt, at - 2, fw, at - 2)
    for at in range(3, 9):
        for row in (4, 12, 20):
            sweep_chunk(va, vb, at, row, 1, 1.0, ew, at - 1, wt, at - 2, fw, at - 2)
    for i in range(4):
        for row in (8, 16):
            out = residual_chunk(va, i + 4, row, 1, 1.0, ew, i + 3, fw, i + 2)
            for c in range(4):
                sol_o[c, i, row - 8 : row, :] = get(va, (c, i + 4), row)
                res_o[c, i, row - 8 : row, :] = out[c]


def call(kernel, outs, scratch, *args):
    specs = [pl.BlockSpec(memory_space=pltpu.SMEM)] + [pl.BlockSpec(memory_space=pltpu.VMEM)] * (len(args) - 1)
    return pl.pallas_call(
        kernel,
        out_shape=[jax.ShapeDtypeStruct(shape, F32) for shape in outs],
        in_specs=specs,
        out_specs=[pl.BlockSpec(memory_space=pltpu.VMEM)] * len(outs),
        scratch_shapes=[pltpu.VMEM(shape, F32) for shape in scratch],
        compiler_params=pltpu.CompilerParams(vmem_limit_bytes=VMEM_LIMIT),
    )(*args)


def shift(value, axis, by):
    peers = lax.axis_size(axis)
    return lax.ppermute(value, axis, [(i, (i + by) % peers) for i in range(peers)])


def local(forcing, viscosity):
    groups, devs = lax.axis_size("grp"), lax.axis_size("dev")
    idx = jnp.stack([lax.axis_index("grp"), lax.axis_index("dev")]).astype(jnp.int32)

    def x_pack(f, e):
        return jnp.concatenate([f.reshape(8, 16, 256), e], axis=0)

    xm = shift(x_pack(forcing[:, 2:4], viscosity[1:4]), "grp", 1)
    xp = shift(x_pack(forcing[:, 0:2], viscosity[0:3]), "grp", -1)
    f8 = jnp.concatenate([xm[:8].reshape(4, 2, 16, 256), forcing, xp[:8].reshape(4, 2, 16, 256)], axis=1)
    e10 = jnp.concatenate([xm[8:], viscosity, xp[8:]], axis=0)

    def y_pack(f, e):
        return jnp.concatenate([jnp.swapaxes(f, 0, 1).reshape(192, 256), e.reshape(80, 256)], axis=0)

    ym = shift(y_pack(f8[:, :, 10:16], e10[:, 8:16]), "dev", 1)
    yp = shift(y_pack(f8[:, :, 0:6], e10[:, 0:8]), "dev", -1)

    pay, x1, ew, wt, fw = call(
        lambda *refs: fine_down(groups, devs, *refs),
        [(208, 256), (4, 8, 2, 32, 128), (10, 2, 32, 128), (8, 2, 32, 128), (4, 8, 2, 32, 128)],
        [(4, 8, 2, 32, 128), (10, 32, 256), (320, 128)],
        idx, forcing, viscosity, xm, xp, ym, yp,
    )

    swap = [(i, i ^ 1) for i in range(groups)]
    beside = [(i, (i + 1) % groups if i % 2 else (i - 1) % groups) for i in range(groups)]
    got = lax.ppermute(pay, "grp", swap)
    xr = lax.ppermute(jnp.concatenate([pay, got[:64]], axis=0), "grp", beside)
    c2 = shift(pay[:64], "grp", 4)
    s3 = lax.ppermute(jnp.concatenate([xr[:64], xr[208:], c2], axis=0), "grp", swap)

    layers = 2 * groups + 8
    tall = 20 * (groups // 2)
    up, dn, low, y_w, b_w, e_w, w_w = call(
        lambda *refs: mid_down(groups, devs, *refs),
        [(tall + 128, 128), (tall + 128, 128), (tall, 128), (4, 10, 16, 128), (4, 10, 16, 128), (10, 16, 128), (10, 16, 128)],
        [(4, layers, 16, 128), (layers, 16, 128), (layers, 16, 128), (4, layers, 16, 128), (4, layers, 16, 128),
         (groups, 5, 8, 128), (5, groups, 8, 128)],
        idx, pay[:64], got[:64], xr, c2, s3,
    )

    m1, p1 = shift(up, "dev", 1), shift(dn, "dev", -1)
    m2, p2 = shift(low, "dev", 2), shift(low, "dev", -2)
    deep = groups + 4
    return tuple(call(
        lambda *refs: up_all(groups, devs, *refs),
        [(4, 4, 16, 256), (4, 4, 16, 256)],
        [(deep, 32, 128), (deep, 32, 128), (4, deep, 32, 128), (4, deep, 32, 128), (4, deep, 32, 128),
         (4, 10, 16, 128), (4, 10, 16, 128), (4, 10, 16, 128), (4, 5, 16, 128), (2, 768, 128),
         (4, 12, 2, 32, 128), (4, 12, 2, 32, 128)],
        idx, low, m1, p1, m2, p2, y_w, b_w, e_w, w_w, x1, ew, wt, fw, got[64:], xr[64:208],
    ))


def solution(mesh):
    in_specs = (P(None, "grp", "dev", None), P("grp", "dev", None))
    out_specs = (P(None, "grp", "dev", None), P(None, "grp", "dev", None))
    return jax.shard_map(local, mesh=mesh, in_specs=in_specs, out_specs=out_specs, check_vma=False)
```

```python
import jax
import jax.numpy as jnp
from jax import lax
from jax.experimental import pallas as pl
from jax.experimental.pallas import tpu as pltpu
from jax.sharding import PartitionSpec as P

COARSE = 6
OMEGA = 0.6
BETA = 0.25
F32 = jnp.float32
VMEM_LIMIT = 48 * 1024 * 1024


def shifts(value, step):
    rows, lanes = value.shape
    lane = lax.broadcasted_iota(jnp.int32, (rows, 128), 1)
    if lanes == 256:
        low, high = value[:, :128], value[:, 128:]
        low_up, high_up = pltpu.roll(low, 127, 1), pltpu.roll(high, 127, 1)
        low_dn, high_dn = pltpu.roll(low, 1, 1), pltpu.roll(high, 1, 1)
        last, first = lane == 127, lane == 0
        plus = jnp.concatenate([jnp.where(last, high_up, low_up), jnp.where(last, 0.0, high_up)], 1)
        minus = jnp.concatenate([jnp.where(first, 0.0, low_dn), jnp.where(first, low_dn, high_dn)], 1)
        return plus, minus
    plus = jnp.where(lane >= 128 - step, 0.0, pltpu.roll(value, 128 - step, 1))
    minus = jnp.where(lane < step, 0.0, pltpu.roll(value, step, 1))
    return plus, minus


def get(ref, lead, row, count=8):
    if len(ref.shape) == len(lead) + 3:
        return jnp.concatenate([ref[(*lead, n, pl.ds(row, count))] for n in range(2)], 1)
    return ref[(*lead, pl.ds(row, count))]


def put(ref, lead, row, value):
    rows = pl.ds(row, value.shape[0])
    if len(ref.shape) == len(lead) + 3:
        for n in range(2):
            ref[(*lead, n, rows)] = value[:, 128 * n : 128 * n + 128]
    else:
        ref[(*lead, rows)] = value


def around(ref, lead, layer, row, step):
    rows = ref.shape[-2]
    here = get(ref, (*lead, layer), row)
    near = [get(ref, (*lead, layer + 1), row), get(ref, (*lead, layer - 1), row)]
    near.append(get(ref, (*lead, layer), row + 1) if row + 9 <= rows else pltpu.roll(here, 7, 0))
    near.append(get(ref, (*lead, layer), row - 1) if row >= 1 else pltpu.roll(here, 1, 0))
    return here, [*near, *shifts(here, step)]


def sums_of(visc, layer, row, step):
    here, near = around(visc, (), layer, row, step)
    sums = [here + other for other in near]
    return here, sums, sum(sums[1:], sums[0])


def stencil(field, layer, row, step, sums):
    here, flux, grad, div = [], [], None, None
    for comp in range(4):
        centre, near = around(field, (comp,), layer, row, step)
        here.append(centre)
        if comp < 3:
            terms = [s * n for s, n in zip(sums, near)]
            flux.append(sum(terms[1:], terms[0]))
            diff = near[2 * comp] - near[2 * comp + 1]
            div = diff if div is None else div + diff
        else:
            grad = [near[2 * c] - near[2 * c + 1] for c in range(3)]
    return here, flux, grad, div


def sweep_chunk(out, field, layer, row, step, spacing, visc, visc_layer, weight, weight_layer, source, source_layer):
    e_here, sums, _ = sums_of(visc, visc_layer, row, step)
    here, flux, grad, div = stencil(field, layer, row, step, sums)
    w = get(weight, (weight_layer,), row)
    for c in range(3):
        b = get(source, (c, source_layer), row)
        value = (1.0 - OMEGA) * here[c] + w * (b + (0.5 / (spacing * spacing)) * flux[c] - (0.5 / spacing) * grad[c])
        put(out, (c, layer), row, value)
    b = get(source, (3, source_layer), row)
    put(out, (3, layer), row, here[3] + (BETA * e_here) * (b - (0.5 / spacing) * div))


def residual_chunk(field, layer, row, step, spacing, visc, visc_layer, source, source_layer):
    _, sums, total = sums_of(visc, visc_layer, row, step)
    here, flux, grad, div = stencil(field, layer, row, step, sums)
    out = []
    for c in range(3):
        b = get(source, (c, source_layer), row)
        out.append(b - ((0.5 / (spacing * spacing)) * (total * here[c] - flux[c]) + (0.5 / spacing) * grad[c]))
    out.append(get(source, (3, source_layer), row) - (0.5 / spacing) * div)
    return out


def start_chunk(out, layer, row, step, spacing, visc, visc_layer, weight, weight_layer, source, source_layer, inside):
    e_here, _, total = sums_of(visc, visc_layer, row, step)
    w = jnp.where(inside, (2.0 * OMEGA * spacing * spacing) / total, 0.0)
    put(weight, (weight_layer,), row, w)
    for c in range(4):
        scale = w if c < 3 else BETA * e_here
        put(out, (c, layer), row, scale * get(source, (c, source_layer), row))


def rows_inside(row, first, count, lanes):
    at = lax.broadcasted_iota(jnp.int32, (8, lanes), 0) + (row + first)
    return (at >= 0) & (at < count)


def fold_matrix(fine, transpose=False):
    shape = (fine // 2, fine) if transpose else (fine, fine // 2)
    a = lax.broadcasted_iota(jnp.int32, shape, 1 if transpose else 0)
    b = lax.broadcasted_iota(jnp.int32, shape, 0 if transpose else 1)
    return jnp.where(a // 2 == b, 1.0, 0.0).astype(F32)


def exact_dot(a, b):
    return jnp.dot(a, b, precision=lax.Precision.HIGHEST, preferred_element_type=F32)


def pick(condition, a, b):
    return jnp.where(condition, a, b)


def pack_first(idx, f, e, cross_o, inner_o):
    even = idx[0] % 2 == 0
    for n in range(11):
        first = f[n // 2, n % 2] if n < 8 else e[n - 8]
        last = f[n // 2, 2 + n % 2] if n < 8 else e[n - 7]
        cross_o[16 * n : 16 * n + 16, :] = pick(even, first, last)
        inner_o[16 * n : 16 * n + 16, :] = pick(even, last, first)


def halo_first(idx, cross, inner, n):
    even = idx[0] % 2 == 0
    a, b = cross[16 * n : 16 * n + 16, :], inner[16 * n : 16 * n + 16, :]
    return pick(even, a, b), pick(even, b, a)


def pack_second(idx, f, e, cross, inner, even_o, odd_o):
    even = idx[1] % 2 == 0

    def write(at, rows, value):
        size = value.shape[0]
        low, high = value[0:rows, :], value[size - rows : size, :]
        even_o[at : at + rows, :] = pick(even, high, low)
        odd_o[at : at + rows, :] = pick(even, low, high)

    for j in range(3):
        before, after = halo_first(idx, cross, inner, 8 + j)
        write(192 + 8 * j, 8, before)
        write(192 + 8 * (7 + j), 8, after)
    for j in range(4):
        write(192 + 8 * (3 + j), 8, e[j])
    for c in range(4):
        for j in range(2):
            before, after = halo_first(idx, cross, inner, 2 * c + j)
            write(24 * j + 6 * c, 6, before)
            write(24 * (6 + j) + 6 * c, 6, after)
        for j in range(4):
            write(24 * (2 + j) + 6 * c, 6, f[c, j])


def fine_down(groups, devs, idx, f, e, cross, inner, odd, even, mid_o, edge_o, x1, ew, wt, fw, x0, pair, half):
    g, d = idx[0], idx[1]
    low_x, high_x = jnp.where(g > 0, 1.0, 0.0), jnp.where(g < groups - 1, 1.0, 0.0)
    low_y, high_y = jnp.where(d > 0, 1.0, 0.0), jnp.where(d < devs - 1, 1.0, 0.0)
    zero = jnp.zeros((2, 256), F32)
    even_dev = d % 2 == 0

    def halo_second(at):
        a, b = odd[at, :], even[at, :]
        return pick(even_dev, a, b), pick(even_dev, b, a)

    for layer in range(10):
        if layer < 3:
            own = halo_first(idx, cross, inner, 8 + layer)[0]
        else:
            own = halo_first(idx, cross, inner, 1 + layer)[1] if layer > 6 else e[layer - 3]
        s = low_x if layer < 3 else high_x if layer > 6 else 1.0
        before, after = halo_second(slice(192 + 8 * layer, 200 + 8 * layer))
        put(ew, (layer,), 0, before * (s * low_y))
        put(ew, (layer,), 8, own * s)
        put(ew, (layer,), 24, after * (s * high_y))
    for layer in range(8):
        for c in range(4):
            if layer < 2:
                own = halo_first(idx, cross, inner, 2 * c + layer)[0]
            else:
                own = halo_first(idx, cross, inner, 2 * c + layer - 6)[1] if layer > 5 else f[c, layer - 2]
            before, after = halo_second(slice(24 * layer + 6 * c, 24 * layer + 6 * c + 6))
            put(fw, (c, layer), 0, jnp.concatenate([zero, before], 0))
            put(fw, (c, layer), 8, own)
            put(fw, (c, layer), 24, jnp.concatenate([after, zero], 0))
    for layer in range(8):
        layer_in = (4 * g - 2 + layer >= 0) & (4 * g - 2 + layer < 4 * groups)
        for row in (0, 8, 16, 24):
            inside = rows_inside(row, 16 * d - 8, 16 * devs, 256) & layer_in
            start_chunk(x0, layer, row, 1, 1.0, ew, layer + 1, wt, layer, fw, layer, inside)
    for layer in range(1, 7):
        for row in (0, 8, 16, 24):
            sweep_chunk(x1, x0, layer, row, 1, 1.0, ew, layer + 1, wt, layer, fw, layer)
    for m in range(2):
        for row in (4, 12, 20):
            a = residual_chunk(x1, 2 * m + 2, row, 1, 1.0, ew, 2 * m + 3, fw, 2 * m + 2)
            b = residual_chunk(x1, 2 * m + 3, row, 1, 1.0, ew, 2 * m + 4, fw, 2 * m + 3)
            for c in range(4):
                pair[2 * c + m, row : row + 8, :] = a[c] + b[c]
        for c in range(4):
            pair[2 * c + m, 0:4, :] = jnp.zeros((4, 256), F32)
            pair[2 * c + m, 28:32, :] = jnp.zeros((4, 256), F32)
        pair[8 + m] = get(ew, (2 * m + 3,), 0, 32) + get(ew, (2 * m + 4,), 0, 32)
    half[...] = exact_dot(pair[...].reshape(320, 256), fold_matrix(256)) * 0.125
    coarse = half[pl.ds(0, 160, stride=2), :] + half[pl.ds(1, 160, stride=2), :]
    coarse = coarse.reshape(10, 16, 128)
    for m in range(2):
        lanes = slice(128 * m, 128 * m + 128)
        for c in range(4):
            mid_o[12 * c : 12 * c + 12, lanes] = coarse[2 * c + m, 2:14, :]
        mid_o[48:64, lanes] = coarse[8 + m]
    for c in range(4):
        for j in range(2):
            at = 18 * (2 * c + j)
            edge_o[at : at + 18, :] = get(x1, (c, 3 + j), 7, 18)


def mid_down(groups, devs, idx, own, partner, xco, cpm, c2, s3, next_o, low_o, y_o, b_o, e_o, w_o, bw, ew, wt, y0, y1, pair, low):
    g, d = idx[0], idx[1]
    chips = groups // 2
    chip, core = g // 2, g % 2
    other = 1 - core
    beside = (chip + chips - 1 + 2 * core) % chips
    across = (chip + 1 + (chips - 2) * core) % chips
    far = (chip + 2) % chips
    layers = 2 * groups
    zero = jnp.zeros((16, 128), F32)
    for i in (0, 1, 2, 3, layers + 4, layers + 5, layers + 6, layers + 7):
        ew[i] = zero
        wt[i] = zero
        for c in range(4):
            bw[c, i] = zero
            y0[c, i] = zero
            y1[c, i] = zero
    for i in range(layers):
        for c in range(4):
            bw[c, i + 4, 0:2, :] = zero[0:2]
            bw[c, i + 4, 14:16, :] = zero[0:2]

    def place(block, at, which, core_at):
        base = 4 + 4 * which + 2 * core_at
        for m in range(2):
            lanes = slice(128 * m, 128 * m + 128)
            for c in range(4):
                bw[c, base + m, 2:14, :] = block[at + 12 * c : at + 12 * c + 12, lanes]
            ew[base + m] = block[at + 48 : at + 64, lanes]

    place(own, 0, chip, core)
    place(partner, 0, chip, other)
    place(xco, 0, beside, other)
    place(cpm, 0, beside, core)
    place(s3, 0, across, core)
    place(s3, 64, across, other)
    place(c2, 0, far, core)
    place(s3, 128, far, other)
    for i in range(4, layers + 4):
        for row in (0, 8):
            inside = rows_inside(row, 8 * d - 4, 8 * devs, 128)
            start_chunk(y0, i, row, 1, 2.0, ew, i, wt, i, bw, i, inside)
    for i in range(4, layers + 4):
        for row in (0, 8):
            sweep_chunk(y1, y0, i, row, 1, 2.0, ew, i, wt, i, bw, i)
    lane = lax.broadcasted_iota(jnp.int32, (4, 128), 1)
    for m in range(groups):
        at = 2 * m + 4
        a = residual_chunk(y1, at, 4, 1, 2.0, ew, at, bw, at)
        b = residual_chunk(y1, at + 1, 4, 1, 2.0, ew, at + 1, bw, at + 1)
        for c in range(5):
            pair[m, c] = a[c] + b[c] if c < 4 else get(ew, (at,), 4) + get(ew, (at + 1,), 4)
    for m in range(groups):
        for c in range(5):
            rows = pair[m, c, pl.ds(0, 4, stride=2), :] + pair[m, c, pl.ds(1, 4, stride=2), :]
            mate = jnp.where(lane % 2 == 0, pltpu.roll(rows, 127, 1), pltpu.roll(rows, 1, 1))
            low[c, m, 0:4, :] = (rows + mate) * 0.125
    for c in range(5):
        for q in range(groups // 2):
            packed = jnp.where(lane % 2 == 0, low[c, 2 * q, 0:4, :], low[c, 2 * q + 1, 0:4, :])
            at = 4 * (c * (groups // 2) + q)
            for out in (next_o, low_o):
                out[at : at + 4, :] = packed
    base = 20 * (groups // 2)
    up = core == 0
    for c in range(4):
        for j in range(8):
            at, i = base + 4 * (8 * c + j), 4 * chip + 2 + j
            next_o[at : at + 4, :] = pick(up, y1[c, i, 8:12, :], y1[c, i, 4:8, :])
        for j in range(4):
            at, i = base + 128 + 4 * (4 * c + j), 4 * chip + 4 + j
            next_o[at : at + 4, :] = pick(up, bw[c, i, 8:12, :], bw[c, i, 4:8, :])
    for j in range(10):
        e_o[j] = ew[2 * g + j]
        w_o[j] = wt[2 * g + j]
        for c in range(4):
            y_o[c, j] = y1[c, 2 * g + j]
            b_o[c, j] = bw[c, 2 * g + j]


def up_all(groups, devs, idx, low, by1, by2, swapped, y_i, b_i, e1, w1, x1, ew, wt, fw, own_edge, far_edge, sol_o, res_o,
           e2, w2, b2, z0, z1, b1, ya, yb, rep, half, va, vb):
    g, d = idx[0], idx[1]
    core = g % 2
    zero = jnp.zeros((32, 128), F32)
    lane = lax.broadcasted_iota(jnp.int32, (4, 128), 1)
    even = lane % 2 == 0

    for i in (0, 1, groups + 2, groups + 3):
        e2[i] = zero
        for c in range(4):
            z0[c, i] = zero
            z1[c, i] = zero
    for i in range(2, groups + 2):
        e2[i, 0:8, :] = zero[0:8]
        e2[i, 16:32, :] = zero[0:16]
        for c in range(4):
            b2[c, i, 0:8, :] = zero[0:8]
            b2[c, i, 16:32, :] = zero[0:16]
    tall = 20 * (groups // 2)
    by1_rows = tall + 192
    first_core = core == 0

    def from_second(by, offset, at):
        a, b = by[at : at + 4, :], swapped[offset + at : offset + at + 4, :]
        return pick(first_core, a, b), pick(first_core, b, a)

    for away in (-2, -1, 0, 1, 2):
        row = 10 + 4 * away
        there = 1.0 if away == 0 else jnp.where((d + away >= 0) & (d + away < devs), 1.0, 0.0)
        for c in range(5):
            for q in range(groups // 2):
                at = 4 * (c * (groups // 2) + q)
                if away == 0:
                    packed = low[at : at + 4, :]
                else:
                    by, offset = (by1, 0) if away in (-1, 1) else (by2, by1_rows)
                    packed = from_second(by, offset, at)[0 if away < 0 else 1]
                first = jnp.where(even, packed, pltpu.roll(packed, 1, 1))
                second = jnp.where(even, pltpu.roll(packed, 127, 1), packed)
                if c == 4:
                    e2[2 * q + 2, row : row + 4, :] = first * there
                    e2[2 * q + 3, row : row + 4, :] = second * there
                else:
                    b2[c, 2 * q + 2, row : row + 4, :] = first
                    b2[c, 2 * q + 3, row : row + 4, :] = second
    for i in range(2, groups + 2):
        for row in (0, 8, 16):
            inside = rows_inside(row, 4 * d - 10, 4 * devs, 128)
            start_chunk(z0, i, row, 2, 4.0, e2, i, w2, i, b2, i, inside)
    here, other = z0, z1
    for _ in range(COARSE - 1):
        for i in range(2, groups + 2):
            for row in (4, 12):
                sweep_chunk(other, here, i, row, 2, 4.0, e2, i, w2, i, b2, i)
        here, other = other, here
    z = here

    low_y, high_y = jnp.where(d > 0, 1.0, 0.0), jnp.where(d < devs - 1, 1.0, 0.0)

    def mid_halo(at, step):
        a, b = from_second(by1, 0, at), from_second(by1, 0, at + step)
        return pick(first_core, a[0], b[0]), pick(first_core, a[1], b[1])

    for c in range(4):
        for k in range(5):
            rows = z[c, g + k, 8:16, :]
            rep[c, k, pl.ds(0, 8, stride=2), :] = rows
            rep[c, k, pl.ds(1, 8, stride=2), :] = rows
    for c in range(4):
        for j in range(10):
            b1[c, j] = b_i[c, j]
            ya[c, j] = y_i[c, j]
        for j in range(2):
            before, after = mid_halo(tall + 128 + 4 * (4 * c + j), 8)
            b1[c, 4 + j, 0:4, :] = before
            b1[c, 4 + j, 12:16, :] = after
        for j in range(6):
            before, after = mid_halo(tall + 4 * (8 * c + j), 8)
            ya[c, 2 + j, 0:4, :] = before * low_y
            ya[c, 2 + j, 12:16, :] = after * high_y
        for j in range(10):
            ya[c, j] = ya[c, j] + rep[c, j // 2]
    for at in range(1, 9):
        for row in (0, 8):
            sweep_chunk(yb, ya, at, row, 1, 2.0, e1, at, w1, at, b1, at)
    for at in range(2, 8):
        for row in (0, 8):
            sweep_chunk(ya, yb, at, row, 1, 2.0, e1, at, w1, at, b1, at)

    spread = fold_matrix(256, True)
    wide = exact_dot(ya[:, 2:8].reshape(384, 128), spread)
    for n in range(2):
        for parity in range(2):
            half[n, pl.ds(parity, 384, stride=2), :] = wide[:, 128 * n : 128 * n + 128]
    low_x, high_x = jnp.where(g > 0, 1.0, 0.0), jnp.where(g < groups - 1, 1.0, 0.0)
    for c in range(4):
        for layer in range(1, 11):
            for n in range(2):
                at = (6 * c + layer // 2) * 32
                rows = half[n, at : at + 32, :]
                va[c, layer, n] = rows + x1[c, layer - 2, n] if 3 <= layer <= 8 else rows
        for j in range(2):
            at = 18 * (2 * c + j)
            own, far = own_edge[at : at + 18, :], far_edge[at : at + 18, :]
            before = jnp.where(core == 0, far, own) * low_x
            after = jnp.where(core == 0, own, far) * high_x
            put(va, (c, 1 + j), 7, get(va, (c, 1 + j), 7, 18) + before)
            put(va, (c, 9 + j), 7, get(va, (c, 9 + j), 7, 18) + after)
    for at in range(2, 10):
        for row in (4, 12, 20):
            sweep_chunk(vb, va, at, row, 1, 1.0, ew, at - 1, wt, at - 2, fw, at - 2)
    for at in range(3, 9):
        for row in (4, 12, 20):
            sweep_chunk(va, vb, at, row, 1, 1.0, ew, at - 1, wt, at - 2, fw, at - 2)
    for i in range(4):
        for row in (8, 16):
            out = residual_chunk(va, i + 4, row, 1, 1.0, ew, i + 3, fw, i + 2)
            for c in range(4):
                sol_o[c, i, row - 8 : row, :] = get(va, (c, i + 4), row)
                res_o[c, i, row - 8 : row, :] = out[c]


def call(kernel, outs, scratch, *args):
    specs = [pl.BlockSpec(memory_space=pltpu.SMEM)] + [pl.BlockSpec(memory_space=pltpu.VMEM)] * (len(args) - 1)
    return pl.pallas_call(
        kernel,
        out_shape=[jax.ShapeDtypeStruct(shape, F32) for shape in outs],
        in_specs=specs,
        out_specs=[pl.BlockSpec(memory_space=pltpu.VMEM)] * len(outs),
        scratch_shapes=[pltpu.VMEM(shape, F32) for shape in scratch],
        compiler_params=pltpu.CompilerParams(vmem_limit_bytes=VMEM_LIMIT),
    )(*args)


def local(forcing, viscosity):
    groups, devs = lax.axis_size("grp"), lax.axis_size("dev")
    idx = jnp.stack([lax.axis_index("grp"), lax.axis_index("dev")]).astype(jnp.int32)
    swap = [(i, i ^ 1) for i in range(groups)]
    beside = [(i, (i + 1) % groups if i % 2 else (i - 1) % groups) for i in range(groups)]
    next_chip = [(i, (i - 2) % groups if i % 2 else (i + 2) % groups) for i in range(groups)]
    far_chip = [(i, (i + 4) % groups) for i in range(groups)]
    even = [(i, i ^ 1) for i in range(devs)]
    odd = [(i, (i + 1) % devs if i % 2 else (i - 1) % devs) for i in range(devs)]

    def along(step):
        to = [(g, (d - step if g % 2 else d + step) % devs) for g in range(groups) for d in range(devs)]
        return [(i, g * devs + d) for i, (g, d) in enumerate(to)]

    cross, inner = call(pack_first, [(176, 256)] * 2, [], idx, forcing, viscosity)
    cross, inner = lax.ppermute(cross, "grp", beside), lax.ppermute(inner, "grp", swap)
    to_even, to_odd = call(pack_second, [(272, 256)] * 2, [], idx, forcing, viscosity, cross, inner)
    from_odd, from_even = lax.ppermute(to_odd, "dev", odd), lax.ppermute(to_even, "dev", even)
    mid, edge, x1, ew, wt, fw = call(
        lambda *refs: fine_down(groups, devs, *refs),
        [(64, 256), (144, 256), (4, 8, 2, 32, 128), (10, 2, 32, 128), (8, 2, 32, 128), (4, 8, 2, 32, 128)],
        [(4, 8, 2, 32, 128), (10, 32, 256), (320, 128)],
        idx, forcing, viscosity, cross, inner, from_odd, from_even,
    )

    c2 = lax.ppermute(mid, "grp", far_chip)
    xco = lax.ppermute(mid, "grp", beside)
    cpm = lax.ppermute(mid, "grp", next_chip)
    partner = lax.ppermute(mid, "grp", swap)
    own_edge = lax.ppermute(edge, "grp", swap)
    far_edge = lax.ppermute(edge, "grp", beside)
    s3 = lax.ppermute(jnp.concatenate([xco, cpm, c2], axis=0), "grp", swap)

    layers = 2 * groups + 8
    tall = 20 * (groups // 2)
    to_next, low, y_w, b_w, e_w, w_w = call(
        lambda *refs: mid_down(groups, devs, *refs),
        [(tall + 192, 128), (tall, 128), (4, 10, 16, 128), (4, 10, 16, 128), (10, 16, 128), (10, 16, 128)],
        [(4, layers, 16, 128), (layers, 16, 128), (layers, 16, 128), (4, layers, 16, 128), (4, layers, 16, 128),
         (groups, 5, 8, 128), (5, groups, 8, 128)],
        idx, mid, partner, xco, cpm, c2, s3,
    )

    by1 = lax.ppermute(to_next, ("grp", "dev"), along(1))
    by2 = lax.ppermute(low, ("grp", "dev"), along(2))
    swapped = lax.ppermute(jnp.concatenate([by1, by2], axis=0), "grp", swap)
    deep = groups + 4
    return tuple(call(
        lambda *refs: up_all(groups, devs, *refs),
        [(4, 4, 16, 256), (4, 4, 16, 256)],
        [(deep, 32, 128), (deep, 32, 128), (4, deep, 32, 128), (4, deep, 32, 128), (4, deep, 32, 128),
         (4, 10, 16, 128), (4, 10, 16, 128), (4, 10, 16, 128), (4, 5, 16, 128), (2, 768, 128),
         (4, 12, 2, 32, 128), (4, 12, 2, 32, 128)],
        idx, low, by1, by2, swapped, y_w, b_w, e_w, w_w, x1, ew, wt, fw, own_edge, far_edge,
    ))


def solution(mesh):
    in_specs = (P(None, "grp", "dev", None), P("grp", "dev", None))
    out_specs = (P(None, "grp", "dev", None), P(None, "grp", "dev", None))
    return jax.shard_map(local, mesh=mesh, in_specs=in_specs, out_specs=out_specs, check_vma=False)
```

```python
import jax
import jax.numpy as jnp
from jax import lax
from jax.experimental import pallas as pl
from jax.experimental.pallas import tpu as pltpu
from jax.sharding import PartitionSpec as P

COARSE = 6
OMEGA = 0.6
BETA = 0.25
F32 = jnp.float32
VMEM_LIMIT = 48 * 1024 * 1024


def shifts(value, step):
    rows, lanes = value.shape
    lane = lax.broadcasted_iota(jnp.int32, (rows, 128), 1)
    if lanes == 256:
        low, high = value[:, :128], value[:, 128:]
        low_up, high_up = pltpu.roll(low, 127, 1), pltpu.roll(high, 127, 1)
        low_dn, high_dn = pltpu.roll(low, 1, 1), pltpu.roll(high, 1, 1)
        last, first = lane == 127, lane == 0
        plus = jnp.concatenate([jnp.where(last, high_up, low_up), jnp.where(last, 0.0, high_up)], 1)
        minus = jnp.concatenate([jnp.where(first, 0.0, low_dn), jnp.where(first, low_dn, high_dn)], 1)
        return plus, minus
    plus = jnp.where(lane >= 128 - step, 0.0, pltpu.roll(value, 128 - step, 1))
    minus = jnp.where(lane < step, 0.0, pltpu.roll(value, step, 1))
    return plus, minus


def get(ref, lead, row, count=8):
    if len(ref.shape) == len(lead) + 3:
        return jnp.concatenate([ref[(*lead, n, pl.ds(row, count))] for n in range(2)], 1)
    return ref[(*lead, pl.ds(row, count))]


def put(ref, lead, row, value):
    rows = pl.ds(row, value.shape[0])
    if len(ref.shape) == len(lead) + 3:
        for n in range(2):
            ref[(*lead, n, rows)] = value[:, 128 * n : 128 * n + 128]
    else:
        ref[(*lead, rows)] = value


def around(ref, lead, layer, row, step):
    rows = ref.shape[-2]
    here = get(ref, (*lead, layer), row)
    near = [get(ref, (*lead, layer + 1), row), get(ref, (*lead, layer - 1), row)]
    near.append(get(ref, (*lead, layer), row + 1) if row + 9 <= rows else pltpu.roll(here, 7, 0))
    near.append(get(ref, (*lead, layer), row - 1) if row >= 1 else pltpu.roll(here, 1, 0))
    return here, [*near, *shifts(here, step)]


def sums_of(visc, layer, row, step):
    here, near = around(visc, (), layer, row, step)
    sums = [here + other for other in near]
    return here, sums, sum(sums[1:], sums[0])


def stencil(field, layer, row, step, sums):
    here, flux, grad, div = [], [], None, None
    for comp in range(4):
        centre, near = around(field, (comp,), layer, row, step)
        here.append(centre)
        if comp < 3:
            terms = [s * n for s, n in zip(sums, near)]
            flux.append(sum(terms[1:], terms[0]))
            diff = near[2 * comp] - near[2 * comp + 1]
            div = diff if div is None else div + diff
        else:
            grad = [near[2 * c] - near[2 * c + 1] for c in range(3)]
    return here, flux, grad, div


def sweep_chunk(out, field, layer, row, step, spacing, visc, visc_layer, weight, weight_layer, source, source_layer):
    e_here, sums, _ = sums_of(visc, visc_layer, row, step)
    here, flux, grad, div = stencil(field, layer, row, step, sums)
    w = get(weight, (weight_layer,), row)
    for c in range(3):
        b = get(source, (c, source_layer), row)
        value = (1.0 - OMEGA) * here[c] + w * (b + (0.5 / (spacing * spacing)) * flux[c] - (0.5 / spacing) * grad[c])
        put(out, (c, layer), row, value)
    b = get(source, (3, source_layer), row)
    put(out, (3, layer), row, here[3] + (BETA * e_here) * (b - (0.5 / spacing) * div))


def residual_chunk(field, layer, row, step, spacing, visc, visc_layer, source, source_layer):
    _, sums, total = sums_of(visc, visc_layer, row, step)
    here, flux, grad, div = stencil(field, layer, row, step, sums)
    out = []
    for c in range(3):
        b = get(source, (c, source_layer), row)
        out.append(b - ((0.5 / (spacing * spacing)) * (total * here[c] - flux[c]) + (0.5 / spacing) * grad[c]))
    out.append(get(source, (3, source_layer), row) - (0.5 / spacing) * div)
    return out


def start_chunk(out, layer, row, step, spacing, visc, visc_layer, weight, weight_layer, source, source_layer, inside):
    e_here, _, total = sums_of(visc, visc_layer, row, step)
    w = jnp.where(inside, (2.0 * OMEGA * spacing * spacing) / total, 0.0)
    put(weight, (weight_layer,), row, w)
    for c in range(4):
        scale = w if c < 3 else BETA * e_here
        put(out, (c, layer), row, scale * get(source, (c, source_layer), row))


def rows_inside(row, first, count, lanes):
    at = lax.broadcasted_iota(jnp.int32, (8, lanes), 0) + (row + first)
    return (at >= 0) & (at < count)


def fold_matrix(fine, transpose=False):
    shape = (fine // 2, fine) if transpose else (fine, fine // 2)
    a = lax.broadcasted_iota(jnp.int32, shape, 1 if transpose else 0)
    b = lax.broadcasted_iota(jnp.int32, shape, 0 if transpose else 1)
    return jnp.where(a // 2 == b, 1.0, 0.0).astype(F32)


def exact_dot(a, b):
    return jnp.dot(a, b, precision=lax.Precision.HIGHEST, preferred_element_type=F32)


def pick(condition, a, b):
    return jnp.where(condition, a, b)


def pack_first(idx, f, e, cross_o, inner_o, sems):
    core = idx[0] % 2
    copies = []
    for n, (out, side) in enumerate(((cross_o, core), (inner_o, 1 - core))):
        for c in range(4):
            copies.append(pltpu.make_async_copy(f.at[c, pl.ds(2 * side, 2)], out.at[pl.ds(2 * c, 2)], sems.at[n, c]))
        copies.append(pltpu.make_async_copy(e.at[pl.ds(side, 3)], out.at[pl.ds(8, 3)], sems.at[n, 4]))
    for copy in copies:
        copy.start()
    for copy in copies:
        copy.wait()


def halo_first(idx, cross, inner, n):
    even = idx[0] % 2 == 0
    a, b = cross[n], inner[n]
    return pick(even, a, b), pick(even, b, a)


F_ROWS = (4, 5, 6, 6, 6, 6, 5, 4)
E_ROWS = (4, 5, 6, 8, 8, 8, 8, 6, 5, 4)
F_AT = tuple(4 * sum(F_ROWS[:n]) for n in range(9))
E_AT = tuple(F_AT[8] + sum(E_ROWS[:n]) for n in range(11))
SECOND_ROWS = 232


def pack_second(idx, f, e, cross, inner, even_o, odd_o):
    even = idx[1] % 2 == 0

    def write(at, rows, value):
        size = value.shape[0]
        low, high = value[0:rows, :], value[size - rows : size, :]
        even_o[at : at + rows, :] = pick(even, high, low)
        odd_o[at : at + rows, :] = pick(even, low, high)

    for layer in range(10):
        if 3 <= layer <= 6:
            value = e[layer - 3]
        else:
            value = halo_first(idx, cross, inner, 8 + layer)[0] if layer < 3 else halo_first(idx, cross, inner, 1 + layer)[1]
        write(E_AT[layer], E_ROWS[layer], value)
    for layer in range(8):
        for c in range(4):
            if 2 <= layer <= 5:
                value = f[c, layer - 2]
            elif layer < 2:
                value = halo_first(idx, cross, inner, 2 * c + layer)[0]
            else:
                value = halo_first(idx, cross, inner, 2 * c + layer - 6)[1]
            write(F_AT[layer] + F_ROWS[layer] * c, F_ROWS[layer], value)
    even_o[E_AT[10] : SECOND_ROWS, :] = jnp.zeros((SECOND_ROWS - E_AT[10], 256), F32)
    odd_o[E_AT[10] : SECOND_ROWS, :] = jnp.zeros((SECOND_ROWS - E_AT[10], 256), F32)


def fine_down(groups, devs, idx, f, e, cross, inner, odd, even, mid_o, pay_o, x1, ew, wt, fw, x0, pair, half):
    g, d = idx[0], idx[1]
    low_x, high_x = jnp.where(g > 0, 1.0, 0.0), jnp.where(g < groups - 1, 1.0, 0.0)
    low_y, high_y = jnp.where(d > 0, 1.0, 0.0), jnp.where(d < devs - 1, 1.0, 0.0)
    even_dev = d % 2 == 0

    def halo_second(at):
        a, b = odd[at, :], even[at, :]
        return pick(even_dev, a, b), pick(even_dev, b, a)

    for layer in range(10):
        if layer < 3:
            own = halo_first(idx, cross, inner, 8 + layer)[0]
        else:
            own = halo_first(idx, cross, inner, 1 + layer)[1] if layer > 6 else e[layer - 3]
        s = low_x if layer < 3 else high_x if layer > 6 else 1.0
        rows = E_ROWS[layer]
        before, after = halo_second(slice(E_AT[layer], E_AT[layer] + rows))
        before, after = before * (s * low_y), after * (s * high_y)
        if rows < 8:
            ones = jnp.ones((8 - rows, 256), F32)
            before, after = jnp.concatenate([ones, before], 0), jnp.concatenate([after, ones], 0)
        put(ew, (layer,), 0, before)
        put(ew, (layer,), 8, own * s)
        put(ew, (layer,), 24, after)
    for layer in range(8):
        for c in range(4):
            if layer < 2:
                own = halo_first(idx, cross, inner, 2 * c + layer)[0]
            else:
                own = halo_first(idx, cross, inner, 2 * c + layer - 6)[1] if layer > 5 else f[c, layer - 2]
            at = F_AT[layer] + F_ROWS[layer] * c
            before, after = halo_second(slice(at, at + F_ROWS[layer]))
            zero = jnp.zeros((8 - F_ROWS[layer], 256), F32)
            put(fw, (c, layer), 0, jnp.concatenate([zero, before], 0))
            put(fw, (c, layer), 8, own)
            put(fw, (c, layer), 24, jnp.concatenate([after, zero], 0))
    for layer in range(8):
        layer_in = (4 * g - 2 + layer >= 0) & (4 * g - 2 + layer < 4 * groups)
        for row in (0, 8, 16, 24):
            inside = rows_inside(row, 16 * d - 8, 16 * devs, 256) & layer_in
            start_chunk(x0, layer, row, 1, 1.0, ew, layer + 1, wt, layer, fw, layer, inside)
    for layer in range(1, 7):
        for row in (0, 8, 16, 24):
            sweep_chunk(x1, x0, layer, row, 1, 1.0, ew, layer + 1, wt, layer, fw, layer)
    for m in range(2):
        for row in (4, 12, 20):
            a = residual_chunk(x1, 2 * m + 2, row, 1, 1.0, ew, 2 * m + 3, fw, 2 * m + 2)
            b = residual_chunk(x1, 2 * m + 3, row, 1, 1.0, ew, 2 * m + 4, fw, 2 * m + 3)
            for c in range(4):
                pair[2 * c + m, row : row + 8, :] = a[c] + b[c]
        for c in range(4):
            pair[2 * c + m, 0:4, :] = jnp.zeros((4, 256), F32)
            pair[2 * c + m, 28:32, :] = jnp.zeros((4, 256), F32)
        pair[8 + m] = get(ew, (2 * m + 3,), 0, 32) + get(ew, (2 * m + 4,), 0, 32)
    half[...] = exact_dot(pair[...].reshape(320, 256), fold_matrix(256)) * 0.125
    coarse = half[pl.ds(0, 160, stride=2), :] + half[pl.ds(1, 160, stride=2), :]
    coarse = coarse.reshape(10, 16, 128)
    for m in range(2):
        lanes = slice(128 * m, 128 * m + 128)
        for c in range(4):
            mid_o[12 * c : 12 * c + 12, lanes] = pay_o[12 * c : 12 * c + 12, lanes] = coarse[2 * c + m, 2:14, :]
        mid_o[48:64, lanes] = pay_o[48:64, lanes] = coarse[8 + m]
    for c in range(4):
        for j in range(2):
            at = 64 + 18 * (2 * c + j)
            pay_o[at : at + 18, :] = get(x1, (c, 3 + j), 7, 18)


def mid_down(groups, devs, idx, own, partner, xco, cpm, c2, s3, next_o, low_o, y_o, b_o, e_o, w_o, bw, ew, wt, y0, y1, pair, low):
    g, d = idx[0], idx[1]
    chips = groups // 2
    chip, core = g // 2, g % 2
    other = 1 - core
    beside = (chip + chips - 1 + 2 * core) % chips
    across = (chip + 1 + (chips - 2) * core) % chips
    far = (chip + 2) % chips
    layers = 2 * groups
    zero = jnp.zeros((16, 128), F32)
    for i in (0, 1, 2, 3, layers + 4, layers + 5, layers + 6, layers + 7):
        ew[i] = zero
        wt[i] = zero
        for c in range(4):
            bw[c, i] = zero
            y0[c, i] = zero
            y1[c, i] = zero
    for i in range(layers):
        for c in range(4):
            bw[c, i + 4, 0:2, :] = zero[0:2]
            bw[c, i + 4, 14:16, :] = zero[0:2]

    def place(block, at, which, core_at):
        base = 4 + 4 * which + 2 * core_at
        for m in range(2):
            lanes = slice(128 * m, 128 * m + 128)
            for c in range(4):
                bw[c, base + m, 2:14, :] = block[at + 12 * c : at + 12 * c + 12, lanes]
            ew[base + m] = block[at + 48 : at + 64, lanes]

    place(own, 0, chip, core)
    place(partner, 0, chip, other)
    place(xco, 0, beside, other)
    place(cpm, 0, beside, core)
    place(s3, 0, across, core)
    place(s3, 64, across, other)
    place(c2, 0, far, core)
    place(s3, 128, far, other)
    for i in range(4, layers + 4):
        for row in (0, 8):
            inside = rows_inside(row, 8 * d - 4, 8 * devs, 128)
            start_chunk(y0, i, row, 1, 2.0, ew, i, wt, i, bw, i, inside)
    for i in range(4, layers + 4):
        for row in (0, 8):
            sweep_chunk(y1, y0, i, row, 1, 2.0, ew, i, wt, i, bw, i)
    lane = lax.broadcasted_iota(jnp.int32, (4, 128), 1)
    for m in range(groups):
        at = 2 * m + 4
        a = residual_chunk(y1, at, 4, 1, 2.0, ew, at, bw, at)
        b = residual_chunk(y1, at + 1, 4, 1, 2.0, ew, at + 1, bw, at + 1)
        for c in range(5):
            pair[m, c] = a[c] + b[c] if c < 4 else get(ew, (at,), 4) + get(ew, (at + 1,), 4)
    for m in range(groups):
        for c in range(5):
            rows = pair[m, c, pl.ds(0, 4, stride=2), :] + pair[m, c, pl.ds(1, 4, stride=2), :]
            mate = jnp.where(lane % 2 == 0, pltpu.roll(rows, 127, 1), pltpu.roll(rows, 1, 1))
            low[c, m, 0:4, :] = (rows + mate) * 0.125
    for c in range(5):
        for q in range(groups // 2):
            packed = jnp.where(lane % 2 == 0, low[c, 2 * q, 0:4, :], low[c, 2 * q + 1, 0:4, :])
            at = 4 * (c * (groups // 2) + q)
            for out in (next_o, low_o):
                out[at : at + 4, :] = packed
    base = 20 * (groups // 2)
    up = core == 0
    for c in range(4):
        for j in range(8):
            at, i = base + 3 * (8 * c + j), 4 * chip + 2 + j
            next_o[at : at + 3, :] = pick(up, y1[c, i, 8:11, :], y1[c, i, 5:8, :])
        for j in range(4):
            at, i = base + 96 + 4 * c + j, 4 * chip + 4 + j
            next_o[at : at + 1, :] = pick(up, bw[c, i, 9:10, :], bw[c, i, 6:7, :])
    for j in range(10):
        e_o[j] = ew[2 * g + j]
        w_o[j] = wt[2 * g + j]
        for c in range(4):
            y_o[c, j] = y1[c, 2 * g + j]
            b_o[c, j] = bw[c, 2 * g + j]


def up_all(groups, devs, idx, low, by1, by2, swapped, y_i, b_i, e1, w1, x1, ew, wt, fw, own_edge, far_edge, sol_o, res_o,
           e2, w2, b2, z0, z1, b1, ya, yb, rep, half, va, vb):
    g, d = idx[0], idx[1]
    core = g % 2
    zero = jnp.zeros((32, 128), F32)
    lane = lax.broadcasted_iota(jnp.int32, (4, 128), 1)
    even = lane % 2 == 0

    for i in (0, 1, groups + 2, groups + 3):
        e2[i] = zero
        for c in range(4):
            z0[c, i] = zero
            z1[c, i] = zero
    for i in range(2, groups + 2):
        e2[i, 0:8, :] = zero[0:8]
        e2[i, 16:32, :] = zero[0:16]
        for c in range(4):
            b2[c, i, 0:8, :] = zero[0:8]
            b2[c, i, 16:32, :] = zero[0:16]
    tall = 20 * (groups // 2)
    by1_rows = tall + 112
    first_core = core == 0

    def from_second(by, offset, at, rows=4):
        a, b = by[at : at + rows, :], swapped[offset + at : offset + at + rows, :]
        return pick(first_core, a, b), pick(first_core, b, a)

    for away in (-2, -1, 0, 1, 2):
        row = 10 + 4 * away
        there = 1.0 if away == 0 else jnp.where((d + away >= 0) & (d + away < devs), 1.0, 0.0)
        for c in range(5):
            for q in range(groups // 2):
                at = 4 * (c * (groups // 2) + q)
                if away == 0:
                    packed = low[at : at + 4, :]
                else:
                    by, offset = (by1, 0) if away in (-1, 1) else (by2, by1_rows)
                    packed = from_second(by, offset, at)[0 if away < 0 else 1]
                first = jnp.where(even, packed, pltpu.roll(packed, 1, 1))
                second = jnp.where(even, pltpu.roll(packed, 127, 1), packed)
                if c == 4:
                    e2[2 * q + 2, row : row + 4, :] = first * there
                    e2[2 * q + 3, row : row + 4, :] = second * there
                else:
                    b2[c, 2 * q + 2, row : row + 4, :] = first
                    b2[c, 2 * q + 3, row : row + 4, :] = second
    for i in range(2, groups + 2):
        for row in (0, 8, 16):
            inside = rows_inside(row, 4 * d - 10, 4 * devs, 128)
            start_chunk(z0, i, row, 2, 4.0, e2, i, w2, i, b2, i, inside)
    here, other = z0, z1
    for _ in range(COARSE - 1):
        for i in range(2, groups + 2):
            for row in (4, 12):
                sweep_chunk(other, here, i, row, 2, 4.0, e2, i, w2, i, b2, i)
        here, other = other, here
    z = here

    low_y, high_y = jnp.where(d > 0, 1.0, 0.0), jnp.where(d < devs - 1, 1.0, 0.0)

    def mid_halo(at, rows):
        a, b = from_second(by1, 0, at, rows), from_second(by1, 0, at + 2 * rows, rows)
        return pick(first_core, a[0], b[0]), pick(first_core, a[1], b[1])

    for c in range(4):
        for k in range(5):
            rows = z[c, g + k, 8:16, :]
            rep[c, k, pl.ds(0, 8, stride=2), :] = rows
            rep[c, k, pl.ds(1, 8, stride=2), :] = rows
    for c in range(4):
        for j in range(10):
            b1[c, j] = b_i[c, j]
            ya[c, j] = y_i[c, j]
        for j in range(2):
            before, after = mid_halo(tall + 96 + 4 * c + j, 1)
            b1[c, 4 + j, 1:2, :] = before
            b1[c, 4 + j, 14:15, :] = after
        for j in range(6):
            before, after = mid_halo(tall + 3 * (8 * c + j), 3)
            ya[c, 2 + j, 0:3, :] = before * low_y
            ya[c, 2 + j, 13:16, :] = after * high_y
        for j in range(10):
            ya[c, j] = ya[c, j] + rep[c, j // 2]
    for at in range(1, 9):
        for row in (0, 8):
            sweep_chunk(yb, ya, at, row, 1, 2.0, e1, at, w1, at, b1, at)
    for at in range(2, 8):
        for row in (0, 8):
            sweep_chunk(ya, yb, at, row, 1, 2.0, e1, at, w1, at, b1, at)

    spread = fold_matrix(256, True)
    wide = exact_dot(ya[:, 2:8].reshape(384, 128), spread)
    for n in range(2):
        for parity in range(2):
            half[n, pl.ds(parity, 384, stride=2), :] = wide[:, 128 * n : 128 * n + 128]
    low_x, high_x = jnp.where(g > 0, 1.0, 0.0), jnp.where(g < groups - 1, 1.0, 0.0)
    for c in range(4):
        for layer in range(1, 11):
            for n in range(2):
                at = (6 * c + layer // 2) * 32
                rows = half[n, at : at + 32, :]
                va[c, layer, n] = rows + x1[c, layer - 2, n] if 3 <= layer <= 8 else rows
        for j in range(2):
            at = 64 + 18 * (2 * c + j)
            own, far = own_edge[at : at + 18, :], far_edge[at : at + 18, :]
            before = jnp.where(core == 0, far, own) * low_x
            after = jnp.where(core == 0, own, far) * high_x
            put(va, (c, 1 + j), 7, get(va, (c, 1 + j), 7, 18) + before)
            put(va, (c, 9 + j), 7, get(va, (c, 9 + j), 7, 18) + after)
    for at in range(2, 10):
        for row in (4, 12, 20):
            sweep_chunk(vb, va, at, row, 1, 1.0, ew, at - 1, wt, at - 2, fw, at - 2)
    for at in range(3, 9):
        for row in (4, 12, 20):
            sweep_chunk(va, vb, at, row, 1, 1.0, ew, at - 1, wt, at - 2, fw, at - 2)
    for i in range(4):
        for row in (8, 16):
            out = residual_chunk(va, i + 4, row, 1, 1.0, ew, i + 3, fw, i + 2)
            for c in range(4):
                sol_o[c, i, row - 8 : row, :] = get(va, (c, i + 4), row)
                res_o[c, i, row - 8 : row, :] = out[c]


def call(kernel, outs, scratch, *args):
    specs = [pl.BlockSpec(memory_space=pltpu.SMEM)] + [pl.BlockSpec(memory_space=pltpu.VMEM)] * (len(args) - 1)
    return pl.pallas_call(
        kernel,
        out_shape=[jax.ShapeDtypeStruct(shape, F32) for shape in outs],
        in_specs=specs,
        out_specs=[pl.BlockSpec(memory_space=pltpu.VMEM)] * len(outs),
        scratch_shapes=[pltpu.VMEM(shape, F32) for shape in scratch],
        compiler_params=pltpu.CompilerParams(vmem_limit_bytes=VMEM_LIMIT),
    )(*args)


def local(forcing, viscosity):
    groups, devs = lax.axis_size("grp"), lax.axis_size("dev")
    idx = jnp.stack([lax.axis_index("grp"), lax.axis_index("dev")]).astype(jnp.int32)
    swap = [(i, i ^ 1) for i in range(groups)]
    beside = [(i, (i + 1) % groups if i % 2 else (i - 1) % groups) for i in range(groups)]
    next_chip = [(i, (i - 2) % groups if i % 2 else (i + 2) % groups) for i in range(groups)]
    far_chip = [(i, (i + 4) % groups) for i in range(groups)]
    even = [(i, i ^ 1) for i in range(devs)]
    odd = [(i, (i + 1) % devs if i % 2 else (i - 1) % devs) for i in range(devs)]

    def along(step):
        to = [(g, (d - step if g % 2 else d + step) % devs) for g in range(groups) for d in range(devs)]
        return [(i, g * devs + d) for i, (g, d) in enumerate(to)]

    cross, inner = pl.pallas_call(
        pack_first,
        out_shape=[jax.ShapeDtypeStruct((11, 16, 256), F32)] * 2,
        in_specs=[pl.BlockSpec(memory_space=pltpu.SMEM), pl.BlockSpec(memory_space=pl.ANY), pl.BlockSpec(memory_space=pl.ANY)],
        out_specs=[pl.BlockSpec(memory_space=pl.ANY)] * 2,
        scratch_shapes=[pltpu.SemaphoreType.DMA((2, 5))],
        compiler_params=pltpu.CompilerParams(vmem_limit_bytes=56 * 1024 * 1024),
    )(idx, forcing, viscosity)
    cross, inner = lax.ppermute(cross, "grp", beside), lax.ppermute(inner, "grp", swap)
    to_even, to_odd = call(pack_second, [(SECOND_ROWS, 256)] * 2, [], idx, forcing, viscosity, cross, inner)
    from_odd, from_even = lax.ppermute(to_odd, "dev", odd), lax.ppermute(to_even, "dev", even)
    mid, pay, x1, ew, wt, fw = call(
        lambda *refs: fine_down(groups, devs, *refs),
        [(64, 256), (208, 256), (4, 8, 2, 32, 128), (10, 2, 32, 128), (8, 2, 32, 128), (4, 8, 2, 32, 128)],
        [(4, 8, 2, 32, 128), (10, 32, 256), (320, 128)],
        idx, forcing, viscosity, cross, inner, from_odd, from_even,
    )

    xco = lax.ppermute(pay, "grp", beside)
    c2 = lax.ppermute(mid, "grp", far_chip)
    cpm = lax.ppermute(mid, "grp", next_chip)
    partner = lax.ppermute(pay, "grp", swap)
    s3 = lax.ppermute(jnp.concatenate([xco[:64], cpm, c2], axis=0), "grp", swap)

    layers = 2 * groups + 8
    tall = 20 * (groups // 2)
    to_next, low, y_w, b_w, e_w, w_w = call(
        lambda *refs: mid_down(groups, devs, *refs),
        [(tall + 112, 128), (tall, 128), (4, 10, 16, 128), (4, 10, 16, 128), (10, 16, 128), (10, 16, 128)],
        [(4, layers, 16, 128), (layers, 16, 128), (layers, 16, 128), (4, layers, 16, 128), (4, layers, 16, 128),
         (groups, 5, 8, 128), (5, groups, 8, 128)],
        idx, mid, partner, xco, cpm, c2, s3,
    )

    by1 = lax.ppermute(to_next, ("grp", "dev"), along(1))
    by2 = lax.ppermute(low, ("grp", "dev"), along(2))
    swapped = lax.ppermute(jnp.concatenate([by1, by2], axis=0), "grp", swap)
    deep = groups + 4
    return tuple(call(
        lambda *refs: up_all(groups, devs, *refs),
        [(4, 4, 16, 256), (4, 4, 16, 256)],
        [(deep, 32, 128), (deep, 32, 128), (4, deep, 32, 128), (4, deep, 32, 128), (4, deep, 32, 128),
         (4, 10, 16, 128), (4, 10, 16, 128), (4, 10, 16, 128), (4, 5, 16, 128), (2, 768, 128),
         (4, 12, 2, 32, 128), (4, 12, 2, 32, 128)],
        idx, low, by1, by2, swapped, y_w, b_w, e_w, w_w, x1, ew, wt, fw, partner, xco,
    ))


def solution(mesh):
    in_specs = (P(None, "grp", "dev", None), P("grp", "dev", None))
    out_specs = (P(None, "grp", "dev", None), P(None, "grp", "dev", None))
    return jax.shard_map(local, mesh=mesh, in_specs=in_specs, out_specs=out_specs, check_vma=False)
```

```python
import jax
import jax.numpy as jnp
from jax import lax
from jax.experimental import pallas as pl
from jax.experimental.pallas import tpu as pltpu
from jax.sharding import PartitionSpec as P

COARSE = 6
OMEGA = 0.6
BETA = 0.25
F32 = jnp.float32
VMEM_LIMIT = 48 * 1024 * 1024


def shifts(value, step):
    rows, lanes = value.shape
    lane = lax.broadcasted_iota(jnp.int32, (rows, 128), 1)
    if lanes == 256:
        low, high = value[:, :128], value[:, 128:]
        low_up, high_up = pltpu.roll(low, 127, 1), pltpu.roll(high, 127, 1)
        low_dn, high_dn = pltpu.roll(low, 1, 1), pltpu.roll(high, 1, 1)
        last, first = lane == 127, lane == 0
        plus = jnp.concatenate([jnp.where(last, high_up, low_up), jnp.where(last, 0.0, high_up)], 1)
        minus = jnp.concatenate([jnp.where(first, 0.0, low_dn), jnp.where(first, low_dn, high_dn)], 1)
        return plus, minus
    plus = jnp.where(lane >= 128 - step, 0.0, pltpu.roll(value, 128 - step, 1))
    minus = jnp.where(lane < step, 0.0, pltpu.roll(value, step, 1))
    return plus, minus


def get(ref, lead, row, count=8):
    if len(ref.shape) == len(lead) + 3:
        return jnp.concatenate([ref[(*lead, n, pl.ds(row, count))] for n in range(2)], 1)
    return ref[(*lead, pl.ds(row, count))]


def put(ref, lead, row, value):
    rows = pl.ds(row, value.shape[0])
    if len(ref.shape) == len(lead) + 3:
        for n in range(2):
            ref[(*lead, n, rows)] = value[:, 128 * n : 128 * n + 128]
    else:
        ref[(*lead, rows)] = value


def around(ref, lead, layer, row, step):
    rows = ref.shape[-2]
    here = get(ref, (*lead, layer), row)
    near = [get(ref, (*lead, layer + 1), row), get(ref, (*lead, layer - 1), row)]
    near.append(get(ref, (*lead, layer), row + 1) if row + 9 <= rows else pltpu.roll(here, 7, 0))
    near.append(get(ref, (*lead, layer), row - 1) if row >= 1 else pltpu.roll(here, 1, 0))
    return here, [*near, *shifts(here, step)]


def sums_of(visc, layer, row, step):
    here, near = around(visc, (), layer, row, step)
    sums = [here + other for other in near]
    return here, sums, sum(sums[1:], sums[0])


def stencil(field, layer, row, step, sums):
    here, flux, grad, div = [], [], None, None
    for comp in range(4):
        centre, near = around(field, (comp,), layer, row, step)
        here.append(centre)
        if comp < 3:
            terms = [s * n for s, n in zip(sums, near)]
            flux.append(sum(terms[1:], terms[0]))
            diff = near[2 * comp] - near[2 * comp + 1]
            div = diff if div is None else div + diff
        else:
            grad = [near[2 * c] - near[2 * c + 1] for c in range(3)]
    return here, flux, grad, div


def sweep_chunk(out, field, layer, row, step, spacing, visc, visc_layer, weight, weight_layer, source, source_layer):
    e_here, sums, _ = sums_of(visc, visc_layer, row, step)
    here, flux, grad, div = stencil(field, layer, row, step, sums)
    w = get(weight, (weight_layer,), row)
    for c in range(3):
        b = get(source, (c, source_layer), row)
        value = (1.0 - OMEGA) * here[c] + w * (b + (0.5 / (spacing * spacing)) * flux[c] - (0.5 / spacing) * grad[c])
        put(out, (c, layer), row, value)
    b = get(source, (3, source_layer), row)
    put(out, (3, layer), row, here[3] + (BETA * e_here) * (b - (0.5 / spacing) * div))


def residual_chunk(field, layer, row, step, spacing, visc, visc_layer, source, source_layer):
    _, sums, total = sums_of(visc, visc_layer, row, step)
    here, flux, grad, div = stencil(field, layer, row, step, sums)
    out = []
    for c in range(3):
        b = get(source, (c, source_layer), row)
        out.append(b - ((0.5 / (spacing * spacing)) * (total * here[c] - flux[c]) + (0.5 / spacing) * grad[c]))
    out.append(get(source, (3, source_layer), row) - (0.5 / spacing) * div)
    return out


def start_chunk(out, layer, row, step, spacing, visc, visc_layer, weight, weight_layer, source, source_layer, inside):
    e_here, _, total = sums_of(visc, visc_layer, row, step)
    w = jnp.where(inside, (2.0 * OMEGA * spacing * spacing) / total, 0.0)
    put(weight, (weight_layer,), row, w)
    for c in range(4):
        scale = w if c < 3 else BETA * e_here
        put(out, (c, layer), row, scale * get(source, (c, source_layer), row))


def rows_inside(row, first, count, lanes):
    at = lax.broadcasted_iota(jnp.int32, (8, lanes), 0) + (row + first)
    return (at >= 0) & (at < count)


def fold_matrix(fine, transpose=False):
    shape = (fine // 2, fine) if transpose else (fine, fine // 2)
    a = lax.broadcasted_iota(jnp.int32, shape, 1 if transpose else 0)
    b = lax.broadcasted_iota(jnp.int32, shape, 0 if transpose else 1)
    return jnp.where(a // 2 == b, 1.0, 0.0).astype(F32)


def exact_dot(a, b):
    return jnp.dot(a, b, precision=lax.Precision.HIGHEST, preferred_element_type=F32)


def pick(condition, a, b):
    return jnp.where(condition, a, b)


def pack_first(idx, f, e, cross_o, inner_o, sems):
    core = idx[0] % 2
    copies = []
    for n, (out, side) in enumerate(((cross_o, core), (inner_o, 1 - core))):
        for c in range(4):
            copies.append(pltpu.make_async_copy(f.at[c, pl.ds(2 * side, 2)], out.at[pl.ds(2 * c, 2)], sems.at[n, c]))
        copies.append(pltpu.make_async_copy(e.at[pl.ds(side, 3)], out.at[pl.ds(8, 3)], sems.at[n, 4]))
    for copy in copies:
        copy.start()
    for copy in copies:
        copy.wait()


def halo_first(idx, cross, inner, n):
    even = idx[0] % 2 == 0
    a, b = cross[n], inner[n]
    return pick(even, a, b), pick(even, b, a)


F_ROWS = (4, 5, 6, 6, 6, 6, 5, 4)
E_ROWS = (4, 5, 6, 8, 8, 8, 8, 6, 5, 4)
F_AT = tuple(4 * sum(F_ROWS[:n]) for n in range(9))
E_AT = tuple(F_AT[8] + sum(E_ROWS[:n]) for n in range(11))
SECOND_ROWS = 232


def pack_second(idx, f, e, cross, inner, even_o, odd_o):
    even = idx[1] % 2 == 0

    def write(at, rows, value):
        size = value.shape[0]
        low, high = value[0:rows, :], value[size - rows : size, :]
        even_o[at : at + rows, :] = pick(even, high, low)
        odd_o[at : at + rows, :] = pick(even, low, high)

    for layer in range(10):
        if 3 <= layer <= 6:
            value = e[layer - 3]
        else:
            value = halo_first(idx, cross, inner, 8 + layer)[0] if layer < 3 else halo_first(idx, cross, inner, 1 + layer)[1]
        write(E_AT[layer], E_ROWS[layer], value)
    for layer in range(8):
        for c in range(4):
            if 2 <= layer <= 5:
                value = f[c, layer - 2]
            elif layer < 2:
                value = halo_first(idx, cross, inner, 2 * c + layer)[0]
            else:
                value = halo_first(idx, cross, inner, 2 * c + layer - 6)[1]
            write(F_AT[layer] + F_ROWS[layer] * c, F_ROWS[layer], value)
    even_o[E_AT[10] : SECOND_ROWS, :] = jnp.zeros((SECOND_ROWS - E_AT[10], 256), F32)
    odd_o[E_AT[10] : SECOND_ROWS, :] = jnp.zeros((SECOND_ROWS - E_AT[10], 256), F32)


def fine_down(groups, devs, idx, f, e, cross, inner, odd, even, mid_o, pay_o, x1, ew, wt, fw, x0, pair, half):
    g, d = idx[0], idx[1]
    low_x, high_x = jnp.where(g > 0, 1.0, 0.0), jnp.where(g < groups - 1, 1.0, 0.0)
    low_y, high_y = jnp.where(d > 0, 1.0, 0.0), jnp.where(d < devs - 1, 1.0, 0.0)
    even_dev = d % 2 == 0

    def halo_second(at):
        a, b = odd[at, :], even[at, :]
        return pick(even_dev, a, b), pick(even_dev, b, a)

    for layer in range(10):
        if layer < 3:
            own = halo_first(idx, cross, inner, 8 + layer)[0]
        else:
            own = halo_first(idx, cross, inner, 1 + layer)[1] if layer > 6 else e[layer - 3]
        s = low_x if layer < 3 else high_x if layer > 6 else 1.0
        rows = E_ROWS[layer]
        before, after = halo_second(slice(E_AT[layer], E_AT[layer] + rows))
        before, after = before * (s * low_y), after * (s * high_y)
        if rows < 8:
            ones = jnp.ones((8 - rows, 256), F32)
            before, after = jnp.concatenate([ones, before], 0), jnp.concatenate([after, ones], 0)
        put(ew, (layer,), 0, before)
        put(ew, (layer,), 8, own * s)
        put(ew, (layer,), 24, after)
    for layer in range(8):
        for c in range(4):
            if layer < 2:
                own = halo_first(idx, cross, inner, 2 * c + layer)[0]
            else:
                own = halo_first(idx, cross, inner, 2 * c + layer - 6)[1] if layer > 5 else f[c, layer - 2]
            at = F_AT[layer] + F_ROWS[layer] * c
            before, after = halo_second(slice(at, at + F_ROWS[layer]))
            zero = jnp.zeros((8 - F_ROWS[layer], 256), F32)
            put(fw, (c, layer), 0, jnp.concatenate([zero, before], 0))
            put(fw, (c, layer), 8, own)
            put(fw, (c, layer), 24, jnp.concatenate([after, zero], 0))
    for layer in range(8):
        layer_in = (4 * g - 2 + layer >= 0) & (4 * g - 2 + layer < 4 * groups)
        for row in (0, 8, 16, 24):
            inside = rows_inside(row, 16 * d - 8, 16 * devs, 256) & layer_in
            start_chunk(x0, layer, row, 1, 1.0, ew, layer + 1, wt, layer, fw, layer, inside)
    for layer in range(1, 7):
        for row in (0, 8, 16, 24):
            sweep_chunk(x1, x0, layer, row, 1, 1.0, ew, layer + 1, wt, layer, fw, layer)
    for m in range(2):
        for row in (4, 12, 20):
            a = residual_chunk(x1, 2 * m + 2, row, 1, 1.0, ew, 2 * m + 3, fw, 2 * m + 2)
            b = residual_chunk(x1, 2 * m + 3, row, 1, 1.0, ew, 2 * m + 4, fw, 2 * m + 3)
            for c in range(4):
                pair[2 * c + m, row : row + 8, :] = a[c] + b[c]
        for c in range(4):
            pair[2 * c + m, 0:4, :] = jnp.zeros((4, 256), F32)
            pair[2 * c + m, 28:32, :] = jnp.zeros((4, 256), F32)
        pair[8 + m] = get(ew, (2 * m + 3,), 0, 32) + get(ew, (2 * m + 4,), 0, 32)
    half[...] = exact_dot(pair[...].reshape(320, 256), fold_matrix(256)) * 0.125
    coarse = half[pl.ds(0, 160, stride=2), :] + half[pl.ds(1, 160, stride=2), :]
    coarse = coarse.reshape(10, 16, 128)
    for m in range(2):
        lanes = slice(128 * m, 128 * m + 128)
        for c in range(4):
            mid_o[12 * c : 12 * c + 12, lanes] = pay_o[12 * c : 12 * c + 12, lanes] = coarse[2 * c + m, 2:14, :]
        mid_o[48:64, lanes] = pay_o[48:64, lanes] = coarse[8 + m]
    for c in range(4):
        for j in range(2):
            at = 64 + 18 * (2 * c + j)
            pay_o[at : at + 18, :] = get(x1, (c, 3 + j), 7, 18)


def mid_down(groups, devs, idx, own, partner, xco, cpm, c2, s3, next_o, low_o, y_o, b_o, e_o, w_o, bw, ew, wt, y0, y1, pair, low):
    g, d = idx[0], idx[1]
    chips = groups // 2
    chip, core = g // 2, g % 2
    other = 1 - core
    beside = (chip + chips - 1 + 2 * core) % chips
    across = (chip + 1 + (chips - 2) * core) % chips
    far = (chip + 2) % chips
    layers = 2 * groups
    zero = jnp.zeros((16, 128), F32)
    for i in (0, 1, 2, 3, layers + 4, layers + 5, layers + 6, layers + 7):
        ew[i] = zero
        wt[i] = zero
        for c in range(4):
            bw[c, i] = zero
            y0[c, i] = zero
            y1[c, i] = zero
    for i in range(layers):
        for c in range(4):
            bw[c, i + 4, 0:2, :] = zero[0:2]
            bw[c, i + 4, 14:16, :] = zero[0:2]

    def place(block, at, which, core_at):
        base = 4 + 4 * which + 2 * core_at
        for m in range(2):
            lanes = slice(128 * m, 128 * m + 128)
            for c in range(4):
                bw[c, base + m, 2:14, :] = block[at + 12 * c : at + 12 * c + 12, lanes]
            ew[base + m] = block[at + 48 : at + 64, lanes]

    place(own, 0, chip, core)
    place(partner, 0, chip, other)
    place(xco, 0, beside, other)
    place(cpm, 0, beside, core)
    place(s3, 0, across, core)
    place(s3, 64, across, other)
    place(c2, 0, far, core)
    place(s3, 128, far, other)
    for i in range(4, layers + 4):
        for row in (0, 8):
            inside = rows_inside(row, 8 * d - 4, 8 * devs, 128)
            start_chunk(y0, i, row, 1, 2.0, ew, i, wt, i, bw, i, inside)
    for i in range(4, layers + 4):
        for row in (0, 8):
            sweep_chunk(y1, y0, i, row, 1, 2.0, ew, i, wt, i, bw, i)
    lane = lax.broadcasted_iota(jnp.int32, (4, 128), 1)
    for m in range(groups):
        at = 2 * m + 4
        a = residual_chunk(y1, at, 4, 1, 2.0, ew, at, bw, at)
        b = residual_chunk(y1, at + 1, 4, 1, 2.0, ew, at + 1, bw, at + 1)
        for c in range(5):
            pair[m, c] = a[c] + b[c] if c < 4 else get(ew, (at,), 4) + get(ew, (at + 1,), 4)
    for m in range(groups):
        for c in range(5):
            rows = pair[m, c, pl.ds(0, 4, stride=2), :] + pair[m, c, pl.ds(1, 4, stride=2), :]
            mate = jnp.where(lane % 2 == 0, pltpu.roll(rows, 127, 1), pltpu.roll(rows, 1, 1))
            low[c, m, 0:4, :] = (rows + mate) * 0.125
    for c in range(5):
        for q in range(groups // 2):
            packed = jnp.where(lane % 2 == 0, low[c, 2 * q, 0:4, :], low[c, 2 * q + 1, 0:4, :])
            at = 4 * (c * (groups // 2) + q)
            for out in (next_o, low_o):
                out[at : at + 4, :] = packed
    base = 20 * (groups // 2)
    up = core == 0
    for c in range(4):
        for j in range(8):
            at, i = base + 3 * (8 * c + j), 4 * chip + 2 + j
            next_o[at : at + 3, :] = pick(up, y1[c, i, 8:11, :], y1[c, i, 5:8, :])
        for j in range(4):
            at, i = base + 96 + 4 * c + j, 4 * chip + 4 + j
            next_o[at : at + 1, :] = pick(up, bw[c, i, 9:10, :], bw[c, i, 6:7, :])
    for j in range(10):
        e_o[j] = ew[2 * g + j]
        w_o[j] = wt[2 * g + j]
        for c in range(4):
            y_o[c, j] = y1[c, 2 * g + j]
            b_o[c, j] = bw[c, 2 * g + j]


def up_all(groups, devs, idx, low, by1, by2, swapped, y_i, b_i, e1, w1, x1, ew, wt, fw, own_edge, far_edge, sol_o, res_o,
           e2, w2, b2, z0, z1, b1, ya, yb, rep, half, va, vb):
    g, d = idx[0], idx[1]
    core = g % 2
    zero = jnp.zeros((32, 128), F32)
    lane = lax.broadcasted_iota(jnp.int32, (4, 128), 1)
    even = lane % 2 == 0

    for i in (0, 1, groups + 2, groups + 3):
        e2[i] = zero
        for c in range(4):
            z0[c, i] = zero
            z1[c, i] = zero
    for i in range(2, groups + 2):
        e2[i, 0:8, :] = zero[0:8]
        e2[i, 16:32, :] = zero[0:16]
        for c in range(4):
            b2[c, i, 0:8, :] = zero[0:8]
            b2[c, i, 16:32, :] = zero[0:16]
    tall = 20 * (groups // 2)
    by1_rows = tall + 112
    first_core = core == 0

    def from_second(by, offset, at, rows=4):
        a, b = by[at : at + rows, :], swapped[offset + at : offset + at + rows, :]
        return pick(first_core, a, b), pick(first_core, b, a)

    for away in (-2, -1, 0, 1, 2):
        row = 10 + 4 * away
        there = 1.0 if away == 0 else jnp.where((d + away >= 0) & (d + away < devs), 1.0, 0.0)
        for c in range(5):
            for q in range(groups // 2):
                at = 4 * (c * (groups // 2) + q)
                if away == 0:
                    packed = low[at : at + 4, :]
                else:
                    by, offset = (by1, 0) if away in (-1, 1) else (by2, by1_rows)
                    packed = from_second(by, offset, at)[0 if away < 0 else 1]
                first = jnp.where(even, packed, pltpu.roll(packed, 1, 1))
                second = jnp.where(even, pltpu.roll(packed, 127, 1), packed)
                if c == 4:
                    e2[2 * q + 2, row : row + 4, :] = first * there
                    e2[2 * q + 3, row : row + 4, :] = second * there
                else:
                    b2[c, 2 * q + 2, row : row + 4, :] = first
                    b2[c, 2 * q + 3, row : row + 4, :] = second
    for i in range(2, groups + 2):
        for row in (0, 8, 16):
            inside = rows_inside(row, 4 * d - 10, 4 * devs, 128)
            start_chunk(z0, i, row, 2, 4.0, e2, i, w2, i, b2, i, inside)
    here, other = z0, z1
    for _ in range(COARSE - 1):
        for i in range(2, groups + 2):
            for row in (4, 12):
                sweep_chunk(other, here, i, row, 2, 4.0, e2, i, w2, i, b2, i)
        here, other = other, here
    z = here

    low_y, high_y = jnp.where(d > 0, 1.0, 0.0), jnp.where(d < devs - 1, 1.0, 0.0)

    def mid_halo(at, rows):
        a, b = from_second(by1, 0, at, rows), from_second(by1, 0, at + 2 * rows, rows)
        return pick(first_core, a[0], b[0]), pick(first_core, a[1], b[1])

    for c in range(4):
        for k in range(5):
            rows = z[c, g + k, 8:16, :]
            rep[c, k, pl.ds(0, 8, stride=2), :] = rows
            rep[c, k, pl.ds(1, 8, stride=2), :] = rows
    for c in range(4):
        for j in range(10):
            b1[c, j] = b_i[c, j]
            ya[c, j] = y_i[c, j]
        for j in range(2):
            before, after = mid_halo(tall + 96 + 4 * c + j, 1)
            b1[c, 4 + j, 1:2, :] = before
            b1[c, 4 + j, 14:15, :] = after
        for j in range(6):
            before, after = mid_halo(tall + 3 * (8 * c + j), 3)
            ya[c, 2 + j, 0:3, :] = before * low_y
            ya[c, 2 + j, 13:16, :] = after * high_y
        for j in range(10):
            ya[c, j] = ya[c, j] + rep[c, j // 2]
    for at in range(1, 9):
        for row in (0, 8):
            sweep_chunk(yb, ya, at, row, 1, 2.0, e1, at, w1, at, b1, at)
    for at in range(2, 8):
        for row in (0, 8):
            sweep_chunk(ya, yb, at, row, 1, 2.0, e1, at, w1, at, b1, at)

    spread = fold_matrix(256, True)
    wide = exact_dot(ya[:, 2:8].reshape(384, 128), spread)
    for n in range(2):
        for parity in range(2):
            half[n, pl.ds(parity, 384, stride=2), :] = wide[:, 128 * n : 128 * n + 128]
    low_x, high_x = jnp.where(g > 0, 1.0, 0.0), jnp.where(g < groups - 1, 1.0, 0.0)
    for c in range(4):
        for layer in range(1, 11):
            for n in range(2):
                at = (6 * c + layer // 2) * 32
                rows = half[n, at : at + 32, :]
                va[c, layer, n] = rows + x1[c, layer - 2, n] if 3 <= layer <= 8 else rows
        for j in range(2):
            at = 64 + 18 * (2 * c + j)
            own, far = own_edge[at : at + 18, :], far_edge[at : at + 18, :]
            before = jnp.where(core == 0, far, own) * low_x
            after = jnp.where(core == 0, own, far) * high_x
            put(va, (c, 1 + j), 7, get(va, (c, 1 + j), 7, 18) + before)
            put(va, (c, 9 + j), 7, get(va, (c, 9 + j), 7, 18) + after)
    for at in range(2, 10):
        for row in (4, 12, 20):
            sweep_chunk(vb, va, at, row, 1, 1.0, ew, at - 1, wt, at - 2, fw, at - 2)
    for at in range(3, 9):
        for row in (4, 12, 20):
            sweep_chunk(va, vb, at, row, 1, 1.0, ew, at - 1, wt, at - 2, fw, at - 2)
    for i in range(4):
        for row in (8, 16):
            out = residual_chunk(va, i + 4, row, 1, 1.0, ew, i + 3, fw, i + 2)
            for c in range(4):
                sol_o[c, i, row - 8 : row, :] = get(va, (c, i + 4), row)
                res_o[c, i, row - 8 : row, :] = out[c]


def call(kernel, outs, scratch, *args):
    specs = [pl.BlockSpec(memory_space=pltpu.SMEM)] + [pl.BlockSpec(memory_space=pltpu.VMEM)] * (len(args) - 1)
    return pl.pallas_call(
        kernel,
        out_shape=[jax.ShapeDtypeStruct(shape, F32) for shape in outs],
        in_specs=specs,
        out_specs=[pl.BlockSpec(memory_space=pltpu.VMEM)] * len(outs),
        scratch_shapes=[pltpu.VMEM(shape, F32) for shape in scratch],
        compiler_params=pltpu.CompilerParams(vmem_limit_bytes=VMEM_LIMIT),
    )(*args)


def local(forcing, viscosity):
    groups, devs = lax.axis_size("grp"), lax.axis_size("dev")
    idx = jnp.stack([lax.axis_index("grp"), lax.axis_index("dev")]).astype(jnp.int32)
    swap = [(i, i ^ 1) for i in range(groups)]
    beside = [(i, (i + 1) % groups if i % 2 else (i - 1) % groups) for i in range(groups)]
    next_chip = [(i, (i - 2) % groups if i % 2 else (i + 2) % groups) for i in range(groups)]
    far_chip = [(i, (i + 4) % groups) for i in range(groups)]
    even = [(i, i ^ 1) for i in range(devs)]
    odd = [(i, (i + 1) % devs if i % 2 else (i - 1) % devs) for i in range(devs)]

    def along(step):
        to = [(g, (d - step if g % 2 else d + step) % devs) for g in range(groups) for d in range(devs)]
        return [(i, g * devs + d) for i, (g, d) in enumerate(to)]

    cross, inner = pl.pallas_call(
        pack_first,
        out_shape=[jax.ShapeDtypeStruct((11, 16, 256), F32)] * 2,
        in_specs=[pl.BlockSpec(memory_space=pltpu.SMEM), pl.BlockSpec(memory_space=pl.ANY), pl.BlockSpec(memory_space=pl.ANY)],
        out_specs=[pl.BlockSpec(memory_space=pltpu.VMEM)] * 2,
        scratch_shapes=[pltpu.SemaphoreType.DMA((2, 5))],
        compiler_params=pltpu.CompilerParams(vmem_limit_bytes=int(53.5 * 1024 * 1024)),
    )(idx, forcing, viscosity)
    cross, inner = lax.ppermute(cross, "grp", beside), lax.ppermute(inner, "grp", swap)
    to_even, to_odd = call(pack_second, [(SECOND_ROWS, 256)] * 2, [], idx, forcing, viscosity, cross, inner)
    from_odd, from_even = lax.ppermute(to_odd, "dev", odd), lax.ppermute(to_even, "dev", even)
    mid, pay, x1, ew, wt, fw = call(
        lambda *refs: fine_down(groups, devs, *refs),
        [(64, 256), (208, 256), (4, 8, 2, 32, 128), (10, 2, 32, 128), (8, 2, 32, 128), (4, 8, 2, 32, 128)],
        [(4, 8, 2, 32, 128), (10, 32, 256), (320, 128)],
        idx, forcing, viscosity, cross, inner, from_odd, from_even,
    )

    xco = lax.ppermute(pay, "grp", beside)
    c2 = lax.ppermute(mid, "grp", far_chip)
    cpm = lax.ppermute(mid, "grp", next_chip)
    partner = lax.ppermute(pay, "grp", swap)
    s3 = lax.ppermute(jnp.concatenate([xco[:64], cpm, c2], axis=0), "grp", swap)

    layers = 2 * groups + 8
    tall = 20 * (groups // 2)
    to_next, low, y_w, b_w, e_w, w_w = call(
        lambda *refs: mid_down(groups, devs, *refs),
        [(tall + 112, 128), (tall, 128), (4, 10, 16, 128), (4, 10, 16, 128), (10, 16, 128), (10, 16, 128)],
        [(4, layers, 16, 128), (layers, 16, 128), (layers, 16, 128), (4, layers, 16, 128), (4, layers, 16, 128),
         (groups, 5, 8, 128), (5, groups, 8, 128)],
        idx, mid, partner, xco, cpm, c2, s3,
    )

    by1 = lax.ppermute(to_next, ("grp", "dev"), along(1))
    by2 = lax.ppermute(low, ("grp", "dev"), along(2))
    swapped = lax.ppermute(jnp.concatenate([by1, by2], axis=0), "grp", swap)
    deep = groups + 4
    return tuple(call(
        lambda *refs: up_all(groups, devs, *refs),
        [(4, 4, 16, 256), (4, 4, 16, 256)],
        [(deep, 32, 128), (deep, 32, 128), (4, deep, 32, 128), (4, deep, 32, 128), (4, deep, 32, 128),
         (4, 10, 16, 128), (4, 10, 16, 128), (4, 10, 16, 128), (4, 5, 16, 128), (2, 768, 128),
         (4, 12, 2, 32, 128), (4, 12, 2, 32, 128)],
        idx, low, by1, by2, swapped, y_w, b_w, e_w, w_w, x1, ew, wt, fw, partner, xco,
    ))


def solution(mesh):
    in_specs = (P(None, "grp", "dev", None), P("grp", "dev", None))
    out_specs = (P(None, "grp", "dev", None), P(None, "grp", "dev", None))
    return jax.shard_map(local, mesh=mesh, in_specs=in_specs, out_specs=out_specs, check_vma=False)
```

```python
import jax
import jax.numpy as jnp
from jax import lax
from jax.experimental import pallas as pl
from jax.experimental.pallas import tpu as pltpu
from jax.sharding import PartitionSpec as P

COARSE = 6
OMEGA = 0.6
BETA = 0.25
F32 = jnp.float32
VMEM_LIMIT = 48 * 1024 * 1024


def shifts(value, step):
    rows, lanes = value.shape
    lane = lax.broadcasted_iota(jnp.int32, (rows, 128), 1)
    if lanes == 256:
        low, high = value[:, :128], value[:, 128:]
        low_up, high_up = pltpu.roll(low, 127, 1), pltpu.roll(high, 127, 1)
        low_dn, high_dn = pltpu.roll(low, 1, 1), pltpu.roll(high, 1, 1)
        last, first = lane == 127, lane == 0
        plus = jnp.concatenate([jnp.where(last, high_up, low_up), jnp.where(last, 0.0, high_up)], 1)
        minus = jnp.concatenate([jnp.where(first, 0.0, low_dn), jnp.where(first, low_dn, high_dn)], 1)
        return plus, minus
    plus = jnp.where(lane >= 128 - step, 0.0, pltpu.roll(value, 128 - step, 1))
    minus = jnp.where(lane < step, 0.0, pltpu.roll(value, step, 1))
    return plus, minus


def get(ref, lead, row, count=8):
    if len(ref.shape) == len(lead) + 3:
        return jnp.concatenate([ref[(*lead, n, pl.ds(row, count))] for n in range(2)], 1)
    return ref[(*lead, pl.ds(row, count))]


def put(ref, lead, row, value):
    rows = pl.ds(row, value.shape[0])
    if len(ref.shape) == len(lead) + 3:
        for n in range(2):
            ref[(*lead, n, rows)] = value[:, 128 * n : 128 * n + 128]
    else:
        ref[(*lead, rows)] = value


def around(ref, lead, layer, row, step):
    rows = ref.shape[-2]
    here = get(ref, (*lead, layer), row)
    near = [get(ref, (*lead, layer + 1), row), get(ref, (*lead, layer - 1), row)]
    near.append(get(ref, (*lead, layer), row + 1) if row + 9 <= rows else pltpu.roll(here, 7, 0))
    near.append(get(ref, (*lead, layer), row - 1) if row >= 1 else pltpu.roll(here, 1, 0))
    return here, [*near, *shifts(here, step)]


def sums_of(visc, layer, row, step):
    here, near = around(visc, (), layer, row, step)
    sums = [here + other for other in near]
    return here, sums, sum(sums[1:], sums[0])


def stencil(field, layer, row, step, sums):
    here, flux, grad, div = [], [], None, None
    for comp in range(4):
        centre, near = around(field, (comp,), layer, row, step)
        here.append(centre)
        if comp < 3:
            terms = [s * n for s, n in zip(sums, near)]
            flux.append(sum(terms[1:], terms[0]))
            diff = near[2 * comp] - near[2 * comp + 1]
            div = diff if div is None else div + diff
        else:
            grad = [near[2 * c] - near[2 * c + 1] for c in range(3)]
    return here, flux, grad, div


def sweep_chunk(out, field, layer, row, step, spacing, visc, visc_layer, weight, weight_layer, source, source_layer):
    e_here, sums, _ = sums_of(visc, visc_layer, row, step)
    here, flux, grad, div = stencil(field, layer, row, step, sums)
    w = get(weight, (weight_layer,), row)
    for c in range(3):
        b = get(source, (c, source_layer), row)
        value = (1.0 - OMEGA) * here[c] + w * (b + (0.5 / (spacing * spacing)) * flux[c] - (0.5 / spacing) * grad[c])
        put(out, (c, layer), row, value)
    b = get(source, (3, source_layer), row)
    put(out, (3, layer), row, here[3] + (BETA * e_here) * (b - (0.5 / spacing) * div))


def residual_chunk(field, layer, row, step, spacing, visc, visc_layer, source, source_layer):
    _, sums, total = sums_of(visc, visc_layer, row, step)
    here, flux, grad, div = stencil(field, layer, row, step, sums)
    out = []
    for c in range(3):
        b = get(source, (c, source_layer), row)
        out.append(b - ((0.5 / (spacing * spacing)) * (total * here[c] - flux[c]) + (0.5 / spacing) * grad[c]))
    out.append(get(source, (3, source_layer), row) - (0.5 / spacing) * div)
    return out


def start_chunk(out, layer, row, step, spacing, visc, visc_layer, weight, weight_layer, source, source_layer, inside):
    e_here, _, total = sums_of(visc, visc_layer, row, step)
    w = jnp.where(inside, (2.0 * OMEGA * spacing * spacing) / total, 0.0)
    put(weight, (weight_layer,), row, w)
    for c in range(4):
        scale = w if c < 3 else BETA * e_here
        put(out, (c, layer), row, scale * get(source, (c, source_layer), row))


def rows_inside(row, first, count, lanes):
    at = lax.broadcasted_iota(jnp.int32, (8, lanes), 0) + (row + first)
    return (at >= 0) & (at < count)


def take(value, at, axis):
    return jnp.take_along_axis(value, at, axis=axis)


def fold(value):
    a = lax.broadcasted_iota(jnp.int32, (256, 128), 0)
    b = lax.broadcasted_iota(jnp.int32, (256, 128), 1)
    pairs = jnp.where(a // 2 == b, 1.0, 0.0).astype(jnp.bfloat16)
    total = None
    for _ in range(3):
        part = value.astype(jnp.bfloat16)
        term = jnp.dot(part, pairs, preferred_element_type=F32)
        total = term if total is None else total + term
        value = value - part.astype(F32)
    return total


def spread(value):
    lane = lax.broadcasted_iota(jnp.int32, (8, 128), 1)
    row = lax.broadcasted_iota(jnp.int32, (8, 128), 0)
    out = []
    for n in range(2):
        wide = take(value, lane // 2 + 64 * n, 1)
        out.append(jnp.concatenate([take(wide, row // 2 + 4 * m, 0) for m in range(2)], 0))
    return out


def pick(condition, a, b):
    return jnp.where(condition, a, b)


def halo_first(idx, cross, inner, n):
    even = idx[0] % 2 == 0
    a, b = cross[n], inner[n]
    return pick(even, a, b), pick(even, b, a)


F_ROWS = (4, 5, 6, 6, 6, 6, 5, 4)
E_ROWS = (4, 5, 6, 8, 8, 8, 8, 6, 5, 4)
F_AT = tuple(4 * sum(F_ROWS[:n]) for n in range(9))
E_AT = tuple(F_AT[8] + sum(E_ROWS[:n]) for n in range(11))
SECOND_ROWS = 232


def pack_second(idx, f, e, cross, inner, even_o, odd_o):
    even = idx[1] % 2 == 0

    def write(at, rows, value):
        size = value.shape[0]
        low, high = value[0:rows, :], value[size - rows : size, :]
        even_o[at : at + rows, :] = pick(even, high, low)
        odd_o[at : at + rows, :] = pick(even, low, high)

    for layer in range(10):
        if 3 <= layer <= 6:
            value = e[layer - 3]
        else:
            value = halo_first(idx, cross, inner, 8 + layer)[0] if layer < 3 else halo_first(idx, cross, inner, 1 + layer)[1]
        write(E_AT[layer], E_ROWS[layer], value)
    for layer in range(8):
        for c in range(4):
            if 2 <= layer <= 5:
                value = f[c, layer - 2]
            elif layer < 2:
                value = halo_first(idx, cross, inner, 2 * c + layer)[0]
            else:
                value = halo_first(idx, cross, inner, 2 * c + layer - 6)[1]
            write(F_AT[layer] + F_ROWS[layer] * c, F_ROWS[layer], value)
    even_o[E_AT[10] : SECOND_ROWS, :] = jnp.zeros((SECOND_ROWS - E_AT[10], 256), F32)
    odd_o[E_AT[10] : SECOND_ROWS, :] = jnp.zeros((SECOND_ROWS - E_AT[10], 256), F32)


def fine_down(groups, devs, idx, f, e, cross, inner, odd, even, mid_o, pay_o, x1, ew, wt, fw, x0, pair, half):
    g, d = idx[0], idx[1]
    low_x, high_x = jnp.where(g > 0, 1.0, 0.0), jnp.where(g < groups - 1, 1.0, 0.0)
    low_y, high_y = jnp.where(d > 0, 1.0, 0.0), jnp.where(d < devs - 1, 1.0, 0.0)
    even_dev = d % 2 == 0

    def halo_second(at):
        a, b = odd[at, :], even[at, :]
        return pick(even_dev, a, b), pick(even_dev, b, a)

    for layer in range(10):
        if layer < 3:
            own = halo_first(idx, cross, inner, 8 + layer)[0]
        else:
            own = halo_first(idx, cross, inner, 1 + layer)[1] if layer > 6 else e[layer - 3]
        s = low_x if layer < 3 else high_x if layer > 6 else 1.0
        rows = E_ROWS[layer]
        before, after = halo_second(slice(E_AT[layer], E_AT[layer] + rows))
        before, after = before * (s * low_y), after * (s * high_y)
        if rows < 8:
            ones = jnp.ones((8 - rows, 256), F32)
            before, after = jnp.concatenate([ones, before], 0), jnp.concatenate([after, ones], 0)
        put(ew, (layer,), 0, before)
        put(ew, (layer,), 8, own * s)
        put(ew, (layer,), 24, after)
    for layer in range(8):
        for c in range(4):
            if layer < 2:
                own = halo_first(idx, cross, inner, 2 * c + layer)[0]
            else:
                own = halo_first(idx, cross, inner, 2 * c + layer - 6)[1] if layer > 5 else f[c, layer - 2]
            at = F_AT[layer] + F_ROWS[layer] * c
            before, after = halo_second(slice(at, at + F_ROWS[layer]))
            zero = jnp.zeros((8 - F_ROWS[layer], 256), F32)
            put(fw, (c, layer), 0, jnp.concatenate([zero, before], 0))
            put(fw, (c, layer), 8, own)
            put(fw, (c, layer), 24, jnp.concatenate([after, zero], 0))
    for layer in range(8):
        layer_in = (4 * g - 2 + layer >= 0) & (4 * g - 2 + layer < 4 * groups)
        for row in (0, 8, 16, 24):
            inside = rows_inside(row, 16 * d - 8, 16 * devs, 256) & layer_in
            start_chunk(x0, layer, row, 1, 1.0, ew, layer + 1, wt, layer, fw, layer, inside)
    for layer in range(1, 7):
        for row in (0, 8, 16, 24):
            sweep_chunk(x1, x0, layer, row, 1, 1.0, ew, layer + 1, wt, layer, fw, layer)
    for m in range(2):
        for row in (4, 12, 20):
            a = residual_chunk(x1, 2 * m + 2, row, 1, 1.0, ew, 2 * m + 3, fw, 2 * m + 2)
            b = residual_chunk(x1, 2 * m + 3, row, 1, 1.0, ew, 2 * m + 4, fw, 2 * m + 3)
            for c in range(4):
                pair[2 * c + m, row : row + 8, :] = a[c] + b[c]
        for c in range(4):
            pair[2 * c + m, 0:4, :] = jnp.zeros((4, 256), F32)
            pair[2 * c + m, 28:32, :] = jnp.zeros((4, 256), F32)
        pair[8 + m] = get(ew, (2 * m + 3,), 0, 32) + get(ew, (2 * m + 4,), 0, 32)
    half[...] = fold(pair[...].reshape(320, 256)) * 0.125
    coarse = half[pl.ds(0, 160, stride=2), :] + half[pl.ds(1, 160, stride=2), :]
    coarse = coarse.reshape(10, 16, 128)
    for m in range(2):
        lanes = slice(128 * m, 128 * m + 128)
        for c in range(4):
            mid_o[12 * c : 12 * c + 12, lanes] = pay_o[12 * c : 12 * c + 12, lanes] = coarse[2 * c + m, 2:14, :]
        mid_o[48:64, lanes] = pay_o[48:64, lanes] = coarse[8 + m]
    for c in range(4):
        for j in range(2):
            at = 64 + 18 * (2 * c + j)
            pay_o[at : at + 18, :] = get(x1, (c, 3 + j), 7, 18)


def mid_down(groups, devs, idx, own, partner, xco, cpm, c2, s3, next_o, low_o, y_o, b_o, e_o, w_o, bw, ew, wt, y0, y1, pair, low):
    g, d = idx[0], idx[1]
    chips = groups // 2
    chip, core = g // 2, g % 2
    other = 1 - core
    beside = (chip + chips - 1 + 2 * core) % chips
    across = (chip + 1 + (chips - 2) * core) % chips
    far = (chip + 2) % chips
    layers = 2 * groups
    zero = jnp.zeros((16, 128), F32)
    for i in (0, 1, 2, 3, layers + 4, layers + 5, layers + 6, layers + 7):
        ew[i] = zero
        wt[i] = zero
        for c in range(4):
            bw[c, i] = zero
            y0[c, i] = zero
            y1[c, i] = zero
    for i in range(layers):
        for c in range(4):
            bw[c, i + 4, 0:2, :] = zero[0:2]
            bw[c, i + 4, 14:16, :] = zero[0:2]

    def place(block, at, which, core_at):
        base = 4 + 4 * which + 2 * core_at
        for m in range(2):
            lanes = slice(128 * m, 128 * m + 128)
            for c in range(4):
                bw[c, base + m, 2:14, :] = block[at + 12 * c : at + 12 * c + 12, lanes]
            ew[base + m] = block[at + 48 : at + 64, lanes]

    place(own, 0, chip, core)
    place(partner, 0, chip, other)
    place(xco, 0, beside, other)
    place(cpm, 0, beside, core)
    place(s3, 0, across, core)
    place(s3, 64, across, other)
    place(c2, 0, far, core)
    place(s3, 128, far, other)
    for i in range(4, layers + 4):
        for row in (0, 8):
            inside = rows_inside(row, 8 * d - 4, 8 * devs, 128)
            start_chunk(y0, i, row, 1, 2.0, ew, i, wt, i, bw, i, inside)
    for i in range(4, layers + 4):
        for row in (0, 8):
            sweep_chunk(y1, y0, i, row, 1, 2.0, ew, i, wt, i, bw, i)
    lane = lax.broadcasted_iota(jnp.int32, (4, 128), 1)
    for m in range(groups):
        at = 2 * m + 4
        a = residual_chunk(y1, at, 4, 1, 2.0, ew, at, bw, at)
        b = residual_chunk(y1, at + 1, 4, 1, 2.0, ew, at + 1, bw, at + 1)
        for c in range(5):
            pair[m, c] = a[c] + b[c] if c < 4 else get(ew, (at,), 4) + get(ew, (at + 1,), 4)
    for m in range(groups):
        for c in range(5):
            rows = pair[m, c, pl.ds(0, 4, stride=2), :] + pair[m, c, pl.ds(1, 4, stride=2), :]
            mate = jnp.where(lane % 2 == 0, pltpu.roll(rows, 127, 1), pltpu.roll(rows, 1, 1))
            low[c, m, 0:4, :] = (rows + mate) * 0.125
    for c in range(5):
        for q in range(groups // 2):
            packed = jnp.where(lane % 2 == 0, low[c, 2 * q, 0:4, :], low[c, 2 * q + 1, 0:4, :])
            at = 4 * (c * (groups // 2) + q)
            for out in (next_o, low_o):
                out[at : at + 4, :] = packed
    base = 20 * (groups // 2)
    up = core == 0
    for c in range(4):
        for j in range(8):
            at, i = base + 3 * (8 * c + j), 4 * chip + 2 + j
            next_o[at : at + 3, :] = pick(up, y1[c, i, 8:11, :], y1[c, i, 5:8, :])
        for j in range(4):
            at, i = base + 96 + 4 * c + j, 4 * chip + 4 + j
            next_o[at : at + 1, :] = pick(up, bw[c, i, 9:10, :], bw[c, i, 6:7, :])
    for j in range(10):
        e_o[j] = ew[2 * g + j]
        w_o[j] = wt[2 * g + j]
        for c in range(4):
            y_o[c, j] = y1[c, 2 * g + j]
            b_o[c, j] = bw[c, 2 * g + j]


def up_all(groups, devs, idx, low, by1, by2, swapped, y_i, b_i, e1, w1, x1, ew, wt, fw, own_edge, far_edge, sol_o, res_o,
           e2, w2, b2, z0, z1, b1, ya, yb, rep, va, vb):
    g, d = idx[0], idx[1]
    core = g % 2
    zero = jnp.zeros((32, 128), F32)
    lane = lax.broadcasted_iota(jnp.int32, (4, 128), 1)
    even = lane % 2 == 0

    for i in (0, 1, groups + 2, groups + 3):
        e2[i] = zero
        for c in range(4):
            z0[c, i] = zero
            z1[c, i] = zero
    for i in range(2, groups + 2):
        e2[i, 0:8, :] = zero[0:8]
        e2[i, 16:32, :] = zero[0:16]
        for c in range(4):
            b2[c, i, 0:8, :] = zero[0:8]
            b2[c, i, 16:32, :] = zero[0:16]
    tall = 20 * (groups // 2)
    by1_rows = tall + 112
    first_core = core == 0

    def from_second(by, offset, at, rows=4):
        a, b = by[at : at + rows, :], swapped[offset + at : offset + at + rows, :]
        return pick(first_core, a, b), pick(first_core, b, a)

    for away in (-2, -1, 0, 1, 2):
        row = 10 + 4 * away
        there = 1.0 if away == 0 else jnp.where((d + away >= 0) & (d + away < devs), 1.0, 0.0)
        for c in range(5):
            for q in range(groups // 2):
                at = 4 * (c * (groups // 2) + q)
                if away == 0:
                    packed = low[at : at + 4, :]
                else:
                    by, offset = (by1, 0) if away in (-1, 1) else (by2, by1_rows)
                    packed = from_second(by, offset, at)[0 if away < 0 else 1]
                first = jnp.where(even, packed, pltpu.roll(packed, 1, 1))
                second = jnp.where(even, pltpu.roll(packed, 127, 1), packed)
                if c == 4:
                    e2[2 * q + 2, row : row + 4, :] = first * there
                    e2[2 * q + 3, row : row + 4, :] = second * there
                else:
                    b2[c, 2 * q + 2, row : row + 4, :] = first
                    b2[c, 2 * q + 3, row : row + 4, :] = second
    for i in range(2, groups + 2):
        for row in (0, 8, 16):
            inside = rows_inside(row, 4 * d - 10, 4 * devs, 128)
            start_chunk(z0, i, row, 2, 4.0, e2, i, w2, i, b2, i, inside)
    here, other = z0, z1
    for _ in range(COARSE - 1):
        for i in range(2, groups + 2):
            for row in (4, 12):
                sweep_chunk(other, here, i, row, 2, 4.0, e2, i, w2, i, b2, i)
        here, other = other, here
    z = here

    low_y, high_y = jnp.where(d > 0, 1.0, 0.0), jnp.where(d < devs - 1, 1.0, 0.0)

    def mid_halo(at, rows):
        a, b = from_second(by1, 0, at, rows), from_second(by1, 0, at + 2 * rows, rows)
        return pick(first_core, a[0], b[0]), pick(first_core, a[1], b[1])

    for c in range(4):
        for k in range(5):
            rows = z[c, g + k, 8:16, :]
            rep[c, k, pl.ds(0, 8, stride=2), :] = rows
            rep[c, k, pl.ds(1, 8, stride=2), :] = rows
    for c in range(4):
        for j in range(10):
            b1[c, j] = b_i[c, j]
            ya[c, j] = y_i[c, j]
        for j in range(2):
            before, after = mid_halo(tall + 96 + 4 * c + j, 1)
            b1[c, 4 + j, 1:2, :] = before
            b1[c, 4 + j, 14:15, :] = after
        for j in range(6):
            before, after = mid_halo(tall + 3 * (8 * c + j), 3)
            ya[c, 2 + j, 0:3, :] = before * low_y
            ya[c, 2 + j, 13:16, :] = after * high_y
        for j in range(10):
            ya[c, j] = ya[c, j] + rep[c, j // 2]
    for at in range(1, 9):
        for row in (0, 8):
            sweep_chunk(yb, ya, at, row, 1, 2.0, e1, at, w1, at, b1, at)
    for at in range(2, 8):
        for row in (0, 8):
            sweep_chunk(ya, yb, at, row, 1, 2.0, e1, at, w1, at, b1, at)

    low_x, high_x = jnp.where(g > 0, 1.0, 0.0), jnp.where(g < groups - 1, 1.0, 0.0)
    for c in range(4):
        for m in range(6):
            for k in range(2):
                both = spread(ya[c, 2 + m, 8 * k : 8 * k + 8, :])
                rows = slice(16 * k, 16 * k + 16)
                for layer in (2 * m, 2 * m + 1):
                    for n in range(2):
                        if 3 <= layer <= 8:
                            va[c, layer, n, rows, :] = both[n] + x1[c, layer - 2, n, rows, :]
                        elif 1 <= layer <= 10:
                            va[c, layer, n, rows, :] = both[n]
        for j in range(2):
            at = 64 + 18 * (2 * c + j)
            own, far = own_edge[at : at + 18, :], far_edge[at : at + 18, :]
            before = jnp.where(core == 0, far, own) * low_x
            after = jnp.where(core == 0, own, far) * high_x
            put(va, (c, 1 + j), 7, get(va, (c, 1 + j), 7, 18) + before)
            put(va, (c, 9 + j), 7, get(va, (c, 9 + j), 7, 18) + after)
    for at in range(2, 10):
        for row in (4, 12, 20):
            sweep_chunk(vb, va, at, row, 1, 1.0, ew, at - 1, wt, at - 2, fw, at - 2)
    for at in range(3, 9):
        for row in (4, 12, 20):
            sweep_chunk(va, vb, at, row, 1, 1.0, ew, at - 1, wt, at - 2, fw, at - 2)
    for i in range(4):
        for row in (8, 16):
            out = residual_chunk(va, i + 4, row, 1, 1.0, ew, i + 3, fw, i + 2)
            for c in range(4):
                sol_o[c, i, row - 8 : row, :] = get(va, (c, i + 4), row)
                res_o[c, i, row - 8 : row, :] = out[c]


def call(kernel, outs, scratch, *args):
    specs = [pl.BlockSpec(memory_space=pltpu.SMEM)] + [pl.BlockSpec(memory_space=pltpu.VMEM)] * (len(args) - 1)
    return pl.pallas_call(
        kernel,
        out_shape=[jax.ShapeDtypeStruct(shape, F32) for shape in outs],
        in_specs=specs,
        out_specs=[pl.BlockSpec(memory_space=pltpu.VMEM)] * len(outs),
        scratch_shapes=[pltpu.VMEM(shape, F32) for shape in scratch],
        compiler_params=pltpu.CompilerParams(vmem_limit_bytes=VMEM_LIMIT),
    )(*args)


def local(forcing, viscosity):
    groups, devs = lax.axis_size("grp"), lax.axis_size("dev")
    idx = jnp.stack([lax.axis_index("grp"), lax.axis_index("dev")]).astype(jnp.int32)
    swap = [(i, i ^ 1) for i in range(groups)]
    beside = [(i, (i + 1) % groups if i % 2 else (i - 1) % groups) for i in range(groups)]
    next_chip = [(i, (i - 2) % groups if i % 2 else (i + 2) % groups) for i in range(groups)]
    far_chip = [(i, (i + 4) % groups) for i in range(groups)]
    even = [(i, i ^ 1) for i in range(devs)]
    odd = [(i, (i + 1) % devs if i % 2 else (i - 1) % devs) for i in range(devs)]

    def along(step):
        to = [(g, (d - step if g % 2 else d + step) % devs) for g in range(groups) for d in range(devs)]
        return [(i, g * devs + d) for i, (g, d) in enumerate(to)]

    f_first, f_last, visc = lax.optimization_barrier((forcing[:, 0:2], forcing[:, 2:4], viscosity))
    first = jnp.concatenate([f_first.reshape(8, 16, 256), visc[0:3]], axis=0)
    last = jnp.concatenate([f_last.reshape(8, 16, 256), visc[1:4]], axis=0)
    cross, inner = pick(idx[0] % 2 == 0, first, last), pick(idx[0] % 2 == 0, last, first)
    cross, inner = lax.optimization_barrier((cross, inner))
    cross, inner = lax.ppermute(cross, "grp", beside), lax.ppermute(inner, "grp", swap)
    to_even, to_odd = call(pack_second, [(SECOND_ROWS, 256)] * 2, [], idx, forcing, viscosity, cross, inner)
    from_odd, from_even = lax.ppermute(to_odd, "dev", odd), lax.ppermute(to_even, "dev", even)
    mid, pay, x1, ew, wt, fw = call(
        lambda *refs: fine_down(groups, devs, *refs),
        [(64, 256), (208, 256), (4, 8, 2, 32, 128), (10, 2, 32, 128), (8, 2, 32, 128), (4, 8, 2, 32, 128)],
        [(4, 8, 2, 32, 128), (10, 32, 256), (320, 128)],
        idx, forcing, viscosity, cross, inner, from_odd, from_even,
    )

    xco = lax.ppermute(pay, "grp", beside)
    c2 = lax.ppermute(mid, "grp", far_chip)
    cpm = lax.ppermute(mid, "grp", next_chip)
    partner = lax.ppermute(pay, "grp", swap)
    s3 = lax.ppermute(jnp.concatenate([xco[:64], cpm, c2], axis=0), "grp", swap)

    layers = 2 * groups + 8
    tall = 20 * (groups // 2)
    to_next, low, y_w, b_w, e_w, w_w = call(
        lambda *refs: mid_down(groups, devs, *refs),
        [(tall + 112, 128), (tall, 128), (4, 10, 16, 128), (4, 10, 16, 128), (10, 16, 128), (10, 16, 128)],
        [(4, layers, 16, 128), (layers, 16, 128), (layers, 16, 128), (4, layers, 16, 128), (4, layers, 16, 128),
         (groups, 5, 8, 128), (5, groups, 8, 128)],
        idx, mid, partner, xco, cpm, c2, s3,
    )

    by1 = lax.ppermute(to_next, ("grp", "dev"), along(1))
    by2 = lax.ppermute(low, ("grp", "dev"), along(2))
    swapped = lax.ppermute(jnp.concatenate([by1, by2], axis=0), "grp", swap)
    deep = groups + 4
    return tuple(call(
        lambda *refs: up_all(groups, devs, *refs),
        [(4, 4, 16, 256), (4, 4, 16, 256)],
        [(deep, 32, 128), (deep, 32, 128), (4, deep, 32, 128), (4, deep, 32, 128), (4, deep, 32, 128),
         (4, 10, 16, 128), (4, 10, 16, 128), (4, 10, 16, 128), (4, 5, 16, 128),
         (4, 12, 2, 32, 128), (4, 12, 2, 32, 128)],
        idx, low, by1, by2, swapped, y_w, b_w, e_w, w_w, x1, ew, wt, fw, partner, xco,
    ))


def solution(mesh):
    in_specs = (P(None, "grp", "dev", None), P("grp", "dev", None))
    out_specs = (P(None, "grp", "dev", None), P(None, "grp", "dev", None))
    return jax.shard_map(local, mesh=mesh, in_specs=in_specs, out_specs=out_specs, check_vma=False)
```

```python
import jax
import jax.numpy as jnp
from jax import lax
from jax.experimental import pallas as pl
from jax.experimental.pallas import tpu as pltpu
from jax.sharding import PartitionSpec as P

COARSE = 6
OMEGA = 0.6
BETA = 0.25
F32 = jnp.float32
VMEM_LIMIT = 48 * 1024 * 1024


def shifts(value, step):
    rows, lanes = value.shape
    lane = lax.broadcasted_iota(jnp.int32, (rows, 128), 1)
    if lanes == 256:
        low, high = value[:, :128], value[:, 128:]
        low_up, high_up = pltpu.roll(low, 127, 1), pltpu.roll(high, 127, 1)
        low_dn, high_dn = pltpu.roll(low, 1, 1), pltpu.roll(high, 1, 1)
        last, first = lane == 127, lane == 0
        plus = jnp.concatenate([jnp.where(last, high_up, low_up), jnp.where(last, 0.0, high_up)], 1)
        minus = jnp.concatenate([jnp.where(first, 0.0, low_dn), jnp.where(first, low_dn, high_dn)], 1)
        return plus, minus
    plus = jnp.where(lane >= 128 - step, 0.0, pltpu.roll(value, 128 - step, 1))
    minus = jnp.where(lane < step, 0.0, pltpu.roll(value, step, 1))
    return plus, minus


def get(ref, lead, row, count=8):
    if len(ref.shape) == len(lead) + 3:
        return jnp.concatenate([ref[(*lead, n, pl.ds(row, count))] for n in range(2)], 1)
    return ref[(*lead, pl.ds(row, count))]


def put(ref, lead, row, value):
    rows = pl.ds(row, value.shape[0])
    if len(ref.shape) == len(lead) + 3:
        for n in range(2):
            ref[(*lead, n, rows)] = value[:, 128 * n : 128 * n + 128]
    else:
        ref[(*lead, rows)] = value


def around(ref, lead, layer, row, step):
    rows = ref.shape[-2]
    here = get(ref, (*lead, layer), row)
    near = [get(ref, (*lead, layer + 1), row), get(ref, (*lead, layer - 1), row)]
    near.append(get(ref, (*lead, layer), row + 1) if row + 9 <= rows else pltpu.roll(here, 7, 0))
    near.append(get(ref, (*lead, layer), row - 1) if row >= 1 else pltpu.roll(here, 1, 0))
    return here, [*near, *shifts(here, step)]


def sums_of(visc, layer, row, step):
    here, near = around(visc, (), layer, row, step)
    sums = [here + other for other in near]
    return here, sums, sum(sums[1:], sums[0])


def stencil(field, layer, row, step, sums):
    here, flux, grad, div = [], [], None, None
    for comp in range(4):
        centre, near = around(field, (comp,), layer, row, step)
        here.append(centre)
        if comp < 3:
            terms = [s * n for s, n in zip(sums, near)]
            flux.append(sum(terms[1:], terms[0]))
            diff = near[2 * comp] - near[2 * comp + 1]
            div = diff if div is None else div + diff
        else:
            grad = [near[2 * c] - near[2 * c + 1] for c in range(3)]
    return here, flux, grad, div


def times(spacing, value):
    return value if spacing == 1.0 else spacing * value


def sweep_chunk(out, field, layer, row, step, spacing, visc, visc_layer, weight, weight_layer, source, source_layer):
    e_here, sums, _ = sums_of(visc, visc_layer, row, step)
    here, flux, grad, div = stencil(field, layer, row, step, sums)
    w = get(weight, (weight_layer,), row)
    for c in range(3):
        b = get(source, (c, source_layer), row)
        value = (1.0 - OMEGA) * here[c] + w * (b + flux[c] - times(spacing, grad[c]))
        put(out, (c, layer), row, value)
    b = get(source, (3, source_layer), row)
    put(out, (3, layer), row, here[3] + (BETA * 0.5 / (spacing * spacing) * e_here) * (b - times(spacing, div)))


def residual_chunk(field, layer, row, step, spacing, visc, visc_layer, source, source_layer):
    _, sums, total = sums_of(visc, visc_layer, row, step)
    here, flux, grad, div = stencil(field, layer, row, step, sums)
    out = []
    for c in range(3):
        b = get(source, (c, source_layer), row)
        out.append(b - (total * here[c] - flux[c] + times(spacing, grad[c])))
    out.append(get(source, (3, source_layer), row) - times(spacing, div))
    return out


def start_chunk(out, layer, row, step, spacing, visc, visc_layer, weight, weight_layer, source, source_layer, inside):
    e_here, _, total = sums_of(visc, visc_layer, row, step)
    w = jnp.where(inside, OMEGA / total, 0.0)
    put(weight, (weight_layer,), row, w)
    for c in range(4):
        scale = w if c < 3 else BETA * 0.5 / (spacing * spacing) * e_here
        put(out, (c, layer), row, scale * get(source, (c, source_layer), row))


def rows_inside(row, first, count, lanes):
    at = lax.broadcasted_iota(jnp.int32, (8, lanes), 0) + (row + first)
    return (at >= 0) & (at < count)


def take(value, at, axis):
    return jnp.take_along_axis(value, at, axis=axis)


def fold(value):
    a = lax.broadcasted_iota(jnp.int32, (256, 128), 0)
    b = lax.broadcasted_iota(jnp.int32, (256, 128), 1)
    pairs = jnp.where(a // 2 == b, 1.0, 0.0).astype(jnp.bfloat16)
    total = None
    for _ in range(3):
        part = value.astype(jnp.bfloat16)
        term = jnp.dot(part, pairs, preferred_element_type=F32)
        total = term if total is None else total + term
        value = value - part.astype(F32)
    return total


def spread(value):
    lane = lax.broadcasted_iota(jnp.int32, (8, 128), 1)
    row = lax.broadcasted_iota(jnp.int32, (8, 128), 0)
    out = []
    for n in range(2):
        wide = take(value, lane // 2 + 64 * n, 1)
        out.append(jnp.concatenate([take(wide, row // 2 + 4 * m, 0) for m in range(2)], 0))
    return out


def pick(condition, a, b):
    return jnp.where(condition, a, b)


def halo_first(idx, cross, inner, n):
    even = idx[0] % 2 == 0
    a, b = cross[n], inner[n]
    return pick(even, a, b), pick(even, b, a)


F_ROWS = (4, 5, 6, 6, 6, 6, 5, 4)
E_ROWS = (4, 5, 6, 8, 8, 8, 8, 6, 5, 4)
F_AT = tuple(4 * sum(F_ROWS[:n]) for n in range(9))
E_AT = tuple(F_AT[8] + sum(E_ROWS[:n]) for n in range(11))
SECOND_ROWS = 232


def pack_second(idx, f, e, cross, inner, even_o, odd_o):
    even = idx[1] % 2 == 0

    def write(at, rows, value):
        size = value.shape[0]
        low, high = value[0:rows, :], value[size - rows : size, :]
        even_o[at : at + rows, :] = pick(even, high, low)
        odd_o[at : at + rows, :] = pick(even, low, high)

    for layer in range(10):
        if 3 <= layer <= 6:
            value = e[layer - 3]
        else:
            value = halo_first(idx, cross, inner, 8 + layer)[0] if layer < 3 else halo_first(idx, cross, inner, 1 + layer)[1]
        write(E_AT[layer], E_ROWS[layer], value)
    for layer in range(8):
        for c in range(4):
            if 2 <= layer <= 5:
                value = f[c, layer - 2]
            elif layer < 2:
                value = halo_first(idx, cross, inner, 2 * c + layer)[0]
            else:
                value = halo_first(idx, cross, inner, 2 * c + layer - 6)[1]
            write(F_AT[layer] + F_ROWS[layer] * c, F_ROWS[layer], value)
    even_o[E_AT[10] : SECOND_ROWS, :] = jnp.zeros((SECOND_ROWS - E_AT[10], 256), F32)
    odd_o[E_AT[10] : SECOND_ROWS, :] = jnp.zeros((SECOND_ROWS - E_AT[10], 256), F32)


def fine_down(groups, devs, idx, f, e, cross, inner, odd, even, mid_o, pay_o, x1, ew, wt, fw, x0, pair, half):
    g, d = idx[0], idx[1]
    low_x, high_x = jnp.where(g > 0, 1.0, 0.0), jnp.where(g < groups - 1, 1.0, 0.0)
    low_y, high_y = jnp.where(d > 0, 1.0, 0.0), jnp.where(d < devs - 1, 1.0, 0.0)
    even_dev = d % 2 == 0

    def halo_second(at):
        a, b = odd[at, :], even[at, :]
        return pick(even_dev, a, b), pick(even_dev, b, a)

    for layer in range(10):
        if layer < 3:
            own = halo_first(idx, cross, inner, 8 + layer)[0]
        else:
            own = halo_first(idx, cross, inner, 1 + layer)[1] if layer > 6 else e[layer - 3]
        s = low_x if layer < 3 else high_x if layer > 6 else 1.0
        rows = E_ROWS[layer]
        before, after = halo_second(slice(E_AT[layer], E_AT[layer] + rows))
        before, after = before * (s * low_y), after * (s * high_y)
        if rows < 8:
            ones = jnp.ones((8 - rows, 256), F32)
            before, after = jnp.concatenate([ones, before], 0), jnp.concatenate([after, ones], 0)
        put(ew, (layer,), 0, before)
        put(ew, (layer,), 8, own * s)
        put(ew, (layer,), 24, after)
    for layer in range(8):
        for c in range(4):
            if layer < 2:
                own = halo_first(idx, cross, inner, 2 * c + layer)[0]
            else:
                own = halo_first(idx, cross, inner, 2 * c + layer - 6)[1] if layer > 5 else f[c, layer - 2]
            at = F_AT[layer] + F_ROWS[layer] * c
            before, after = halo_second(slice(at, at + F_ROWS[layer]))
            zero = jnp.zeros((8 - F_ROWS[layer], 256), F32)
            put(fw, (c, layer), 0, jnp.concatenate([zero, 2.0 * before], 0))
            put(fw, (c, layer), 8, 2.0 * own)
            put(fw, (c, layer), 24, jnp.concatenate([2.0 * after, zero], 0))
    for layer in range(8):
        layer_in = (4 * g - 2 + layer >= 0) & (4 * g - 2 + layer < 4 * groups)
        for row in (0, 8, 16, 24) if 0 < layer < 7 else (4, 12, 20):
            inside = rows_inside(row, 16 * d - 8, 16 * devs, 256) & layer_in
            start_chunk(x0, layer, row, 1, 1.0, ew, layer + 1, wt, layer, fw, layer, inside)
    for layer in range(1, 7):
        for row in (0, 8, 16, 24) if 1 < layer < 6 else (4, 12, 20):
            sweep_chunk(x1, x0, layer, row, 1, 1.0, ew, layer + 1, wt, layer, fw, layer)
    for m in range(2):
        for row in (4, 12, 20):
            a = residual_chunk(x1, 2 * m + 2, row, 1, 1.0, ew, 2 * m + 3, fw, 2 * m + 2)
            b = residual_chunk(x1, 2 * m + 3, row, 1, 1.0, ew, 2 * m + 4, fw, 2 * m + 3)
            for c in range(4):
                pair[2 * c + m, row : row + 8, :] = a[c] + b[c]
        for c in range(4):
            pair[2 * c + m, 0:4, :] = jnp.zeros((4, 256), F32)
            pair[2 * c + m, 28:32, :] = jnp.zeros((4, 256), F32)
        pair[8 + m] = get(ew, (2 * m + 3,), 0, 32) + get(ew, (2 * m + 4,), 0, 32)
    half[...] = fold(pair[...].reshape(320, 256))
    coarse = half[pl.ds(0, 160, stride=2), :] + half[pl.ds(1, 160, stride=2), :]
    coarse = coarse.reshape(10, 16, 128)
    for m in range(2):
        lanes = slice(128 * m, 128 * m + 128)
        for c in range(4):
            mid_o[12 * c : 12 * c + 12, lanes] = pay_o[12 * c : 12 * c + 12, lanes] = coarse[2 * c + m, 2:14, :] * 0.5
        mid_o[48:64, lanes] = pay_o[48:64, lanes] = coarse[8 + m] * 0.125
    for c in range(4):
        for j in range(2):
            at = 64 + 18 * (2 * c + j)
            pay_o[at : at + 18, :] = get(x1, (c, 3 + j), 7, 18)


def mid_down(groups, devs, idx, own, partner, xco, cpm, c2, s3, next_o, low_o, y_o, b_o, e_o, w_o, bw, ew, wt, y0, y1, pair, low):
    g, d = idx[0], idx[1]
    chips = groups // 2
    chip, core = g // 2, g % 2
    other = 1 - core
    beside = (chip + chips - 1 + 2 * core) % chips
    across = (chip + 1 + (chips - 2) * core) % chips
    far = (chip + 2) % chips
    layers = 2 * groups
    zero = jnp.zeros((16, 128), F32)
    for i in (0, 1, 2, 3, layers + 4, layers + 5, layers + 6, layers + 7):
        ew[i] = zero
        wt[i] = zero
        for c in range(4):
            bw[c, i] = zero
            y0[c, i] = zero
            y1[c, i] = zero
    for i in range(layers):
        for c in range(4):
            bw[c, i + 4, 0:2, :] = zero[0:2]
            bw[c, i + 4, 14:16, :] = zero[0:2]

    def place(block, at, which, core_at):
        base = 4 + 4 * which + 2 * core_at
        for m in range(2):
            lanes = slice(128 * m, 128 * m + 128)
            for c in range(4):
                bw[c, base + m, 2:14, :] = block[at + 12 * c : at + 12 * c + 12, lanes]
            ew[base + m] = block[at + 48 : at + 64, lanes]

    place(own, 0, chip, core)
    place(partner, 0, chip, other)
    place(xco, 0, beside, other)
    place(cpm, 0, beside, core)
    place(s3, 0, across, core)
    place(s3, 64, across, other)
    place(c2, 0, far, core)
    place(s3, 128, far, other)
    for i in range(4, layers + 4):
        for row in (0, 8):
            inside = rows_inside(row, 8 * d - 4, 8 * devs, 128)
            start_chunk(y0, i, row, 1, 2.0, ew, i, wt, i, bw, i, inside)
    for i in range(4, layers + 4):
        for row in (0, 8):
            sweep_chunk(y1, y0, i, row, 1, 2.0, ew, i, wt, i, bw, i)
    lane = lax.broadcasted_iota(jnp.int32, (4, 128), 1)
    for m in range(groups):
        at = 2 * m + 4
        a = residual_chunk(y1, at, 4, 1, 2.0, ew, at, bw, at)
        b = residual_chunk(y1, at + 1, 4, 1, 2.0, ew, at + 1, bw, at + 1)
        for c in range(5):
            pair[m, c] = a[c] + b[c] if c < 4 else get(ew, (at,), 4) + get(ew, (at + 1,), 4)
    for m in range(groups):
        for c in range(5):
            rows = pair[m, c, pl.ds(0, 4, stride=2), :] + pair[m, c, pl.ds(1, 4, stride=2), :]
            mate = jnp.where(lane % 2 == 0, pltpu.roll(rows, 127, 1), pltpu.roll(rows, 1, 1))
            low[c, m, 0:4, :] = (rows + mate) * (0.5 if c < 4 else 0.125)
    for c in range(5):
        for q in range(groups // 2):
            packed = jnp.where(lane % 2 == 0, low[c, 2 * q, 0:4, :], low[c, 2 * q + 1, 0:4, :])
            at = 4 * (c * (groups // 2) + q)
            for out in (next_o, low_o):
                out[at : at + 4, :] = packed
    base = 20 * (groups // 2)
    up = core == 0
    for c in range(4):
        for j in range(8):
            at, i = base + 3 * (8 * c + j), 4 * chip + 2 + j
            next_o[at : at + 3, :] = pick(up, y1[c, i, 8:11, :], y1[c, i, 5:8, :])
        for j in range(4):
            at, i = base + 96 + 4 * c + j, 4 * chip + 4 + j
            next_o[at : at + 1, :] = pick(up, bw[c, i, 9:10, :], bw[c, i, 6:7, :])
    for j in range(10):
        e_o[j] = ew[2 * g + j]
        w_o[j] = wt[2 * g + j]
        for c in range(4):
            y_o[c, j] = y1[c, 2 * g + j]
            b_o[c, j] = bw[c, 2 * g + j]


def up_all(groups, devs, idx, low, by1, by2, swapped, y_i, b_i, e1, w1, x1, ew, wt, fw, own_edge, far_edge, sol_o, res_o,
           e2, w2, b2, z0, z1, b1, ya, yb, rep, va, vb):
    g, d = idx[0], idx[1]
    core = g % 2
    zero = jnp.zeros((32, 128), F32)
    lane = lax.broadcasted_iota(jnp.int32, (4, 128), 1)
    even = lane % 2 == 0

    for i in (0, 1, groups + 2, groups + 3):
        e2[i] = zero
        for c in range(4):
            z0[c, i] = zero
            z1[c, i] = zero
    for i in range(2, groups + 2):
        e2[i, 0:8, :] = zero[0:8]
        e2[i, 16:32, :] = zero[0:16]
        for c in range(4):
            b2[c, i, 0:8, :] = zero[0:8]
            b2[c, i, 16:32, :] = zero[0:16]
    tall = 20 * (groups // 2)
    by1_rows = tall + 112
    first_core = core == 0

    def from_second(by, offset, at, rows=4):
        a, b = by[at : at + rows, :], swapped[offset + at : offset + at + rows, :]
        return pick(first_core, a, b), pick(first_core, b, a)

    for away in (-2, -1, 0, 1, 2):
        row = 10 + 4 * away
        there = 1.0 if away == 0 else jnp.where((d + away >= 0) & (d + away < devs), 1.0, 0.0)
        for c in range(5):
            for q in range(groups // 2):
                at = 4 * (c * (groups // 2) + q)
                if away == 0:
                    packed = low[at : at + 4, :]
                else:
                    by, offset = (by1, 0) if away in (-1, 1) else (by2, by1_rows)
                    packed = from_second(by, offset, at)[0 if away < 0 else 1]
                first = jnp.where(even, packed, pltpu.roll(packed, 1, 1))
                second = jnp.where(even, pltpu.roll(packed, 127, 1), packed)
                if c == 4:
                    e2[2 * q + 2, row : row + 4, :] = first * there
                    e2[2 * q + 3, row : row + 4, :] = second * there
                else:
                    b2[c, 2 * q + 2, row : row + 4, :] = first
                    b2[c, 2 * q + 3, row : row + 4, :] = second
    for i in range(2, groups + 2):
        for row in (0, 8, 16):
            inside = rows_inside(row, 4 * d - 10, 4 * devs, 128)
            start_chunk(z0, i, row, 2, 4.0, e2, i, w2, i, b2, i, inside)
    here, other = z0, z1
    for k in range(COARSE - 1):
        for i in range(2, groups + 2):
            for row in (4, 12) if k < COARSE - 2 else (8,):
                sweep_chunk(other, here, i, row, 2, 4.0, e2, i, w2, i, b2, i)
        here, other = other, here
    z = here

    low_y, high_y = jnp.where(d > 0, 1.0, 0.0), jnp.where(d < devs - 1, 1.0, 0.0)

    def mid_halo(at, rows):
        a, b = from_second(by1, 0, at, rows), from_second(by1, 0, at + 2 * rows, rows)
        return pick(first_core, a[0], b[0]), pick(first_core, a[1], b[1])

    for c in range(4):
        for k in range(5):
            rows = z[c, g + k, 8:16, :]
            rep[c, k, pl.ds(0, 8, stride=2), :] = rows
            rep[c, k, pl.ds(1, 8, stride=2), :] = rows
    for c in range(4):
        for j in range(10):
            b1[c, j] = b_i[c, j]
            ya[c, j] = y_i[c, j]
        for j in range(2):
            before, after = mid_halo(tall + 96 + 4 * c + j, 1)
            b1[c, 4 + j, 1:2, :] = before
            b1[c, 4 + j, 14:15, :] = after
        for j in range(6):
            before, after = mid_halo(tall + 3 * (8 * c + j), 3)
            ya[c, 2 + j, 0:3, :] = before * low_y
            ya[c, 2 + j, 13:16, :] = after * high_y
        for j in range(10):
            ya[c, j] = ya[c, j] + rep[c, j // 2]
    for at in range(1, 9):
        for row in (0, 8) if 1 < at < 8 else (4,):
            sweep_chunk(yb, ya, at, row, 1, 2.0, e1, at, w1, at, b1, at)
    for at in range(2, 8):
        for row in (0, 8) if 2 < at < 7 else (4,):
            sweep_chunk(ya, yb, at, row, 1, 2.0, e1, at, w1, at, b1, at)

    low_x, high_x = jnp.where(g > 0, 1.0, 0.0), jnp.where(g < groups - 1, 1.0, 0.0)
    for c in range(4):
        for m in range(6):
            for k in range(2):
                both = spread(ya[c, 2 + m, 8 * k : 8 * k + 8, :])
                rows = slice(16 * k, 16 * k + 16)
                for layer in (2 * m, 2 * m + 1):
                    for n in range(2):
                        if 3 <= layer <= 8:
                            va[c, layer, n, rows, :] = both[n] + x1[c, layer - 2, n, rows, :]
                        elif 1 <= layer <= 10:
                            va[c, layer, n, rows, :] = both[n]
        for j in range(2):
            at = 64 + 18 * (2 * c + j)
            own, far = own_edge[at : at + 18, :], far_edge[at : at + 18, :]
            before = jnp.where(core == 0, far, own) * low_x
            after = jnp.where(core == 0, own, far) * high_x
            put(va, (c, 1 + j), 7, get(va, (c, 1 + j), 7, 18) + before)
            put(va, (c, 9 + j), 7, get(va, (c, 9 + j), 7, 18) + after)
    for at in range(2, 10):
        for row in (4, 12, 20) if 2 < at < 9 else (8, 16):
            sweep_chunk(vb, va, at, row, 1, 1.0, ew, at - 1, wt, at - 2, fw, at - 2)
    for at in range(3, 9):
        for row in (4, 12, 20) if 3 < at < 8 else (8, 16):
            sweep_chunk(va, vb, at, row, 1, 1.0, ew, at - 1, wt, at - 2, fw, at - 2)
    for i in range(4):
        for row in (8, 16):
            out = residual_chunk(va, i + 4, row, 1, 1.0, ew, i + 3, fw, i + 2)
            for c in range(4):
                sol_o[c, i, row - 8 : row, :] = get(va, (c, i + 4), row)
                res_o[c, i, row - 8 : row, :] = 0.5 * out[c]


def call(kernel, outs, scratch, *args):
    specs = [pl.BlockSpec(memory_space=pltpu.SMEM)] + [pl.BlockSpec(memory_space=pltpu.VMEM)] * (len(args) - 1)
    return pl.pallas_call(
        kernel,
        out_shape=[jax.ShapeDtypeStruct(shape, F32) for shape in outs],
        in_specs=specs,
        out_specs=[pl.BlockSpec(memory_space=pltpu.VMEM)] * len(outs),
        scratch_shapes=[pltpu.VMEM(shape, F32) for shape in scratch],
        compiler_params=pltpu.CompilerParams(vmem_limit_bytes=VMEM_LIMIT),
    )(*args)


def local(forcing, viscosity):
    groups, devs = lax.axis_size("grp"), lax.axis_size("dev")
    idx = jnp.stack([lax.axis_index("grp"), lax.axis_index("dev")]).astype(jnp.int32)
    swap = [(i, i ^ 1) for i in range(groups)]
    beside = [(i, (i + 1) % groups if i % 2 else (i - 1) % groups) for i in range(groups)]
    next_chip = [(i, (i - 2) % groups if i % 2 else (i + 2) % groups) for i in range(groups)]
    far_chip = [(i, (i + 4) % groups) for i in range(groups)]
    even = [(i, i ^ 1) for i in range(devs)]
    odd = [(i, (i + 1) % devs if i % 2 else (i - 1) % devs) for i in range(devs)]

    def along(step):
        to = [(g, (d - step if g % 2 else d + step) % devs) for g in range(groups) for d in range(devs)]
        return [(i, g * devs + d) for i, (g, d) in enumerate(to)]

    f_first, f_last, visc = lax.optimization_barrier((forcing[:, 0:2], forcing[:, 2:4], viscosity))
    first = jnp.concatenate([f_first.reshape(8, 16, 256), visc[0:3]], axis=0)
    last = jnp.concatenate([f_last.reshape(8, 16, 256), visc[1:4]], axis=0)
    cross, inner = pick(idx[0] % 2 == 0, first, last), pick(idx[0] % 2 == 0, last, first)
    cross, inner = lax.optimization_barrier((cross, inner))
    cross, inner = lax.ppermute(cross, "grp", beside), lax.ppermute(inner, "grp", swap)
    to_even, to_odd = call(pack_second, [(SECOND_ROWS, 256)] * 2, [], idx, forcing, viscosity, cross, inner)
    from_odd, from_even = lax.ppermute(to_odd, "dev", odd), lax.ppermute(to_even, "dev", even)
    mid, pay, x1, ew, wt, fw = call(
        lambda *refs: fine_down(groups, devs, *refs),
        [(64, 256), (208, 256), (4, 8, 2, 32, 128), (10, 2, 32, 128), (8, 2, 32, 128), (4, 8, 2, 32, 128)],
        [(4, 8, 2, 32, 128), (10, 32, 256), (320, 128)],
        idx, forcing, viscosity, cross, inner, from_odd, from_even,
    )

    xco = lax.ppermute(pay, "grp", beside)
    c2 = lax.ppermute(mid, "grp", far_chip)
    cpm = lax.ppermute(mid, "grp", next_chip)
    partner = lax.ppermute(pay, "grp", swap)
    s3 = lax.ppermute(jnp.concatenate([xco[:64], cpm, c2], axis=0), "grp", swap)

    layers = 2 * groups + 8
    tall = 20 * (groups // 2)
    to_next, low, y_w, b_w, e_w, w_w = call(
        lambda *refs: mid_down(groups, devs, *refs),
        [(tall + 112, 128), (tall, 128), (4, 10, 16, 128), (4, 10, 16, 128), (10, 16, 128), (10, 16, 128)],
        [(4, layers, 16, 128), (layers, 16, 128), (layers, 16, 128), (4, layers, 16, 128), (4, layers, 16, 128),
         (groups, 5, 8, 128), (5, groups, 8, 128)],
        idx, mid, partner, xco, cpm, c2, s3,
    )

    by1 = lax.ppermute(to_next, ("grp", "dev"), along(1))
    by2 = lax.ppermute(low, ("grp", "dev"), along(2))
    swapped = lax.ppermute(jnp.concatenate([by1, by2], axis=0), "grp", swap)
    deep = groups + 4
    return tuple(call(
        lambda *refs: up_all(groups, devs, *refs),
        [(4, 4, 16, 256), (4, 4, 16, 256)],
        [(deep, 32, 128), (deep, 32, 128), (4, deep, 32, 128), (4, deep, 32, 128), (4, deep, 32, 128),
         (4, 10, 16, 128), (4, 10, 16, 128), (4, 10, 16, 128), (4, 5, 16, 128),
         (4, 12, 2, 32, 128), (4, 12, 2, 32, 128)],
        idx, low, by1, by2, swapped, y_w, b_w, e_w, w_w, x1, ew, wt, fw, partner, xco,
    ))


def solution(mesh):
    in_specs = (P(None, "grp", "dev", None), P("grp", "dev", None))
    out_specs = (P(None, "grp", "dev", None), P(None, "grp", "dev", None))
    return jax.shard_map(local, mesh=mesh, in_specs=in_specs, out_specs=out_specs, check_vma=False)
```

```python
import jax
import jax.numpy as jnp
from jax import lax
from jax.experimental import pallas as pl
from jax.experimental.pallas import tpu as pltpu
from jax.sharding import PartitionSpec as P

COARSE = 6
OMEGA = 0.6
BETA = 0.25
F32 = jnp.float32
VMEM_LIMIT = 48 * 1024 * 1024


def shifts(value, step):
    rows, lanes = value.shape
    lane = lax.broadcasted_iota(jnp.int32, (rows, 128), 1)
    if lanes == 256:
        low, high = value[:, :128], value[:, 128:]
        low_up, high_up = pltpu.roll(low, 127, 1), pltpu.roll(high, 127, 1)
        low_dn, high_dn = pltpu.roll(low, 1, 1), pltpu.roll(high, 1, 1)
        last, first = lane == 127, lane == 0
        plus = jnp.concatenate([jnp.where(last, high_up, low_up), jnp.where(last, 0.0, high_up)], 1)
        minus = jnp.concatenate([jnp.where(first, 0.0, low_dn), jnp.where(first, low_dn, high_dn)], 1)
        return plus, minus
    plus = jnp.where(lane >= 128 - step, 0.0, pltpu.roll(value, 128 - step, 1))
    minus = jnp.where(lane < step, 0.0, pltpu.roll(value, step, 1))
    return plus, minus


def get(ref, lead, row, count=8):
    if len(ref.shape) == len(lead) + 3:
        return jnp.concatenate([ref[(*lead, n, pl.ds(row, count))] for n in range(2)], 1)
    return ref[(*lead, pl.ds(row, count))]


def put(ref, lead, row, value):
    rows = pl.ds(row, value.shape[0])
    if len(ref.shape) == len(lead) + 3:
        for n in range(2):
            ref[(*lead, n, rows)] = value[:, 128 * n : 128 * n + 128]
    else:
        ref[(*lead, rows)] = value


def around(ref, lead, layer, row, step):
    rows = ref.shape[-2]
    here = get(ref, (*lead, layer), row)
    near = [get(ref, (*lead, layer + 1), row), get(ref, (*lead, layer - 1), row)]
    near.append(get(ref, (*lead, layer), row + 1) if row + 9 <= rows else pltpu.roll(here, 7, 0))
    near.append(get(ref, (*lead, layer), row - 1) if row >= 1 else pltpu.roll(here, 1, 0))
    return here, [*near, *shifts(here, step)]


def sums_of(visc, layer, row, step):
    here, near = around(visc, (), layer, row, step)
    sums = [here + other for other in near]
    return here, sums, sum(sums[1:], sums[0])


def stencil(field, layer, row, step, sums):
    here, flux, grad, div = [], [], None, None
    for comp in range(4):
        centre, near = around(field, (comp,), layer, row, step)
        here.append(centre)
        if comp < 3:
            terms = [s * n for s, n in zip(sums, near)]
            flux.append(sum(terms[1:], terms[0]))
            diff = near[2 * comp] - near[2 * comp + 1]
            div = diff if div is None else div + diff
        else:
            grad = [near[2 * c] - near[2 * c + 1] for c in range(3)]
    return here, flux, grad, div


def times(spacing, value):
    return value if spacing == 1.0 else spacing * value


def sweep_chunk(out, field, layer, row, step, spacing, visc, visc_layer, weight, weight_layer, source, source_layer):
    e_here, sums, _ = sums_of(visc, visc_layer, row, step)
    here, flux, grad, div = stencil(field, layer, row, step, sums)
    w = get(weight, (weight_layer,), row)
    for c in range(3):
        b = get(source, (c, source_layer), row)
        value = (1.0 - OMEGA) * here[c] + w * (b + flux[c] - times(spacing, grad[c]))
        put(out, (c, layer), row, value)
    b = get(source, (3, source_layer), row)
    put(out, (3, layer), row, here[3] + (BETA * 0.5 / (spacing * spacing) * e_here) * (b - times(spacing, div)))


def residual_chunk(field, layer, row, step, spacing, visc, visc_layer, source, source_layer):
    _, sums, total = sums_of(visc, visc_layer, row, step)
    here, flux, grad, div = stencil(field, layer, row, step, sums)
    out = []
    for c in range(3):
        b = get(source, (c, source_layer), row)
        out.append(b - (total * here[c] - flux[c] + times(spacing, grad[c])))
    out.append(get(source, (3, source_layer), row) - times(spacing, div))
    return out


def start_chunk(out, layer, row, step, spacing, visc, visc_layer, weight, weight_layer, source, source_layer, inside):
    e_here, _, total = sums_of(visc, visc_layer, row, step)
    w = jnp.where(inside, OMEGA / total, 0.0)
    put(weight, (weight_layer,), row, w)
    for c in range(4):
        scale = w if c < 3 else BETA * 0.5 / (spacing * spacing) * e_here
        put(out, (c, layer), row, scale * get(source, (c, source_layer), row))


def rows_inside(row, first, count, lanes):
    at = lax.broadcasted_iota(jnp.int32, (8, lanes), 0) + (row + first)
    return (at >= 0) & (at < count)


def take(value, at, axis):
    return jnp.take_along_axis(value, at, axis=axis)


def fold(value):
    a = lax.broadcasted_iota(jnp.int32, (256, 128), 0)
    b = lax.broadcasted_iota(jnp.int32, (256, 128), 1)
    pairs = jnp.where(a // 2 == b, 1.0, 0.0).astype(jnp.bfloat16)
    total = None
    for _ in range(3):
        part = value.astype(jnp.bfloat16)
        term = jnp.dot(part, pairs, preferred_element_type=F32)
        total = term if total is None else total + term
        value = value - part.astype(F32)
    return total


def spread(value):
    lane = lax.broadcasted_iota(jnp.int32, (8, 128), 1)
    row = lax.broadcasted_iota(jnp.int32, (8, 128), 0)
    out = []
    for n in range(2):
        wide = take(value, lane // 2 + 64 * n, 1)
        out.append(jnp.concatenate([take(wide, row // 2 + 4 * m, 0) for m in range(2)], 0))
    return out


def pick(condition, a, b):
    return jnp.where(condition, a, b)


def halo_first(idx, cross, inner, n):
    even = idx[0] % 2 == 0
    a, b = cross[n], inner[n]
    return pick(even, a, b), pick(even, b, a)


F_ROWS = (4, 5, 6, 6, 6, 6, 5, 4)
E_ROWS = (4, 5, 6, 8, 8, 8, 8, 6, 5, 4)
F_AT = tuple(4 * sum(F_ROWS[:n]) for n in range(9))
E_AT = tuple(F_AT[8] + sum(E_ROWS[:n]) for n in range(11))
SECOND_ROWS = 232


def pack_second(idx, f, e, cross, inner, even_o, odd_o):
    even = idx[1] % 2 == 0

    def write(at, rows, value):
        size = value.shape[0]
        low, high = value[0:rows, :], value[size - rows : size, :]
        even_o[at : at + rows, :] = pick(even, high, low)
        odd_o[at : at + rows, :] = pick(even, low, high)

    for layer in range(10):
        if 3 <= layer <= 6:
            value = e[layer - 3]
        else:
            value = halo_first(idx, cross, inner, 8 + layer)[0] if layer < 3 else halo_first(idx, cross, inner, 1 + layer)[1]
        write(E_AT[layer], E_ROWS[layer], value)
    for layer in range(8):
        for c in range(4):
            if 2 <= layer <= 5:
                value = f[c, layer - 2]
            elif layer < 2:
                value = halo_first(idx, cross, inner, 2 * c + layer)[0]
            else:
                value = halo_first(idx, cross, inner, 2 * c + layer - 6)[1]
            write(F_AT[layer] + F_ROWS[layer] * c, F_ROWS[layer], value)
    even_o[E_AT[10] : SECOND_ROWS, :] = jnp.zeros((SECOND_ROWS - E_AT[10], 256), F32)
    odd_o[E_AT[10] : SECOND_ROWS, :] = jnp.zeros((SECOND_ROWS - E_AT[10], 256), F32)


def fine_down(groups, devs, idx, f, e, cross, inner, odd, even, mid_o, pay_o, x1, ew, wt, fw, x0, pair, half):
    g, d = idx[0], idx[1]
    low_x, high_x = jnp.where(g > 0, 1.0, 0.0), jnp.where(g < groups - 1, 1.0, 0.0)
    low_y, high_y = jnp.where(d > 0, 1.0, 0.0), jnp.where(d < devs - 1, 1.0, 0.0)
    even_dev = d % 2 == 0

    def halo_second(at):
        a, b = odd[at, :], even[at, :]
        return pick(even_dev, a, b), pick(even_dev, b, a)

    for layer in range(10):
        if layer < 3:
            own = halo_first(idx, cross, inner, 8 + layer)[0]
        else:
            own = halo_first(idx, cross, inner, 1 + layer)[1] if layer > 6 else e[layer - 3]
        s = low_x if layer < 3 else high_x if layer > 6 else 1.0
        rows = E_ROWS[layer]
        before, after = halo_second(slice(E_AT[layer], E_AT[layer] + rows))
        before, after = before * (s * low_y), after * (s * high_y)
        if rows < 8:
            ones = jnp.ones((8 - rows, 256), F32)
            before, after = jnp.concatenate([ones, before], 0), jnp.concatenate([after, ones], 0)
        put(ew, (layer,), 0, before)
        put(ew, (layer,), 8, own * s)
        put(ew, (layer,), 24, after)
    for layer in range(8):
        for c in range(4):
            if layer < 2:
                own = halo_first(idx, cross, inner, 2 * c + layer)[0]
            else:
                own = halo_first(idx, cross, inner, 2 * c + layer - 6)[1] if layer > 5 else f[c, layer - 2]
            at = F_AT[layer] + F_ROWS[layer] * c
            before, after = halo_second(slice(at, at + F_ROWS[layer]))
            zero = jnp.zeros((8 - F_ROWS[layer], 256), F32)
            put(fw, (c, layer), 0, jnp.concatenate([zero, 2.0 * before], 0))
            put(fw, (c, layer), 8, 2.0 * own)
            put(fw, (c, layer), 24, jnp.concatenate([2.0 * after, zero], 0))
    for layer in range(8):
        layer_in = (4 * g - 2 + layer >= 0) & (4 * g - 2 + layer < 4 * groups)
        for row in (0, 8, 16, 24) if 0 < layer < 7 else (4, 12, 20):
            inside = rows_inside(row, 16 * d - 8, 16 * devs, 256) & layer_in
            start_chunk(x0, layer, row, 1, 1.0, ew, layer + 1, wt, layer, fw, layer, inside)
    for layer in range(1, 7):
        for row in (0, 8, 16, 24) if 1 < layer < 6 else (4, 12, 20):
            sweep_chunk(x1, x0, layer, row, 1, 1.0, ew, layer + 1, wt, layer, fw, layer)
    for m in range(2):
        for row in (4, 12, 20):
            a = residual_chunk(x1, 2 * m + 2, row, 1, 1.0, ew, 2 * m + 3, fw, 2 * m + 2)
            b = residual_chunk(x1, 2 * m + 3, row, 1, 1.0, ew, 2 * m + 4, fw, 2 * m + 3)
            for c in range(4):
                pair[2 * c + m, row : row + 8, :] = a[c] + b[c]
        for c in range(4):
            pair[2 * c + m, 0:4, :] = jnp.zeros((4, 256), F32)
            pair[2 * c + m, 28:32, :] = jnp.zeros((4, 256), F32)
        pair[8 + m] = get(ew, (2 * m + 3,), 0, 32) + get(ew, (2 * m + 4,), 0, 32)
    half[...] = fold(pair[...].reshape(320, 256))
    coarse = half[pl.ds(0, 160, stride=2), :] + half[pl.ds(1, 160, stride=2), :]
    coarse = coarse.reshape(10, 16, 128)
    for m in range(2):
        lanes = slice(128 * m, 128 * m + 128)
        for c in range(4):
            mid_o[12 * c : 12 * c + 12, lanes] = pay_o[12 * c : 12 * c + 12, lanes] = coarse[2 * c + m, 2:14, :] * 0.5
        mid_o[48:64, lanes] = pay_o[48:64, lanes] = coarse[8 + m] * 0.125
    for c in range(4):
        for j in range(2):
            at = 64 + 18 * (2 * c + j)
            pay_o[at : at + 18, :] = get(x1, (c, 3 + j), 7, 18)


def mid_down(groups, devs, idx, own, partner, xco, cpm, c2, s3, next_o, low_o, y_o, b_o, e_o, w_o, bw, ew, wt, y0, y1, pair, low):
    g, d = idx[0], idx[1]
    chips = groups // 2
    chip, core = g // 2, g % 2
    other = 1 - core
    beside = (chip + chips - 1 + 2 * core) % chips
    across = (chip + 1 + (chips - 2) * core) % chips
    far = (chip + 2) % chips
    layers = 2 * groups
    zero = jnp.zeros((16, 128), F32)
    for i in (0, 1, 2, 3, layers + 4, layers + 5, layers + 6, layers + 7):
        ew[i] = zero
        wt[i] = zero
        for c in range(4):
            bw[c, i] = zero
            y0[c, i] = zero
            y1[c, i] = zero
    for i in range(layers):
        for c in range(4):
            bw[c, i + 4, 0:2, :] = zero[0:2]
            bw[c, i + 4, 14:16, :] = zero[0:2]

    def place(block, at, which, core_at):
        base = 4 + 4 * which + 2 * core_at
        for m in range(2):
            lanes = slice(128 * m, 128 * m + 128)
            for c in range(4):
                bw[c, base + m, 2:14, :] = block[at + 12 * c : at + 12 * c + 12, lanes]
            ew[base + m] = block[at + 48 : at + 64, lanes]

    place(own, 0, chip, core)
    place(partner, 0, chip, other)
    place(xco, 0, beside, other)
    place(cpm, 0, beside, core)
    place(s3, 0, across, core)
    place(s3, 64, across, other)
    place(c2, 0, far, core)
    place(s3, 128, far, other)
    for i in range(4, layers + 4):
        for row in (0, 8):
            inside = rows_inside(row, 8 * d - 4, 8 * devs, 128)
            start_chunk(y0, i, row, 1, 2.0, ew, i, wt, i, bw, i, inside)
    for i in range(4, layers + 4):
        for row in (0, 8):
            sweep_chunk(y1, y0, i, row, 1, 2.0, ew, i, wt, i, bw, i)
    lane = lax.broadcasted_iota(jnp.int32, (4, 128), 1)
    for m in range(groups):
        at = 2 * m + 4
        a = residual_chunk(y1, at, 4, 1, 2.0, ew, at, bw, at)
        b = residual_chunk(y1, at + 1, 4, 1, 2.0, ew, at + 1, bw, at + 1)
        for c in range(5):
            pair[m, c] = a[c] + b[c] if c < 4 else get(ew, (at,), 4) + get(ew, (at + 1,), 4)
    for m in range(groups):
        for c in range(5):
            rows = pair[m, c, pl.ds(0, 4, stride=2), :] + pair[m, c, pl.ds(1, 4, stride=2), :]
            mate = jnp.where(lane % 2 == 0, pltpu.roll(rows, 127, 1), pltpu.roll(rows, 1, 1))
            low[c, m, 0:4, :] = (rows + mate) * (0.5 if c < 4 else 0.125)
    for c in range(5):
        for q in range(groups // 2):
            packed = jnp.where(lane % 2 == 0, low[c, 2 * q, 0:4, :], low[c, 2 * q + 1, 0:4, :])
            at = 4 * (c * (groups // 2) + q)
            for out in (next_o, low_o):
                out[at : at + 4, :] = packed
    base = 20 * (groups // 2)
    up = core == 0
    for c in range(4):
        for j in range(8):
            at, i = base + 3 * (8 * c + j), 4 * chip + 2 + j
            next_o[at : at + 3, :] = pick(up, y1[c, i, 8:11, :], y1[c, i, 5:8, :])
        for j in range(4):
            at, i = base + 96 + 4 * c + j, 4 * chip + 4 + j
            next_o[at : at + 1, :] = pick(up, bw[c, i, 9:10, :], bw[c, i, 6:7, :])
    for j in range(10):
        e_o[j] = ew[2 * g + j]
        w_o[j] = wt[2 * g + j]
        for c in range(4):
            y_o[c, j] = y1[c, 2 * g + j]
            b_o[c, j] = bw[c, 2 * g + j]


def up_all(groups, devs, idx, low, by1, by2, swapped, y_i, b_i, e1, w1, x1, ew, wt, fw, own_edge, far_edge, sol_o, res_o,
           e2, w2, b2, z0, z1, b1, ya, yb, rep, va, vb):
    g, d = idx[0], idx[1]
    core = g % 2
    zero = jnp.zeros((32, 128), F32)
    lane = lax.broadcasted_iota(jnp.int32, (4, 128), 1)
    even = lane % 2 == 0

    for i in (0, 1, groups + 2, groups + 3):
        e2[i] = zero
        for c in range(4):
            z0[c, i] = zero
            z1[c, i] = zero
    for i in range(2, groups + 2):
        e2[i, 0:8, :] = zero[0:8]
        e2[i, 16:32, :] = zero[0:16]
        for c in range(4):
            b2[c, i, 0:8, :] = zero[0:8]
            b2[c, i, 16:32, :] = zero[0:16]
    tall = 20 * (groups // 2)
    by1_rows = tall + 112
    first_core = core == 0

    def from_second(by, offset, at, rows=4):
        a, b = by[at : at + rows, :], swapped[offset + at : offset + at + rows, :]
        return pick(first_core, a, b), pick(first_core, b, a)

    for away in (-2, -1, 0, 1, 2):
        row = 10 + 4 * away
        there = 1.0 if away == 0 else jnp.where((d + away >= 0) & (d + away < devs), 1.0, 0.0)
        for c in range(5):
            for q in range(groups // 2):
                at = 4 * (c * (groups // 2) + q)
                if away == 0:
                    packed = low[at : at + 4, :]
                else:
                    by, offset = (by1, 0) if away in (-1, 1) else (by2, by1_rows)
                    packed = from_second(by, offset, at)[0 if away < 0 else 1]
                first = jnp.where(even, packed, pltpu.roll(packed, 1, 1))
                second = jnp.where(even, pltpu.roll(packed, 127, 1), packed)
                if c == 4:
                    e2[2 * q + 2, row : row + 4, :] = first * there
                    e2[2 * q + 3, row : row + 4, :] = second * there
                else:
                    b2[c, 2 * q + 2, row : row + 4, :] = first
                    b2[c, 2 * q + 3, row : row + 4, :] = second
    for i in range(2, groups + 2):
        for row in (0, 8, 16):
            inside = rows_inside(row, 4 * d - 10, 4 * devs, 128)
            start_chunk(z0, i, row, 2, 4.0, e2, i, w2, i, b2, i, inside)
    here, other = z0, z1
    for k in range(COARSE - 1):
        for i in range(2, groups + 2):
            for row in (4, 12) if k < COARSE - 2 else (8,):
                sweep_chunk(other, here, i, row, 2, 4.0, e2, i, w2, i, b2, i)
        here, other = other, here
    z = here

    low_y, high_y = jnp.where(d > 0, 1.0, 0.0), jnp.where(d < devs - 1, 1.0, 0.0)

    def mid_halo(at, rows):
        a, b = from_second(by1, 0, at, rows), from_second(by1, 0, at + 2 * rows, rows)
        return pick(first_core, a[0], b[0]), pick(first_core, a[1], b[1])

    for c in range(4):
        for k in range(5):
            rows = z[c, g + k, 8:16, :]
            rep[c, k, pl.ds(0, 8, stride=2), :] = rows
            rep[c, k, pl.ds(1, 8, stride=2), :] = rows
    for c in range(4):
        for j in range(10):
            b1[c, j] = b_i[c, j]
            ya[c, j] = y_i[c, j]
        for j in range(2):
            before, after = mid_halo(tall + 96 + 4 * c + j, 1)
            b1[c, 4 + j, 1:2, :] = before
            b1[c, 4 + j, 14:15, :] = after
        for j in range(6):
            before, after = mid_halo(tall + 3 * (8 * c + j), 3)
            ya[c, 2 + j, 0:3, :] = before * low_y
            ya[c, 2 + j, 13:16, :] = after * high_y
        for j in range(10):
            ya[c, j] = ya[c, j] + rep[c, j // 2]
    for at in range(1, 9):
        for row in (0, 8) if 1 < at < 8 else (4,):
            sweep_chunk(yb, ya, at, row, 1, 2.0, e1, at, w1, at, b1, at)
    for at in range(2, 8):
        for row in (0, 8) if 2 < at < 7 else (4,):
            sweep_chunk(ya, yb, at, row, 1, 2.0, e1, at, w1, at, b1, at)

    low_x, high_x = jnp.where(g > 0, 1.0, 0.0), jnp.where(g < groups - 1, 1.0, 0.0)
    for c in range(4):
        for m in range(6):
            for k in range(2):
                both = spread(ya[c, 2 + m, 8 * k : 8 * k + 8, :])
                rows = slice(16 * k, 16 * k + 16)
                for layer in (2 * m, 2 * m + 1):
                    for n in range(2):
                        if 3 <= layer <= 8:
                            va[c, layer, n, rows, :] = both[n] + x1[c, layer - 2, n, rows, :]
                        elif 1 <= layer <= 10:
                            va[c, layer, n, rows, :] = both[n]
        for j in range(2):
            at = 64 + 18 * (2 * c + j)
            own, far = own_edge[at : at + 18, :], far_edge[at : at + 18, :]
            before = jnp.where(core == 0, far, own) * low_x
            after = jnp.where(core == 0, own, far) * high_x
            put(va, (c, 1 + j), 7, get(va, (c, 1 + j), 7, 18) + before)
            put(va, (c, 9 + j), 7, get(va, (c, 9 + j), 7, 18) + after)
    for at in range(2, 10):
        for row in (4, 12, 20) if 2 < at < 9 else (8, 16):
            sweep_chunk(vb, va, at, row, 1, 1.0, ew, at - 1, wt, at - 2, fw, at - 2)
    for at in range(3, 9):
        for row in (4, 12, 20) if 3 < at < 8 else (8, 16):
            sweep_chunk(va, vb, at, row, 1, 1.0, ew, at - 1, wt, at - 2, fw, at - 2)
    for i in range(4):
        for row in (8, 16):
            out = residual_chunk(va, i + 4, row, 1, 1.0, ew, i + 3, fw, i + 2)
            for c in range(4):
                sol_o[c, i, row - 8 : row, :] = get(va, (c, i + 4), row)
                res_o[c, i, row - 8 : row, :] = 0.5 * out[c]


def call(kernel, outs, scratch, *args):
    specs = [pl.BlockSpec(memory_space=pltpu.SMEM)] + [pl.BlockSpec(memory_space=pltpu.VMEM)] * (len(args) - 1)
    return pl.pallas_call(
        kernel,
        out_shape=[jax.ShapeDtypeStruct(shape, F32) for shape in outs],
        in_specs=specs,
        out_specs=[pl.BlockSpec(memory_space=pltpu.VMEM)] * len(outs),
        scratch_shapes=[pltpu.VMEM(shape, F32) for shape in scratch],
        compiler_params=pltpu.CompilerParams(vmem_limit_bytes=VMEM_LIMIT),
    )(*args)


def local(forcing, viscosity):
    groups, devs = lax.axis_size("grp"), lax.axis_size("dev")
    idx = jnp.stack([lax.axis_index("grp"), lax.axis_index("dev")]).astype(jnp.int32)
    swap = [(i, i ^ 1) for i in range(groups)]
    beside = [(i, (i + 1) % groups if i % 2 else (i - 1) % groups) for i in range(groups)]
    next_chip = [(i, (i - 2) % groups if i % 2 else (i + 2) % groups) for i in range(groups)]
    far_chip = [(i, (i + 4) % groups) for i in range(groups)]
    even = [(i, i ^ 1) for i in range(devs)]
    odd = [(i, min(max(i + 1 if i % 2 else i - 1, 0), devs - 1)) for i in range(devs)]
    beside_inside = [(i, min(max(i + 1 if i % 2 else i - 1, 0), groups - 1)) for i in range(groups)]

    def along(step):
        pairs = []
        for g in range(groups):
            for d in range(devs):
                to = d - step if g % 2 else d + step
                pairs.append((g * devs + d, g * devs + to if 0 <= to < devs else (g ^ 1) * devs + d))
        return pairs

    f_first, f_last, visc = lax.optimization_barrier((forcing[:, 0:2], forcing[:, 2:4], viscosity))
    first = jnp.concatenate([f_first.reshape(8, 16, 256), visc[0:3]], axis=0)
    last = jnp.concatenate([f_last.reshape(8, 16, 256), visc[1:4]], axis=0)
    cross, inner = pick(idx[0] % 2 == 0, first, last), pick(idx[0] % 2 == 0, last, first)
    cross, inner = lax.optimization_barrier((cross, inner))
    cross, inner = lax.ppermute(cross, "grp", beside_inside), lax.ppermute(inner, "grp", swap)
    to_even, to_odd = call(pack_second, [(SECOND_ROWS, 256)] * 2, [], idx, forcing, viscosity, cross, inner)
    from_odd, from_even = lax.ppermute(to_odd, "dev", odd), lax.ppermute(to_even, "dev", even)
    mid, pay, x1, ew, wt, fw = call(
        lambda *refs: fine_down(groups, devs, *refs),
        [(64, 256), (208, 256), (4, 8, 2, 32, 128), (10, 2, 32, 128), (8, 2, 32, 128), (4, 8, 2, 32, 128)],
        [(4, 8, 2, 32, 128), (10, 32, 256), (320, 128)],
        idx, forcing, viscosity, cross, inner, from_odd, from_even,
    )

    xco = lax.ppermute(pay, "grp", beside)
    c2 = lax.ppermute(mid, "grp", far_chip)
    cpm = lax.ppermute(mid, "grp", next_chip)
    partner = lax.ppermute(pay, "grp", swap)
    s3 = lax.ppermute(jnp.concatenate([xco[:64], cpm, c2], axis=0), "grp", swap)

    layers = 2 * groups + 8
    tall = 20 * (groups // 2)
    to_next, low, y_w, b_w, e_w, w_w = call(
        lambda *refs: mid_down(groups, devs, *refs),
        [(tall + 112, 128), (tall, 128), (4, 10, 16, 128), (4, 10, 16, 128), (10, 16, 128), (10, 16, 128)],
        [(4, layers, 16, 128), (layers, 16, 128), (layers, 16, 128), (4, layers, 16, 128), (4, layers, 16, 128),
         (groups, 5, 8, 128), (5, groups, 8, 128)],
        idx, mid, partner, xco, cpm, c2, s3,
    )

    by1 = lax.ppermute(to_next, ("grp", "dev"), along(1))
    by2 = lax.ppermute(low, ("grp", "dev"), along(2))
    swapped = lax.ppermute(jnp.concatenate([by1, by2], axis=0), "grp", swap)
    deep = groups + 4
    return tuple(call(
        lambda *refs: up_all(groups, devs, *refs),
        [(4, 4, 16, 256), (4, 4, 16, 256)],
        [(deep, 32, 128), (deep, 32, 128), (4, deep, 32, 128), (4, deep, 32, 128), (4, deep, 32, 128),
         (4, 10, 16, 128), (4, 10, 16, 128), (4, 10, 16, 128), (4, 5, 16, 128),
         (4, 12, 2, 32, 128), (4, 12, 2, 32, 128)],
        idx, low, by1, by2, swapped, y_w, b_w, e_w, w_w, x1, ew, wt, fw, partner, xco,
    ))


def solution(mesh):
    in_specs = (P(None, "grp", "dev", None), P("grp", "dev", None))
    out_specs = (P(None, "grp", "dev", None), P(None, "grp", "dev", None))
    return jax.shard_map(local, mesh=mesh, in_specs=in_specs, out_specs=out_specs, check_vma=False)
```

```python
import jax
import jax.numpy as jnp
from jax import lax
from jax.experimental import pallas as pl
from jax.experimental.pallas import tpu as pltpu
from jax.sharding import PartitionSpec as P

COARSE = 6
OMEGA = 0.6
BETA = 0.25
F32 = jnp.float32
VMEM_LIMIT = 48 * 1024 * 1024


def shifts(value, step):
    rows, lanes = value.shape
    lane = lax.broadcasted_iota(jnp.int32, (rows, 128), 1)
    if lanes == 256:
        low, high = value[:, :128], value[:, 128:]
        low_up, high_up = pltpu.roll(low, 127, 1), pltpu.roll(high, 127, 1)
        low_dn, high_dn = pltpu.roll(low, 1, 1), pltpu.roll(high, 1, 1)
        last, first = lane == 127, lane == 0
        plus = jnp.concatenate([jnp.where(last, high_up, low_up), jnp.where(last, 0.0, high_up)], 1)
        minus = jnp.concatenate([jnp.where(first, 0.0, low_dn), jnp.where(first, low_dn, high_dn)], 1)
        return plus, minus
    plus = jnp.where(lane >= 128 - step, 0.0, pltpu.roll(value, 128 - step, 1))
    minus = jnp.where(lane < step, 0.0, pltpu.roll(value, step, 1))
    return plus, minus


def get(ref, lead, row, count=8):
    if len(ref.shape) == len(lead) + 3:
        return jnp.concatenate([ref[(*lead, n, pl.ds(row, count))] for n in range(2)], 1)
    return ref[(*lead, pl.ds(row, count))]


def put(ref, lead, row, value):
    rows = pl.ds(row, value.shape[0])
    if len(ref.shape) == len(lead) + 3:
        for n in range(2):
            ref[(*lead, n, rows)] = value[:, 128 * n : 128 * n + 128]
    else:
        ref[(*lead, rows)] = value


def around(ref, lead, layer, row, step):
    rows = ref.shape[-2]
    here = get(ref, (*lead, layer), row)
    near = [get(ref, (*lead, layer + 1), row), get(ref, (*lead, layer - 1), row)]
    near.append(get(ref, (*lead, layer), row + 1) if row + 9 <= rows else pltpu.roll(here, 7, 0))
    near.append(get(ref, (*lead, layer), row - 1) if row >= 1 else pltpu.roll(here, 1, 0))
    return here, [*near, *shifts(here, step)]


def sums_of(visc, layer, row, step):
    here, near = around(visc, (), layer, row, step)
    sums = [here + other for other in near]
    return here, sums, sum(sums[1:], sums[0])


def stencil(field, layer, row, step, sums):
    here, flux, grad, div = [], [], None, None
    for comp in range(4):
        centre, near = around(field, (comp,), layer, row, step)
        here.append(centre)
        if comp < 3:
            terms = [s * n for s, n in zip(sums, near)]
            flux.append(sum(terms[1:], terms[0]))
            diff = near[2 * comp] - near[2 * comp + 1]
            div = diff if div is None else div + diff
        else:
            grad = [near[2 * c] - near[2 * c + 1] for c in range(3)]
    return here, flux, grad, div


def times(spacing, value):
    return value if spacing == 1.0 else spacing * value


def sweep_chunk(out, field, layer, row, step, spacing, visc, visc_layer, weight, weight_layer, source, source_layer):
    e_here, sums, _ = sums_of(visc, visc_layer, row, step)
    here, flux, grad, div = stencil(field, layer, row, step, sums)
    w = get(weight, (weight_layer,), row)
    for c in range(3):
        b = get(source, (c, source_layer), row)
        value = (1.0 - OMEGA) * here[c] + w * (b + flux[c] - times(spacing, grad[c]))
        put(out, (c, layer), row, value)
    b = get(source, (3, source_layer), row)
    put(out, (3, layer), row, here[3] + (BETA * 0.5 / (spacing * spacing) * e_here) * (b - times(spacing, div)))


def residual_chunk(field, layer, row, step, spacing, visc, visc_layer, source, source_layer):
    _, sums, total = sums_of(visc, visc_layer, row, step)
    here, flux, grad, div = stencil(field, layer, row, step, sums)
    out = []
    for c in range(3):
        b = get(source, (c, source_layer), row)
        out.append(b - (total * here[c] - flux[c] + times(spacing, grad[c])))
    out.append(get(source, (3, source_layer), row) - times(spacing, div))
    return out


def start_chunk(out, layer, row, step, spacing, visc, visc_layer, weight, weight_layer, source, source_layer, inside):
    e_here, _, total = sums_of(visc, visc_layer, row, step)
    w = jnp.where(inside, OMEGA / total, 0.0)
    put(weight, (weight_layer,), row, w)
    for c in range(4):
        scale = w if c < 3 else BETA * 0.5 / (spacing * spacing) * e_here
        put(out, (c, layer), row, scale * get(source, (c, source_layer), row))


def rows_inside(row, first, count, lanes):
    at = lax.broadcasted_iota(jnp.int32, (8, lanes), 0) + (row + first)
    return (at >= 0) & (at < count)


def take(value, at, axis):
    return jnp.take_along_axis(value, at, axis=axis)


def fold(value):
    a = lax.broadcasted_iota(jnp.int32, (256, 128), 0)
    b = lax.broadcasted_iota(jnp.int32, (256, 128), 1)
    pairs = jnp.where(a // 2 == b, 1.0, 0.0).astype(jnp.bfloat16)
    total = None
    for _ in range(3):
        part = value.astype(jnp.bfloat16)
        term = jnp.dot(part, pairs, preferred_element_type=F32)
        total = term if total is None else total + term
        value = value - part.astype(F32)
    return total


def spread(value):
    lane = lax.broadcasted_iota(jnp.int32, (8, 128), 1)
    row = lax.broadcasted_iota(jnp.int32, (8, 128), 0)
    out = []
    for n in range(2):
        wide = take(value, lane // 2 + 64 * n, 1)
        out.append(jnp.concatenate([take(wide, row // 2 + 4 * m, 0) for m in range(2)], 0))
    return out


def pick(condition, a, b):
    return jnp.where(condition, a, b)


def halo_first(idx, cross, inner, n):
    even = idx[0] % 2 == 0
    a, b = cross[n], inner[n]
    return pick(even, a, b), pick(even, b, a)


F_ROWS = (4, 5, 6, 6, 6, 6, 5, 4)
E_ROWS = (4, 5, 6, 8, 8, 8, 8, 6, 5, 4)
F_AT = tuple(4 * sum(F_ROWS[:n]) for n in range(9))
E_AT = tuple(F_AT[8] + sum(E_ROWS[:n]) for n in range(11))
SECOND_ROWS = 232


def pack_second(idx, f, e, cross, inner, even_o, odd_o):
    even = idx[1] % 2 == 0

    def write(at, rows, value):
        size = value.shape[0]
        low, high = value[0:rows, :], value[size - rows : size, :]
        even_o[at : at + rows, :] = pick(even, high, low)
        odd_o[at : at + rows, :] = pick(even, low, high)

    for layer in range(10):
        if 3 <= layer <= 6:
            value = e[layer - 3]
        else:
            value = halo_first(idx, cross, inner, 8 + layer)[0] if layer < 3 else halo_first(idx, cross, inner, 1 + layer)[1]
        write(E_AT[layer], E_ROWS[layer], value)
    for layer in range(8):
        for c in range(4):
            if 2 <= layer <= 5:
                value = f[c, layer - 2]
            elif layer < 2:
                value = halo_first(idx, cross, inner, 2 * c + layer)[0]
            else:
                value = halo_first(idx, cross, inner, 2 * c + layer - 6)[1]
            write(F_AT[layer] + F_ROWS[layer] * c, F_ROWS[layer], value)
    even_o[E_AT[10] : SECOND_ROWS, :] = jnp.zeros((SECOND_ROWS - E_AT[10], 256), F32)
    odd_o[E_AT[10] : SECOND_ROWS, :] = jnp.zeros((SECOND_ROWS - E_AT[10], 256), F32)


def fine_down(groups, devs, idx, f, e, cross, inner, odd, even, mid_o, pay_o, x1, ew, wt, fw, x0, pair, half):
    g, d = idx[0], idx[1]
    low_x, high_x = jnp.where(g > 0, 1.0, 0.0), jnp.where(g < groups - 1, 1.0, 0.0)
    low_y, high_y = jnp.where(d > 0, 1.0, 0.0), jnp.where(d < devs - 1, 1.0, 0.0)
    even_dev = d % 2 == 0

    def halo_second(at):
        a, b = odd[at, :], even[at, :]
        return pick(even_dev, a, b), pick(even_dev, b, a)

    for layer in range(10):
        if layer < 3:
            own = halo_first(idx, cross, inner, 8 + layer)[0]
        else:
            own = halo_first(idx, cross, inner, 1 + layer)[1] if layer > 6 else e[layer - 3]
        s = low_x if layer < 3 else high_x if layer > 6 else 1.0
        rows = E_ROWS[layer]
        before, after = halo_second(slice(E_AT[layer], E_AT[layer] + rows))
        before, after = before * (s * low_y), after * (s * high_y)
        if rows < 8:
            ones = jnp.ones((8 - rows, 256), F32)
            before, after = jnp.concatenate([ones, before], 0), jnp.concatenate([after, ones], 0)
        put(ew, (layer,), 0, before)
        put(ew, (layer,), 8, own * s)
        put(ew, (layer,), 24, after)
    for layer in range(8):
        for c in range(4):
            if layer < 2:
                own = halo_first(idx, cross, inner, 2 * c + layer)[0]
            else:
                own = halo_first(idx, cross, inner, 2 * c + layer - 6)[1] if layer > 5 else f[c, layer - 2]
            at = F_AT[layer] + F_ROWS[layer] * c
            before, after = halo_second(slice(at, at + F_ROWS[layer]))
            zero = jnp.zeros((8 - F_ROWS[layer], 256), F32)
            put(fw, (c, layer), 0, jnp.concatenate([zero, 2.0 * before], 0))
            put(fw, (c, layer), 8, 2.0 * own)
            put(fw, (c, layer), 24, jnp.concatenate([2.0 * after, zero], 0))
    for layer in range(8):
        layer_in = (4 * g - 2 + layer >= 0) & (4 * g - 2 + layer < 4 * groups)
        for row in (0, 8, 16, 24) if 0 < layer < 7 else (4, 12, 20):
            inside = rows_inside(row, 16 * d - 8, 16 * devs, 256) & layer_in
            start_chunk(x0, layer, row, 1, 1.0, ew, layer + 1, wt, layer, fw, layer, inside)
    for layer in range(1, 7):
        for row in (0, 8, 16, 24) if 1 < layer < 6 else (4, 12, 20):
            sweep_chunk(x1, x0, layer, row, 1, 1.0, ew, layer + 1, wt, layer, fw, layer)
    for m in range(2):
        for row in (4, 12, 20):
            a = residual_chunk(x1, 2 * m + 2, row, 1, 1.0, ew, 2 * m + 3, fw, 2 * m + 2)
            b = residual_chunk(x1, 2 * m + 3, row, 1, 1.0, ew, 2 * m + 4, fw, 2 * m + 3)
            for c in range(4):
                pair[2 * c + m, row : row + 8, :] = a[c] + b[c]
        for c in range(4):
            pair[2 * c + m, 0:4, :] = jnp.zeros((4, 256), F32)
            pair[2 * c + m, 28:32, :] = jnp.zeros((4, 256), F32)
        pair[8 + m] = get(ew, (2 * m + 3,), 0, 32) + get(ew, (2 * m + 4,), 0, 32)
    half[...] = fold(pair[...].reshape(320, 256))
    coarse = half[pl.ds(0, 160, stride=2), :] + half[pl.ds(1, 160, stride=2), :]
    coarse = coarse.reshape(10, 16, 128)
    for m in range(2):
        lanes = slice(128 * m, 128 * m + 128)
        for c in range(4):
            mid_o[12 * c : 12 * c + 12, lanes] = pay_o[12 * c : 12 * c + 12, lanes] = coarse[2 * c + m, 2:14, :] * 0.5
        mid_o[48:64, lanes] = pay_o[48:64, lanes] = coarse[8 + m] * 0.125
    for c in range(4):
        for j in range(2):
            at = 64 + 18 * (2 * c + j)
            pay_o[at : at + 18, :] = get(x1, (c, 3 + j), 7, 18)


def mid_down(groups, devs, idx, own, partner, xco, cpm, c2, s3, next_o, low_o, y_o, b_o, e_o, w_o, bw, ew, wt, y0, y1, pair, low):
    g, d = idx[0], idx[1]
    chips = groups // 2
    chip, core = g // 2, g % 2
    other = 1 - core
    beside = (chip + chips - 1 + 2 * core) % chips
    across = (chip + 1 + (chips - 2) * core) % chips
    far = (chip + 2) % chips
    layers = 2 * groups
    zero = jnp.zeros((16, 128), F32)
    for i in (0, 1, 2, 3, layers + 4, layers + 5, layers + 6, layers + 7):
        ew[i] = zero
        wt[i] = zero
        for c in range(4):
            bw[c, i] = zero
            y0[c, i] = zero
            y1[c, i] = zero
    for i in range(layers):
        for c in range(4):
            bw[c, i + 4, 0:2, :] = zero[0:2]
            bw[c, i + 4, 14:16, :] = zero[0:2]

    def place(block, at, which, core_at):
        base = 4 + 4 * which + 2 * core_at
        for m in range(2):
            lanes = slice(128 * m, 128 * m + 128)
            for c in range(4):
                bw[c, base + m, 2:14, :] = block[at + 12 * c : at + 12 * c + 12, lanes]
            ew[base + m] = block[at + 48 : at + 64, lanes]

    place(own, 0, chip, core)
    place(partner, 0, chip, other)
    place(xco, 0, beside, other)
    place(cpm, 0, beside, core)
    place(s3, 0, across, core)
    place(s3, 64, across, other)
    place(c2, 0, far, core)
    place(s3, 128, far, other)
    for i in range(4, layers + 4):
        for row in (0, 8):
            inside = rows_inside(row, 8 * d - 4, 8 * devs, 128)
            start_chunk(y0, i, row, 1, 2.0, ew, i, wt, i, bw, i, inside)
    for i in range(4, layers + 4):
        for row in (0, 8):
            sweep_chunk(y1, y0, i, row, 1, 2.0, ew, i, wt, i, bw, i)
    lane = lax.broadcasted_iota(jnp.int32, (4, 128), 1)
    for m in range(groups):
        at = 2 * m + 4
        a = residual_chunk(y1, at, 4, 1, 2.0, ew, at, bw, at)
        b = residual_chunk(y1, at + 1, 4, 1, 2.0, ew, at + 1, bw, at + 1)
        for c in range(5):
            pair[m, c] = a[c] + b[c] if c < 4 else get(ew, (at,), 4) + get(ew, (at + 1,), 4)
    for m in range(groups):
        for c in range(5):
            rows = pair[m, c, pl.ds(0, 4, stride=2), :] + pair[m, c, pl.ds(1, 4, stride=2), :]
            mate = jnp.where(lane % 2 == 0, pltpu.roll(rows, 127, 1), pltpu.roll(rows, 1, 1))
            low[c, m, 0:4, :] = (rows + mate) * (0.5 if c < 4 else 0.125)
    for c in range(5):
        for q in range(groups // 2):
            packed = jnp.where(lane % 2 == 0, low[c, 2 * q, 0:4, :], low[c, 2 * q + 1, 0:4, :])
            at = 4 * (c * (groups // 2) + q)
            for out in (next_o, low_o):
                out[at : at + 4, :] = packed
    base = 20 * (groups // 2)
    up = core == 0
    for c in range(4):
        for j in range(8):
            at, i = base + 3 * (8 * c + j), 4 * chip + 2 + j
            next_o[at : at + 3, :] = pick(up, y1[c, i, 8:11, :], y1[c, i, 5:8, :])
        for j in range(4):
            at, i = base + 96 + 4 * c + j, 4 * chip + 4 + j
            next_o[at : at + 1, :] = pick(up, bw[c, i, 9:10, :], bw[c, i, 6:7, :])
    for j in range(10):
        e_o[j] = ew[2 * g + j]
        w_o[j] = wt[2 * g + j]
        for c in range(4):
            y_o[c, j] = y1[c, 2 * g + j]
            b_o[c, j] = bw[c, 2 * g + j]


def up_all(groups, devs, idx, low, by1, by2, swapped, y_i, b_i, e1, w1, x1, ew, wt, fw, own_edge, far_edge, sol_o, res_o,
           e2, w2, b2, z0, z1, b1, ya, yb, rep, va, vb):
    g, d = idx[0], idx[1]
    core = g % 2
    zero = jnp.zeros((32, 128), F32)
    lane = lax.broadcasted_iota(jnp.int32, (4, 128), 1)
    even = lane % 2 == 0

    for i in (0, 1, groups + 2, groups + 3):
        e2[i] = zero
        for c in range(4):
            z0[c, i] = zero
            z1[c, i] = zero
    for i in range(2, groups + 2):
        e2[i, 0:8, :] = zero[0:8]
        e2[i, 16:32, :] = zero[0:16]
        for c in range(4):
            b2[c, i, 0:8, :] = zero[0:8]
            b2[c, i, 16:32, :] = zero[0:16]
    tall = 20 * (groups // 2)
    by1_rows = tall + 112
    first_core = core == 0

    def from_second(by, offset, at, rows=4):
        a, b = by[at : at + rows, :], swapped[offset + at : offset + at + rows, :]
        return pick(first_core, a, b), pick(first_core, b, a)

    for away in (-2, -1, 0, 1, 2):
        row = 10 + 4 * away
        there = 1.0 if away == 0 else jnp.where((d + away >= 0) & (d + away < devs), 1.0, 0.0)
        for c in range(5):
            for q in range(groups // 2):
                at = 4 * (c * (groups // 2) + q)
                if away == 0:
                    packed = low[at : at + 4, :]
                else:
                    by, offset = (by1, 0) if away in (-1, 1) else (by2, by1_rows)
                    packed = from_second(by, offset, at)[0 if away < 0 else 1]
                first = jnp.where(even, packed, pltpu.roll(packed, 1, 1))
                second = jnp.where(even, pltpu.roll(packed, 127, 1), packed)
                if c == 4:
                    e2[2 * q + 2, row : row + 4, :] = first * there
                    e2[2 * q + 3, row : row + 4, :] = second * there
                else:
                    b2[c, 2 * q + 2, row : row + 4, :] = first
                    b2[c, 2 * q + 3, row : row + 4, :] = second
    for i in range(2, groups + 2):
        for row in (0, 8, 16):
            inside = rows_inside(row, 4 * d - 10, 4 * devs, 128)
            start_chunk(z0, i, row, 2, 4.0, e2, i, w2, i, b2, i, inside)
    here, other = z0, z1
    for k in range(COARSE - 1):
        for i in range(2, groups + 2):
            for row in (4, 12) if k < COARSE - 2 else (8,):
                sweep_chunk(other, here, i, row, 2, 4.0, e2, i, w2, i, b2, i)
        here, other = other, here
    z = here

    low_y, high_y = jnp.where(d > 0, 1.0, 0.0), jnp.where(d < devs - 1, 1.0, 0.0)

    def mid_halo(at, rows):
        a, b = from_second(by1, 0, at, rows), from_second(by1, 0, at + 2 * rows, rows)
        return pick(first_core, a[0], b[0]), pick(first_core, a[1], b[1])

    for c in range(4):
        for k in range(5):
            rows = z[c, g + k, 8:16, :]
            rep[c, k, pl.ds(0, 8, stride=2), :] = rows
            rep[c, k, pl.ds(1, 8, stride=2), :] = rows
    for c in range(4):
        for j in range(10):
            b1[c, j] = b_i[c, j]
            ya[c, j] = y_i[c, j]
        for j in range(2):
            before, after = mid_halo(tall + 96 + 4 * c + j, 1)
            b1[c, 4 + j, 1:2, :] = before
            b1[c, 4 + j, 14:15, :] = after
        for j in range(6):
            before, after = mid_halo(tall + 3 * (8 * c + j), 3)
            ya[c, 2 + j, 0:3, :] = before * low_y
            ya[c, 2 + j, 13:16, :] = after * high_y
        for j in range(10):
            ya[c, j] = ya[c, j] + rep[c, j // 2]
    for at in range(1, 9):
        for row in (0, 8) if 1 < at < 8 else (4,):
            sweep_chunk(yb, ya, at, row, 1, 2.0, e1, at, w1, at, b1, at)
    for at in range(2, 8):
        for row in (0, 8) if 2 < at < 7 else (4,):
            sweep_chunk(ya, yb, at, row, 1, 2.0, e1, at, w1, at, b1, at)

    low_x, high_x = jnp.where(g > 0, 1.0, 0.0), jnp.where(g < groups - 1, 1.0, 0.0)
    for c in range(4):
        for m in range(6):
            for k in range(2):
                both = spread(ya[c, 2 + m, 8 * k : 8 * k + 8, :])
                rows = slice(16 * k, 16 * k + 16)
                for layer in (2 * m, 2 * m + 1):
                    for n in range(2):
                        if 3 <= layer <= 8:
                            va[c, layer, n, rows, :] = both[n] + x1[c, layer - 2, n, rows, :]
                        elif 1 <= layer <= 10:
                            va[c, layer, n, rows, :] = both[n]
        for j in range(2):
            at = 64 + 18 * (2 * c + j)
            own, far = own_edge[at : at + 18, :], far_edge[at : at + 18, :]
            before = jnp.where(core == 0, far, own) * low_x
            after = jnp.where(core == 0, own, far) * high_x
            put(va, (c, 1 + j), 7, get(va, (c, 1 + j), 7, 18) + before)
            put(va, (c, 9 + j), 7, get(va, (c, 9 + j), 7, 18) + after)
    for at in range(2, 10):
        for row in (4, 12, 20) if 2 < at < 9 else (8, 16):
            sweep_chunk(vb, va, at, row, 1, 1.0, ew, at - 1, wt, at - 2, fw, at - 2)
    for at in range(3, 9):
        for row in (4, 12, 20) if 3 < at < 8 else (8, 16):
            sweep_chunk(va, vb, at, row, 1, 1.0, ew, at - 1, wt, at - 2, fw, at - 2)
    for i in range(4):
        for row in (8, 16):
            out = residual_chunk(va, i + 4, row, 1, 1.0, ew, i + 3, fw, i + 2)
            for c in range(4):
                sol_o[c, i, row - 8 : row, :] = get(va, (c, i + 4), row)
                res_o[c, i, row - 8 : row, :] = 0.5 * out[c]


def call(kernel, outs, scratch, *args):
    specs = [pl.BlockSpec(memory_space=pltpu.SMEM)] + [pl.BlockSpec(memory_space=pltpu.VMEM)] * (len(args) - 1)
    return pl.pallas_call(
        kernel,
        out_shape=[jax.ShapeDtypeStruct(shape, F32) for shape in outs],
        in_specs=specs,
        out_specs=[pl.BlockSpec(memory_space=pltpu.VMEM)] * len(outs),
        scratch_shapes=[pltpu.VMEM(shape, F32) for shape in scratch],
        compiler_params=pltpu.CompilerParams(vmem_limit_bytes=VMEM_LIMIT),
    )(*args)


def local(forcing, viscosity):
    groups, devs = lax.axis_size("grp"), lax.axis_size("dev")
    idx = jnp.stack([lax.axis_index("grp"), lax.axis_index("dev")]).astype(jnp.int32)
    swap = [(i, i ^ 1) for i in range(groups)]
    beside = [(i, (i + 1) % groups if i % 2 else (i - 1) % groups) for i in range(groups)]
    next_chip = [(i, (i - 2) % groups if i % 2 else (i + 2) % groups) for i in range(groups)]
    far_chip = [(i, (i + 4) % groups) for i in range(groups)]
    even = [(i, i ^ 1) for i in range(devs)]

    def pairs_of(to):
        every = [(g, d) for g in range(groups) for d in range(devs)]
        return [(g * devs + d, to(g, d)[0] * devs + to(g, d)[1]) for g, d in every]

    cross_pairs = pairs_of(lambda g, d: (beside[g][1], d) if 0 < g < groups - 1 else (g, d ^ 1))
    odd_pairs = pairs_of(lambda g, d: (g, d + 1 if d % 2 else d - 1) if 0 < d < devs - 1 else (g ^ 1, d))

    def along(step):
        def to(g, d):
            there = d - step if g % 2 else d + step
            return (g, there) if 0 <= there < devs else (g ^ 1, d)

        return pairs_of(to)

    f_first, f_last, visc = lax.optimization_barrier((forcing[:, 0:2], forcing[:, 2:4], viscosity))
    first = jnp.concatenate([f_first.reshape(8, 16, 256), visc[0:3]], axis=0)
    last = jnp.concatenate([f_last.reshape(8, 16, 256), visc[1:4]], axis=0)
    cross, inner = pick(idx[0] % 2 == 0, first, last), pick(idx[0] % 2 == 0, last, first)
    cross, inner = lax.optimization_barrier((cross, inner))
    cross, inner = lax.ppermute(cross, ("grp", "dev"), cross_pairs), lax.ppermute(inner, "grp", swap)
    to_even, to_odd = call(pack_second, [(SECOND_ROWS, 256)] * 2, [], idx, forcing, viscosity, cross, inner)
    from_odd, from_even = lax.ppermute(to_odd, ("grp", "dev"), odd_pairs), lax.ppermute(to_even, "dev", even)
    mid, pay, x1, ew, wt, fw = call(
        lambda *refs: fine_down(groups, devs, *refs),
        [(64, 256), (208, 256), (4, 8, 2, 32, 128), (10, 2, 32, 128), (8, 2, 32, 128), (4, 8, 2, 32, 128)],
        [(4, 8, 2, 32, 128), (10, 32, 256), (320, 128)],
        idx, forcing, viscosity, cross, inner, from_odd, from_even,
    )

    xco = lax.ppermute(pay, "grp", beside)
    c2 = lax.ppermute(mid, "grp", far_chip)
    cpm = lax.ppermute(mid, "grp", next_chip)
    partner = lax.ppermute(pay, "grp", swap)
    s3 = lax.ppermute(jnp.concatenate([xco[:64], cpm, c2], axis=0), "grp", swap)

    layers = 2 * groups + 8
    tall = 20 * (groups // 2)
    to_next, low, y_w, b_w, e_w, w_w = call(
        lambda *refs: mid_down(groups, devs, *refs),
        [(tall + 112, 128), (tall, 128), (4, 10, 16, 128), (4, 10, 16, 128), (10, 16, 128), (10, 16, 128)],
        [(4, layers, 16, 128), (layers, 16, 128), (layers, 16, 128), (4, layers, 16, 128), (4, layers, 16, 128),
         (groups, 5, 8, 128), (5, groups, 8, 128)],
        idx, mid, partner, xco, cpm, c2, s3,
    )

    by1 = lax.ppermute(to_next, ("grp", "dev"), along(1))
    by2 = lax.ppermute(low, ("grp", "dev"), along(2))
    swapped = lax.ppermute(jnp.concatenate([by1, by2], axis=0), "grp", swap)
    deep = groups + 4
    return tuple(call(
        lambda *refs: up_all(groups, devs, *refs),
        [(4, 4, 16, 256), (4, 4, 16, 256)],
        [(deep, 32, 128), (deep, 32, 128), (4, deep, 32, 128), (4, deep, 32, 128), (4, deep, 32, 128),
         (4, 10, 16, 128), (4, 10, 16, 128), (4, 10, 16, 128), (4, 5, 16, 128),
         (4, 12, 2, 32, 128), (4, 12, 2, 32, 128)],
        idx, low, by1, by2, swapped, y_w, b_w, e_w, w_w, x1, ew, wt, fw, partner, xco,
    ))


def solution(mesh):
    in_specs = (P(None, "grp", "dev", None), P("grp", "dev", None))
    out_specs = (P(None, "grp", "dev", None), P(None, "grp", "dev", None))
    return jax.shard_map(local, mesh=mesh, in_specs=in_specs, out_specs=out_specs, check_vma=False)
```

```python
import jax
import jax.numpy as jnp
from jax import lax
from jax.experimental import pallas as pl
from jax.experimental.pallas import tpu as pltpu
from jax.sharding import PartitionSpec as P

COARSE = 6
OMEGA = 0.6
BETA = 0.25
F32 = jnp.float32
VMEM_LIMIT = 48 * 1024 * 1024


def shifts(value, step):
    rows, lanes = value.shape
    lane = lax.broadcasted_iota(jnp.int32, (rows, 128), 1)
    if lanes == 256:
        low, high = value[:, :128], value[:, 128:]
        low_up, high_up = pltpu.roll(low, 127, 1), pltpu.roll(high, 127, 1)
        low_dn, high_dn = pltpu.roll(low, 1, 1), pltpu.roll(high, 1, 1)
        last, first = lane == 127, lane == 0
        plus = jnp.concatenate([jnp.where(last, high_up, low_up), jnp.where(last, 0.0, high_up)], 1)
        minus = jnp.concatenate([jnp.where(first, 0.0, low_dn), jnp.where(first, low_dn, high_dn)], 1)
        return plus, minus
    plus = jnp.where(lane >= 128 - step, 0.0, pltpu.roll(value, 128 - step, 1))
    minus = jnp.where(lane < step, 0.0, pltpu.roll(value, step, 1))
    return plus, minus


def get(ref, lead, row, count=8):
    if len(ref.shape) == len(lead) + 3:
        return jnp.concatenate([ref[(*lead, n, pl.ds(row, count))] for n in range(2)], 1)
    return ref[(*lead, pl.ds(row, count))]


def put(ref, lead, row, value):
    rows = pl.ds(row, value.shape[0])
    if len(ref.shape) == len(lead) + 3:
        for n in range(2):
            ref[(*lead, n, rows)] = value[:, 128 * n : 128 * n + 128]
    else:
        ref[(*lead, rows)] = value


def around(ref, lead, layer, row, step):
    rows = ref.shape[-2]
    here = get(ref, (*lead, layer), row)
    near = [get(ref, (*lead, layer + 1), row), get(ref, (*lead, layer - 1), row)]
    near.append(get(ref, (*lead, layer), row + 1) if row + 9 <= rows else pltpu.roll(here, 7, 0))
    near.append(get(ref, (*lead, layer), row - 1) if row >= 1 else pltpu.roll(here, 1, 0))
    return here, [*near, *shifts(here, step)]


def sums_of(visc, layer, row, step):
    here, near = around(visc, (), layer, row, step)
    sums = [here + other for other in near]
    return here, sums, sum(sums[1:], sums[0])


def stencil(field, layer, row, step, sums):
    here, flux, grad, div = [], [], None, None
    for comp in range(4):
        centre, near = around(field, (comp,), layer, row, step)
        here.append(centre)
        if comp < 3:
            terms = [s * n for s, n in zip(sums, near)]
            flux.append(sum(terms[1:], terms[0]))
            diff = near[2 * comp] - near[2 * comp + 1]
            div = diff if div is None else div + diff
        else:
            grad = [near[2 * c] - near[2 * c + 1] for c in range(3)]
    return here, flux, grad, div


def times(spacing, value):
    return value if spacing == 1.0 else spacing * value


def sweep_chunk(out, field, layer, row, step, spacing, visc, visc_layer, weight, weight_layer, source, source_layer):
    e_here, sums, _ = sums_of(visc, visc_layer, row, step)
    here, flux, grad, div = stencil(field, layer, row, step, sums)
    w = get(weight, (weight_layer,), row)
    for c in range(3):
        b = get(source, (c, source_layer), row)
        value = (1.0 - OMEGA) * here[c] + w * (b + flux[c] - times(spacing, grad[c]))
        put(out, (c, layer), row, value)
    b = get(source, (3, source_layer), row)
    put(out, (3, layer), row, here[3] + (BETA * 0.5 / (spacing * spacing) * e_here) * (b - times(spacing, div)))


def residual_chunk(field, layer, row, step, spacing, visc, visc_layer, source, source_layer):
    _, sums, total = sums_of(visc, visc_layer, row, step)
    here, flux, grad, div = stencil(field, layer, row, step, sums)
    out = []
    for c in range(3):
        b = get(source, (c, source_layer), row)
        out.append(b - (total * here[c] - flux[c] + times(spacing, grad[c])))
    out.append(get(source, (3, source_layer), row) - times(spacing, div))
    return out


def start_chunk(out, layer, row, step, spacing, visc, visc_layer, weight, weight_layer, source, source_layer, inside):
    e_here, _, total = sums_of(visc, visc_layer, row, step)
    w = jnp.where(inside, OMEGA / total, 0.0)
    put(weight, (weight_layer,), row, w)
    for c in range(4):
        scale = w if c < 3 else BETA * 0.5 / (spacing * spacing) * e_here
        put(out, (c, layer), row, scale * get(source, (c, source_layer), row))


def rows_inside(row, first, count, lanes):
    at = lax.broadcasted_iota(jnp.int32, (8, lanes), 0) + (row + first)
    return (at >= 0) & (at < count)


def take(value, at, axis):
    return jnp.take_along_axis(value, at, axis=axis)


def fold(value):
    a = lax.broadcasted_iota(jnp.int32, (256, 128), 0)
    b = lax.broadcasted_iota(jnp.int32, (256, 128), 1)
    pairs = jnp.where(a // 2 == b, 1.0, 0.0).astype(jnp.bfloat16)
    total = None
    for _ in range(3):
        part = value.astype(jnp.bfloat16)
        term = jnp.dot(part, pairs, preferred_element_type=F32)
        total = term if total is None else total + term
        value = value - part.astype(F32)
    return total


def spread(value):
    lane = lax.broadcasted_iota(jnp.int32, (8, 128), 1)
    row = lax.broadcasted_iota(jnp.int32, (8, 128), 0)
    out = []
    for n in range(2):
        wide = take(value, lane // 2 + 64 * n, 1)
        out.append(jnp.concatenate([take(wide, row // 2 + 4 * m, 0) for m in range(2)], 0))
    return out


def pick(condition, a, b):
    return jnp.where(condition, a, b)


def halo_first(idx, cross, inner, n):
    even = idx[0] % 2 == 0
    a, b = cross[n], inner[n]
    return pick(even, a, b), pick(even, b, a)


F_ROWS = (4, 5, 6, 6, 6, 6, 5, 4)
E_ROWS = (4, 5, 6, 8, 8, 8, 8, 6, 5, 4)
F_AT = tuple(4 * sum(F_ROWS[:n]) for n in range(9))
E_AT = tuple(F_AT[8] + sum(E_ROWS[:n]) for n in range(11))
SECOND_ROWS = 232


def pack_second(idx, f, e, cross, inner, even_o, odd_o):
    even = (idx[0] + idx[1]) % 2 == 0

    def write(at, rows, value):
        size = value.shape[0]
        low, high = value[0:rows, :], value[size - rows : size, :]
        even_o[at : at + rows, :] = pick(even, high, low)
        odd_o[at : at + rows, :] = pick(even, low, high)

    for layer in range(10):
        if 3 <= layer <= 6:
            value = e[layer - 3]
        else:
            value = halo_first(idx, cross, inner, 8 + layer)[0] if layer < 3 else halo_first(idx, cross, inner, 1 + layer)[1]
        write(E_AT[layer], E_ROWS[layer], value)
    for layer in range(8):
        for c in range(4):
            if 2 <= layer <= 5:
                value = f[c, layer - 2]
            elif layer < 2:
                value = halo_first(idx, cross, inner, 2 * c + layer)[0]
            else:
                value = halo_first(idx, cross, inner, 2 * c + layer - 6)[1]
            write(F_AT[layer] + F_ROWS[layer] * c, F_ROWS[layer], value)
    even_o[E_AT[10] : SECOND_ROWS, :] = jnp.zeros((SECOND_ROWS - E_AT[10], 256), F32)
    odd_o[E_AT[10] : SECOND_ROWS, :] = jnp.zeros((SECOND_ROWS - E_AT[10], 256), F32)


def fine_down(groups, devs, idx, f, e, cross, inner, odd, even, mid_o, pay_o, x1, ew, wt, fw, x0, pair, half):
    g, d = idx[0], idx[1]
    low_x, high_x = jnp.where(g > 0, 1.0, 0.0), jnp.where(g < groups - 1, 1.0, 0.0)
    low_y, high_y = jnp.where(d > 0, 1.0, 0.0), jnp.where(d < devs - 1, 1.0, 0.0)
    even_dev = (g + d) % 2 == 0

    def halo_second(at):
        a, b = odd[at, :], even[at, :]
        return pick(even_dev, a, b), pick(even_dev, b, a)

    for layer in range(10):
        if layer < 3:
            own = halo_first(idx, cross, inner, 8 + layer)[0]
        else:
            own = halo_first(idx, cross, inner, 1 + layer)[1] if layer > 6 else e[layer - 3]
        s = low_x if layer < 3 else high_x if layer > 6 else 1.0
        rows = E_ROWS[layer]
        before, after = halo_second(slice(E_AT[layer], E_AT[layer] + rows))
        before, after = before * (s * low_y), after * (s * high_y)
        if rows < 8:
            ones = jnp.ones((8 - rows, 256), F32)
            before, after = jnp.concatenate([ones, before], 0), jnp.concatenate([after, ones], 0)
        put(ew, (layer,), 0, before)
        put(ew, (layer,), 8, own * s)
        put(ew, (layer,), 24, after)
    for layer in range(8):
        for c in range(4):
            if layer < 2:
                own = halo_first(idx, cross, inner, 2 * c + layer)[0]
            else:
                own = halo_first(idx, cross, inner, 2 * c + layer - 6)[1] if layer > 5 else f[c, layer - 2]
            at = F_AT[layer] + F_ROWS[layer] * c
            before, after = halo_second(slice(at, at + F_ROWS[layer]))
            zero = jnp.zeros((8 - F_ROWS[layer], 256), F32)
            put(fw, (c, layer), 0, jnp.concatenate([zero, 2.0 * before], 0))
            put(fw, (c, layer), 8, 2.0 * own)
            put(fw, (c, layer), 24, jnp.concatenate([2.0 * after, zero], 0))
    for layer in range(8):
        layer_in = (4 * g - 2 + layer >= 0) & (4 * g - 2 + layer < 4 * groups)
        for row in (0, 8, 16, 24) if 0 < layer < 7 else (4, 12, 20):
            inside = rows_inside(row, 16 * d - 8, 16 * devs, 256) & layer_in
            start_chunk(x0, layer, row, 1, 1.0, ew, layer + 1, wt, layer, fw, layer, inside)
    for layer in range(1, 7):
        for row in (0, 8, 16, 24) if 1 < layer < 6 else (4, 12, 20):
            sweep_chunk(x1, x0, layer, row, 1, 1.0, ew, layer + 1, wt, layer, fw, layer)
    for m in range(2):
        for row in (4, 12, 20):
            a = residual_chunk(x1, 2 * m + 2, row, 1, 1.0, ew, 2 * m + 3, fw, 2 * m + 2)
            b = residual_chunk(x1, 2 * m + 3, row, 1, 1.0, ew, 2 * m + 4, fw, 2 * m + 3)
            for c in range(4):
                pair[2 * c + m, row : row + 8, :] = a[c] + b[c]
        for c in range(4):
            pair[2 * c + m, 0:4, :] = jnp.zeros((4, 256), F32)
            pair[2 * c + m, 28:32, :] = jnp.zeros((4, 256), F32)
        pair[8 + m] = get(ew, (2 * m + 3,), 0, 32) + get(ew, (2 * m + 4,), 0, 32)
    half[...] = fold(pair[...].reshape(320, 256))
    coarse = half[pl.ds(0, 160, stride=2), :] + half[pl.ds(1, 160, stride=2), :]
    coarse = coarse.reshape(10, 16, 128)
    for m in range(2):
        lanes = slice(128 * m, 128 * m + 128)
        for c in range(4):
            mid_o[12 * c : 12 * c + 12, lanes] = pay_o[12 * c : 12 * c + 12, lanes] = coarse[2 * c + m, 2:14, :] * 0.5
        mid_o[48:64, lanes] = pay_o[48:64, lanes] = coarse[8 + m] * 0.125
    for c in range(4):
        for j in range(2):
            at = 64 + 18 * (2 * c + j)
            pay_o[at : at + 18, :] = get(x1, (c, 3 + j), 7, 18)


def mid_down(groups, devs, idx, own, partner, xco, cpm, c2, s3, next_o, low_o, y_o, b_o, e_o, w_o, bw, ew, wt, y0, y1, pair, low):
    g, d = idx[0], idx[1]
    chips = groups // 2
    chip, core = g // 2, g % 2
    other = 1 - core
    beside = (chip + chips - 1 + 2 * core) % chips
    across = (chip + 1 + (chips - 2) * core) % chips
    far = (chip + 2) % chips
    layers = 2 * groups
    zero = jnp.zeros((16, 128), F32)
    for i in (0, 1, 2, 3, layers + 4, layers + 5, layers + 6, layers + 7):
        ew[i] = zero
        wt[i] = zero
        for c in range(4):
            bw[c, i] = zero
            y0[c, i] = zero
            y1[c, i] = zero
    for i in range(layers):
        for c in range(4):
            bw[c, i + 4, 0:2, :] = zero[0:2]
            bw[c, i + 4, 14:16, :] = zero[0:2]

    def place(block, at, which, core_at):
        base = 4 + 4 * which + 2 * core_at
        for m in range(2):
            lanes = slice(128 * m, 128 * m + 128)
            for c in range(4):
                bw[c, base + m, 2:14, :] = block[at + 12 * c : at + 12 * c + 12, lanes]
            ew[base + m] = block[at + 48 : at + 64, lanes]

    place(own, 0, chip, core)
    place(partner, 0, chip, other)
    place(xco, 0, beside, other)
    place(cpm, 0, beside, core)
    place(s3, 0, across, core)
    place(s3, 64, across, other)
    place(c2, 0, far, core)
    place(s3, 128, far, other)
    for i in range(4, layers + 4):
        for row in (0, 8):
            inside = rows_inside(row, 8 * d - 4, 8 * devs, 128)
            start_chunk(y0, i, row, 1, 2.0, ew, i, wt, i, bw, i, inside)
    for i in range(4, layers + 4):
        for row in (0, 8):
            sweep_chunk(y1, y0, i, row, 1, 2.0, ew, i, wt, i, bw, i)
    lane = lax.broadcasted_iota(jnp.int32, (4, 128), 1)
    for m in range(groups):
        at = 2 * m + 4
        a = residual_chunk(y1, at, 4, 1, 2.0, ew, at, bw, at)
        b = residual_chunk(y1, at + 1, 4, 1, 2.0, ew, at + 1, bw, at + 1)
        for c in range(5):
            pair[m, c] = a[c] + b[c] if c < 4 else get(ew, (at,), 4) + get(ew, (at + 1,), 4)
    for m in range(groups):
        for c in range(5):
            rows = pair[m, c, pl.ds(0, 4, stride=2), :] + pair[m, c, pl.ds(1, 4, stride=2), :]
            mate = jnp.where(lane % 2 == 0, pltpu.roll(rows, 127, 1), pltpu.roll(rows, 1, 1))
            low[c, m, 0:4, :] = (rows + mate) * (0.5 if c < 4 else 0.125)
    for c in range(5):
        for q in range(groups // 2):
            packed = jnp.where(lane % 2 == 0, low[c, 2 * q, 0:4, :], low[c, 2 * q + 1, 0:4, :])
            at = 4 * (c * (groups // 2) + q)
            for out in (next_o, low_o):
                out[at : at + 4, :] = packed
    base = 20 * (groups // 2)
    up = core == 0
    for c in range(4):
        for j in range(8):
            at, i = base + 3 * (8 * c + j), 4 * chip + 2 + j
            next_o[at : at + 3, :] = pick(up, y1[c, i, 8:11, :], y1[c, i, 5:8, :])
        for j in range(4):
            at, i = base + 96 + 4 * c + j, 4 * chip + 4 + j
            next_o[at : at + 1, :] = pick(up, bw[c, i, 9:10, :], bw[c, i, 6:7, :])
    for j in range(10):
        e_o[j] = ew[2 * g + j]
        w_o[j] = wt[2 * g + j]
        for c in range(4):
            y_o[c, j] = y1[c, 2 * g + j]
            b_o[c, j] = bw[c, 2 * g + j]


def up_all(groups, devs, idx, low, by1, by2, swapped, y_i, b_i, e1, w1, x1, ew, wt, fw, own_edge, far_edge, sol_o, res_o,
           e2, w2, b2, z0, z1, b1, ya, yb, rep, va, vb):
    g, d = idx[0], idx[1]
    core = g % 2
    zero = jnp.zeros((32, 128), F32)
    lane = lax.broadcasted_iota(jnp.int32, (4, 128), 1)
    even = lane % 2 == 0

    for i in (0, 1, groups + 2, groups + 3):
        e2[i] = zero
        for c in range(4):
            z0[c, i] = zero
            z1[c, i] = zero
    for i in range(2, groups + 2):
        e2[i, 0:8, :] = zero[0:8]
        e2[i, 16:32, :] = zero[0:16]
        for c in range(4):
            b2[c, i, 0:8, :] = zero[0:8]
            b2[c, i, 16:32, :] = zero[0:16]
    tall = 20 * (groups // 2)
    by1_rows = tall + 112
    first_core = core == 0

    def from_second(by, offset, at, rows=4):
        a, b = by[at : at + rows, :], swapped[offset + at : offset + at + rows, :]
        return pick(first_core, a, b), pick(first_core, b, a)

    for away in (-2, -1, 0, 1, 2):
        row = 10 + 4 * away
        there = 1.0 if away == 0 else jnp.where((d + away >= 0) & (d + away < devs), 1.0, 0.0)
        for c in range(5):
            for q in range(groups // 2):
                at = 4 * (c * (groups // 2) + q)
                if away == 0:
                    packed = low[at : at + 4, :]
                else:
                    by, offset = (by1, 0) if away in (-1, 1) else (by2, by1_rows)
                    packed = from_second(by, offset, at)[0 if away < 0 else 1]
                first = jnp.where(even, packed, pltpu.roll(packed, 1, 1))
                second = jnp.where(even, pltpu.roll(packed, 127, 1), packed)
                if c == 4:
                    e2[2 * q + 2, row : row + 4, :] = first * there
                    e2[2 * q + 3, row : row + 4, :] = second * there
                else:
                    b2[c, 2 * q + 2, row : row + 4, :] = first
                    b2[c, 2 * q + 3, row : row + 4, :] = second
    for i in range(2, groups + 2):
        for row in (0, 8, 16):
            inside = rows_inside(row, 4 * d - 10, 4 * devs, 128)
            start_chunk(z0, i, row, 2, 4.0, e2, i, w2, i, b2, i, inside)
    here, other = z0, z1
    for k in range(COARSE - 1):
        for i in range(2, groups + 2):
            for row in (4, 12) if k < COARSE - 2 else (8,):
                sweep_chunk(other, here, i, row, 2, 4.0, e2, i, w2, i, b2, i)
        here, other = other, here
    z = here

    low_y, high_y = jnp.where(d > 0, 1.0, 0.0), jnp.where(d < devs - 1, 1.0, 0.0)

    def mid_halo(at, rows):
        a, b = from_second(by1, 0, at, rows), from_second(by1, 0, at + 2 * rows, rows)
        return pick(first_core, a[0], b[0]), pick(first_core, a[1], b[1])

    for c in range(4):
        for k in range(5):
            rows = z[c, g + k, 8:16, :]
            rep[c, k, pl.ds(0, 8, stride=2), :] = rows
            rep[c, k, pl.ds(1, 8, stride=2), :] = rows
    for c in range(4):
        for j in range(10):
            b1[c, j] = b_i[c, j]
            ya[c, j] = y_i[c, j]
        for j in range(2):
            before, after = mid_halo(tall + 96 + 4 * c + j, 1)
            b1[c, 4 + j, 1:2, :] = before
            b1[c, 4 + j, 14:15, :] = after
        for j in range(6):
            before, after = mid_halo(tall + 3 * (8 * c + j), 3)
            ya[c, 2 + j, 0:3, :] = before * low_y
            ya[c, 2 + j, 13:16, :] = after * high_y
        for j in range(10):
            ya[c, j] = ya[c, j] + rep[c, j // 2]
    for at in range(1, 9):
        for row in (0, 8) if 1 < at < 8 else (4,):
            sweep_chunk(yb, ya, at, row, 1, 2.0, e1, at, w1, at, b1, at)
    for at in range(2, 8):
        for row in (0, 8) if 2 < at < 7 else (4,):
            sweep_chunk(ya, yb, at, row, 1, 2.0, e1, at, w1, at, b1, at)

    low_x, high_x = jnp.where(g > 0, 1.0, 0.0), jnp.where(g < groups - 1, 1.0, 0.0)
    for c in range(4):
        for m in range(6):
            for k in range(2):
                both = spread(ya[c, 2 + m, 8 * k : 8 * k + 8, :])
                rows = slice(16 * k, 16 * k + 16)
                for layer in (2 * m, 2 * m + 1):
                    for n in range(2):
                        if 3 <= layer <= 8:
                            va[c, layer, n, rows, :] = both[n] + x1[c, layer - 2, n, rows, :]
                        elif 1 <= layer <= 10:
                            va[c, layer, n, rows, :] = both[n]
        for j in range(2):
            at = 64 + 18 * (2 * c + j)
            own, far = own_edge[at : at + 18, :], far_edge[at : at + 18, :]
            before = jnp.where(core == 0, far, own) * low_x
            after = jnp.where(core == 0, own, far) * high_x
            put(va, (c, 1 + j), 7, get(va, (c, 1 + j), 7, 18) + before)
            put(va, (c, 9 + j), 7, get(va, (c, 9 + j), 7, 18) + after)
    for at in range(2, 10):
        for row in (4, 12, 20) if 2 < at < 9 else (8, 16):
            sweep_chunk(vb, va, at, row, 1, 1.0, ew, at - 1, wt, at - 2, fw, at - 2)
    for at in range(3, 9):
        for row in (4, 12, 20) if 3 < at < 8 else (8, 16):
            sweep_chunk(va, vb, at, row, 1, 1.0, ew, at - 1, wt, at - 2, fw, at - 2)
    for i in range(4):
        for row in (8, 16):
            out = residual_chunk(va, i + 4, row, 1, 1.0, ew, i + 3, fw, i + 2)
            for c in range(4):
                sol_o[c, i, row - 8 : row, :] = get(va, (c, i + 4), row)
                res_o[c, i, row - 8 : row, :] = 0.5 * out[c]


def call(kernel, outs, scratch, *args):
    specs = [pl.BlockSpec(memory_space=pltpu.SMEM)] + [pl.BlockSpec(memory_space=pltpu.VMEM)] * (len(args) - 1)
    return pl.pallas_call(
        kernel,
        out_shape=[jax.ShapeDtypeStruct(shape, F32) for shape in outs],
        in_specs=specs,
        out_specs=[pl.BlockSpec(memory_space=pltpu.VMEM)] * len(outs),
        scratch_shapes=[pltpu.VMEM(shape, F32) for shape in scratch],
        compiler_params=pltpu.CompilerParams(vmem_limit_bytes=VMEM_LIMIT),
    )(*args)


def local(forcing, viscosity):
    groups, devs = lax.axis_size("grp"), lax.axis_size("dev")
    idx = jnp.stack([lax.axis_index("grp"), lax.axis_index("dev")]).astype(jnp.int32)
    swap = [(i, i ^ 1) for i in range(groups)]
    beside = [(i, (i + 1) % groups if i % 2 else (i - 1) % groups) for i in range(groups)]
    next_chip = [(i, (i - 2) % groups if i % 2 else (i + 2) % groups) for i in range(groups)]
    far_chip = [(i, (i + 4) % groups) for i in range(groups)]

    def pairs_of(to):
        every = [(g, d) for g in range(groups) for d in range(devs)]
        return [(g * devs + d, to(g, d)[0] * devs + to(g, d)[1]) for g, d in every]

    cross_pairs = pairs_of(lambda g, d: (beside[g][1], d) if 0 < g < groups - 1 else (g, d ^ 1))

    def second(first_core):
        odd = lambda g, d: (g, d + 1 if d % 2 else d - 1) if 0 < d < devs - 1 else (g ^ 2, d)
        return pairs_of(lambda g, d: odd(g, d) if g % 2 == first_core else (g, d ^ 1))

    def along(step):
        def to(g, d):
            there = d - step if g % 2 else d + step
            return (g, there) if 0 <= there < devs else (g ^ 1, d)

        return pairs_of(to)

    f_first, f_last, visc = lax.optimization_barrier((forcing[:, 0:2], forcing[:, 2:4], viscosity))
    first = jnp.concatenate([f_first.reshape(8, 16, 256), visc[0:3]], axis=0)
    last = jnp.concatenate([f_last.reshape(8, 16, 256), visc[1:4]], axis=0)
    cross, inner = pick(idx[0] % 2 == 0, first, last), pick(idx[0] % 2 == 0, last, first)
    cross, inner = lax.optimization_barrier((cross, inner))
    cross, inner = lax.ppermute(cross, ("grp", "dev"), cross_pairs), lax.ppermute(inner, "grp", swap)
    to_even, to_odd = call(pack_second, [(SECOND_ROWS, 256)] * 2, [], idx, forcing, viscosity, cross, inner)
    from_odd, from_even = lax.ppermute(to_odd, ("grp", "dev"), second(0)), lax.ppermute(to_even, ("grp", "dev"), second(1))
    mid, pay, x1, ew, wt, fw = call(
        lambda *refs: fine_down(groups, devs, *refs),
        [(64, 256), (208, 256), (4, 8, 2, 32, 128), (10, 2, 32, 128), (8, 2, 32, 128), (4, 8, 2, 32, 128)],
        [(4, 8, 2, 32, 128), (10, 32, 256), (320, 128)],
        idx, forcing, viscosity, cross, inner, from_odd, from_even,
    )

    xco = lax.ppermute(pay, "grp", beside)
    c2 = lax.ppermute(mid, "grp", far_chip)
    cpm = lax.ppermute(mid, "grp", next_chip)
    partner = lax.ppermute(pay, "grp", swap)
    s3 = lax.ppermute(jnp.concatenate([xco[:64], cpm, c2], axis=0), "grp", swap)

    layers = 2 * groups + 8
    tall = 20 * (groups // 2)
    to_next, low, y_w, b_w, e_w, w_w = call(
        lambda *refs: mid_down(groups, devs, *refs),
        [(tall + 112, 128), (tall, 128), (4, 10, 16, 128), (4, 10, 16, 128), (10, 16, 128), (10, 16, 128)],
        [(4, layers, 16, 128), (layers, 16, 128), (layers, 16, 128), (4, layers, 16, 128), (4, layers, 16, 128),
         (groups, 5, 8, 128), (5, groups, 8, 128)],
        idx, mid, partner, xco, cpm, c2, s3,
    )

    by1 = lax.ppermute(to_next, ("grp", "dev"), along(1))
    by2 = lax.ppermute(low, ("grp", "dev"), along(2))
    swapped = lax.ppermute(jnp.concatenate([by1, by2], axis=0), "grp", swap)
    deep = groups + 4
    return tuple(call(
        lambda *refs: up_all(groups, devs, *refs),
        [(4, 4, 16, 256), (4, 4, 16, 256)],
        [(deep, 32, 128), (deep, 32, 128), (4, deep, 32, 128), (4, deep, 32, 128), (4, deep, 32, 128),
         (4, 10, 16, 128), (4, 10, 16, 128), (4, 10, 16, 128), (4, 5, 16, 128),
         (4, 12, 2, 32, 128), (4, 12, 2, 32, 128)],
        idx, low, by1, by2, swapped, y_w, b_w, e_w, w_w, x1, ew, wt, fw, partner, xco,
    ))


def solution(mesh):
    in_specs = (P(None, "grp", "dev", None), P("grp", "dev", None))
    out_specs = (P(None, "grp", "dev", None), P(None, "grp", "dev", None))
    return jax.shard_map(local, mesh=mesh, in_specs=in_specs, out_specs=out_specs, check_vma=False)
```

```python
import jax
import jax.numpy as jnp
from jax import lax
from jax.experimental import pallas as pl
from jax.experimental.pallas import tpu as pltpu
from jax.sharding import PartitionSpec as P

COARSE = 6
OMEGA = 0.6
BETA = 0.25
F32 = jnp.float32
VMEM_LIMIT = 48 * 1024 * 1024


def shifts(value, step):
    rows, lanes = value.shape
    lane = lax.broadcasted_iota(jnp.int32, (rows, 128), 1)
    if lanes == 256:
        low, high = value[:, :128], value[:, 128:]
        low_up, high_up = pltpu.roll(low, 127, 1), pltpu.roll(high, 127, 1)
        low_dn, high_dn = pltpu.roll(low, 1, 1), pltpu.roll(high, 1, 1)
        last, first = lane == 127, lane == 0
        plus = jnp.concatenate([jnp.where(last, high_up, low_up), jnp.where(last, 0.0, high_up)], 1)
        minus = jnp.concatenate([jnp.where(first, 0.0, low_dn), jnp.where(first, low_dn, high_dn)], 1)
        return plus, minus
    plus = jnp.where(lane >= 128 - step, 0.0, pltpu.roll(value, 128 - step, 1))
    minus = jnp.where(lane < step, 0.0, pltpu.roll(value, step, 1))
    return plus, minus


def get(ref, lead, row, count=8):
    if len(ref.shape) == len(lead) + 3:
        return jnp.concatenate([ref[(*lead, n, pl.ds(row, count))] for n in range(2)], 1)
    return ref[(*lead, pl.ds(row, count))]


def put(ref, lead, row, value):
    rows = pl.ds(row, value.shape[0])
    if len(ref.shape) == len(lead) + 3:
        for n in range(2):
            ref[(*lead, n, rows)] = value[:, 128 * n : 128 * n + 128]
    else:
        ref[(*lead, rows)] = value


def around(ref, lead, layer, row, step):
    rows = ref.shape[-2]
    here = get(ref, (*lead, layer), row)
    near = [get(ref, (*lead, layer + 1), row), get(ref, (*lead, layer - 1), row)]
    near.append(get(ref, (*lead, layer), row + 1) if row + 9 <= rows else pltpu.roll(here, 7, 0))
    near.append(get(ref, (*lead, layer), row - 1) if row >= 1 else pltpu.roll(here, 1, 0))
    return here, [*near, *shifts(here, step)]


def sums_of(visc, layer, row, step):
    here, near = around(visc, (), layer, row, step)
    sums = [here + other for other in near]
    return here, sums, sum(sums[1:], sums[0])


def stencil(field, layer, row, step, sums):
    here, flux, grad, div = [], [], None, None
    for comp in range(4):
        centre, near = around(field, (comp,), layer, row, step)
        here.append(centre)
        if comp < 3:
            terms = [s * n for s, n in zip(sums, near)]
            flux.append(sum(terms[1:], terms[0]))
            diff = near[2 * comp] - near[2 * comp + 1]
            div = diff if div is None else div + diff
        else:
            grad = [near[2 * c] - near[2 * c + 1] for c in range(3)]
    return here, flux, grad, div


def times(spacing, value):
    return value if spacing == 1.0 else spacing * value


def sweep_chunk(out, field, layer, row, step, spacing, visc, visc_layer, weight, weight_layer, source, source_layer):
    e_here, sums, _ = sums_of(visc, visc_layer, row, step)
    here, flux, grad, div = stencil(field, layer, row, step, sums)
    w = get(weight, (weight_layer,), row)
    for c in range(3):
        b = get(source, (c, source_layer), row)
        value = (1.0 - OMEGA) * here[c] + w * (b + flux[c] - times(spacing, grad[c]))
        put(out, (c, layer), row, value)
    b = get(source, (3, source_layer), row)
    put(out, (3, layer), row, here[3] + (BETA * 0.5 / (spacing * spacing) * e_here) * (b - times(spacing, div)))


def residual_chunk(field, layer, row, step, spacing, visc, visc_layer, source, source_layer):
    _, sums, total = sums_of(visc, visc_layer, row, step)
    here, flux, grad, div = stencil(field, layer, row, step, sums)
    out = []
    for c in range(3):
        b = get(source, (c, source_layer), row)
        out.append(b - (total * here[c] - flux[c] + times(spacing, grad[c])))
    out.append(get(source, (3, source_layer), row) - times(spacing, div))
    return out


def start_chunk(out, layer, row, step, spacing, visc, visc_layer, weight, weight_layer, source, source_layer, inside):
    e_here, _, total = sums_of(visc, visc_layer, row, step)
    w = jnp.where(inside, OMEGA / total, 0.0)
    put(weight, (weight_layer,), row, w)
    for c in range(4):
        scale = w if c < 3 else BETA * 0.5 / (spacing * spacing) * e_here
        put(out, (c, layer), row, scale * get(source, (c, source_layer), row))


def rows_inside(row, first, count, lanes):
    at = lax.broadcasted_iota(jnp.int32, (8, lanes), 0) + (row + first)
    return (at >= 0) & (at < count)


def take(value, at, axis):
    return jnp.take_along_axis(value, at, axis=axis)


def fold(value):
    a = lax.broadcasted_iota(jnp.int32, (256, 128), 0)
    b = lax.broadcasted_iota(jnp.int32, (256, 128), 1)
    pairs = jnp.where(a // 2 == b, 1.0, 0.0).astype(jnp.bfloat16)
    total = None
    for _ in range(3):
        part = value.astype(jnp.bfloat16)
        term = jnp.dot(part, pairs, preferred_element_type=F32)
        total = term if total is None else total + term
        value = value - part.astype(F32)
    return total


def spread(value):
    lane = lax.broadcasted_iota(jnp.int32, (8, 128), 1)
    row = lax.broadcasted_iota(jnp.int32, (8, 128), 0)
    out = []
    for n in range(2):
        wide = take(value, lane // 2 + 64 * n, 1)
        out.append(jnp.concatenate([take(wide, row // 2 + 4 * m, 0) for m in range(2)], 0))
    return out


def pick(condition, a, b):
    return jnp.where(condition, a, b)


def halo_first(idx, cross, inner, n):
    even = idx[0] % 2 == 0
    a, b = cross[n], inner[n]
    return pick(even, a, b), pick(even, b, a)


F_ROWS = (4, 5, 6, 6, 6, 6, 5, 4)
E_ROWS = (4, 5, 6, 8, 8, 8, 8, 6, 5, 4)
F_AT = tuple(4 * sum(F_ROWS[:n]) for n in range(9))
E_AT = tuple(F_AT[8] + sum(E_ROWS[:n]) for n in range(11))
SECOND_ROWS = 232


def pack_second(idx, f, e, cross, inner, even_o, odd_o):
    even = idx[1] % 2 == 0

    def write(at, rows, value):
        size = value.shape[0]
        low, high = value[0:rows, :], value[size - rows : size, :]
        even_o[at : at + rows, :] = pick(even, high, low)
        odd_o[at : at + rows, :] = pick(even, low, high)

    for layer in range(10):
        if 3 <= layer <= 6:
            value = e[layer - 3]
        else:
            value = halo_first(idx, cross, inner, 8 + layer)[0] if layer < 3 else halo_first(idx, cross, inner, 1 + layer)[1]
        write(E_AT[layer], E_ROWS[layer], value)
    for layer in range(8):
        for c in range(4):
            if 2 <= layer <= 5:
                value = f[c, layer - 2]
            elif layer < 2:
                value = halo_first(idx, cross, inner, 2 * c + layer)[0]
            else:
                value = halo_first(idx, cross, inner, 2 * c + layer - 6)[1]
            write(F_AT[layer] + F_ROWS[layer] * c, F_ROWS[layer], value)
    even_o[E_AT[10] : SECOND_ROWS, :] = jnp.zeros((SECOND_ROWS - E_AT[10], 256), F32)
    odd_o[E_AT[10] : SECOND_ROWS, :] = jnp.zeros((SECOND_ROWS - E_AT[10], 256), F32)


def fine_down(groups, devs, idx, f, e, cross, inner, odd, even, mid_o, pay_o, x1, ew, wt, fw, x0, pair, half):
    g, d = idx[0], idx[1]
    low_x, high_x = jnp.where(g > 0, 1.0, 0.0), jnp.where(g < groups - 1, 1.0, 0.0)
    low_y, high_y = jnp.where(d > 0, 1.0, 0.0), jnp.where(d < devs - 1, 1.0, 0.0)
    even_dev = d % 2 == 0

    def halo_second(at):
        a, b = odd[at, :], even[at, :]
        return pick(even_dev, a, b), pick(even_dev, b, a)

    for layer in range(10):
        if layer < 3:
            own = halo_first(idx, cross, inner, 8 + layer)[0]
        else:
            own = halo_first(idx, cross, inner, 1 + layer)[1] if layer > 6 else e[layer - 3]
        s = low_x if layer < 3 else high_x if layer > 6 else 1.0
        rows = E_ROWS[layer]
        before, after = halo_second(slice(E_AT[layer], E_AT[layer] + rows))
        before, after = before * (s * low_y), after * (s * high_y)
        if rows < 8:
            ones = jnp.ones((8 - rows, 256), F32)
            before, after = jnp.concatenate([ones, before], 0), jnp.concatenate([after, ones], 0)
        put(ew, (layer,), 0, before)
        put(ew, (layer,), 8, own * s)
        put(ew, (layer,), 24, after)
    for layer in range(8):
        for c in range(4):
            if layer < 2:
                own = halo_first(idx, cross, inner, 2 * c + layer)[0]
            else:
                own = halo_first(idx, cross, inner, 2 * c + layer - 6)[1] if layer > 5 else f[c, layer - 2]
            at = F_AT[layer] + F_ROWS[layer] * c
            before, after = halo_second(slice(at, at + F_ROWS[layer]))
            zero = jnp.zeros((8 - F_ROWS[layer], 256), F32)
            put(fw, (c, layer), 0, jnp.concatenate([zero, 2.0 * before], 0))
            put(fw, (c, layer), 8, 2.0 * own)
            put(fw, (c, layer), 24, jnp.concatenate([2.0 * after, zero], 0))
    for layer in range(8):
        layer_in = (4 * g - 2 + layer >= 0) & (4 * g - 2 + layer < 4 * groups)
        for row in (0, 8, 16, 24) if 0 < layer < 7 else (4, 12, 20):
            inside = rows_inside(row, 16 * d - 8, 16 * devs, 256) & layer_in
            start_chunk(x0, layer, row, 1, 1.0, ew, layer + 1, wt, layer, fw, layer, inside)
    for layer in range(1, 7):
        for row in (0, 8, 16, 24) if 1 < layer < 6 else (4, 12, 20):
            sweep_chunk(x1, x0, layer, row, 1, 1.0, ew, layer + 1, wt, layer, fw, layer)
    for m in range(2):
        for row in (4, 12, 20):
            a = residual_chunk(x1, 2 * m + 2, row, 1, 1.0, ew, 2 * m + 3, fw, 2 * m + 2)
            b = residual_chunk(x1, 2 * m + 3, row, 1, 1.0, ew, 2 * m + 4, fw, 2 * m + 3)
            for c in range(4):
                pair[2 * c + m, row : row + 8, :] = a[c] + b[c]
        for c in range(4):
            pair[2 * c + m, 0:4, :] = jnp.zeros((4, 256), F32)
            pair[2 * c + m, 28:32, :] = jnp.zeros((4, 256), F32)
        pair[8 + m] = get(ew, (2 * m + 3,), 0, 32) + get(ew, (2 * m + 4,), 0, 32)
    half[...] = fold(pair[...].reshape(320, 256))
    coarse = half[pl.ds(0, 160, stride=2), :] + half[pl.ds(1, 160, stride=2), :]
    coarse = coarse.reshape(10, 16, 128)
    for m in range(2):
        lanes = slice(128 * m, 128 * m + 128)
        for c in range(4):
            mid_o[12 * c : 12 * c + 12, lanes] = pay_o[12 * c : 12 * c + 12, lanes] = coarse[2 * c + m, 2:14, :] * 0.5
        mid_o[48:64, lanes] = pay_o[48:64, lanes] = coarse[8 + m] * 0.125
    for c in range(4):
        for j in range(2):
            at = 64 + 18 * (2 * c + j)
            pay_o[at : at + 18, :] = get(x1, (c, 3 + j), 7, 18)


def mid_down(groups, devs, idx, own, partner, xco, cpm, c2, s1, s3, next_o, low_o, y_o, b_o, e_o, w_o, bw, ew, wt, y0, y1, pair, low):
    g, d = idx[0], idx[1]
    chips = groups // 2
    chip, core = g // 2, g % 2
    other = 1 - core
    beside = (chip + chips - 1 + 2 * core) % chips
    across = (chip + 1 + (chips - 2) * core) % chips
    far = (chip + 2) % chips
    layers = 2 * groups
    zero = jnp.zeros((16, 128), F32)
    for i in (0, 1, 2, 3, layers + 4, layers + 5, layers + 6, layers + 7):
        ew[i] = zero
        wt[i] = zero
        for c in range(4):
            bw[c, i] = zero
            y0[c, i] = zero
            y1[c, i] = zero
    for i in range(layers):
        for c in range(4):
            bw[c, i + 4, 0:2, :] = zero[0:2]
            bw[c, i + 4, 14:16, :] = zero[0:2]

    def place(block, at, which, core_at):
        base = 4 + 4 * which + 2 * core_at
        for m in range(2):
            lanes = slice(128 * m, 128 * m + 128)
            for c in range(4):
                bw[c, base + m, 2:14, :] = block[at + 12 * c : at + 12 * c + 12, lanes]
            ew[base + m] = block[at + 48 : at + 64, lanes]

    place(own, 0, chip, core)
    place(partner, 0, chip, other)
    place(xco, 0, beside, other)
    place(cpm, 0, beside, core)
    place(s1, 0, across, core)
    place(s3, 0, across, other)
    place(c2, 0, far, core)
    place(s3, 64, far, other)
    for i in range(4, layers + 4):
        for row in (0, 8):
            inside = rows_inside(row, 8 * d - 4, 8 * devs, 128)
            start_chunk(y0, i, row, 1, 2.0, ew, i, wt, i, bw, i, inside)
    for i in range(4, layers + 4):
        for row in (0, 8):
            sweep_chunk(y1, y0, i, row, 1, 2.0, ew, i, wt, i, bw, i)
    lane = lax.broadcasted_iota(jnp.int32, (4, 128), 1)
    for m in range(groups):
        at = 2 * m + 4
        a = residual_chunk(y1, at, 4, 1, 2.0, ew, at, bw, at)
        b = residual_chunk(y1, at + 1, 4, 1, 2.0, ew, at + 1, bw, at + 1)
        for c in range(5):
            pair[m, c] = a[c] + b[c] if c < 4 else get(ew, (at,), 4) + get(ew, (at + 1,), 4)
    for m in range(groups):
        for c in range(5):
            rows = pair[m, c, pl.ds(0, 4, stride=2), :] + pair[m, c, pl.ds(1, 4, stride=2), :]
            mate = jnp.where(lane % 2 == 0, pltpu.roll(rows, 127, 1), pltpu.roll(rows, 1, 1))
            low[c, m, 0:4, :] = (rows + mate) * (0.5 if c < 4 else 0.125)
    for c in range(5):
        for q in range(groups // 2):
            packed = jnp.where(lane % 2 == 0, low[c, 2 * q, 0:4, :], low[c, 2 * q + 1, 0:4, :])
            at = 4 * (c * (groups // 2) + q)
            for out in (next_o, low_o):
                out[at : at + 4, :] = packed
    base = 20 * (groups // 2)
    up = core == 0
    for c in range(4):
        for j in range(8):
            at, i = base + 3 * (8 * c + j), 4 * chip + 2 + j
            next_o[at : at + 3, :] = pick(up, y1[c, i, 8:11, :], y1[c, i, 5:8, :])
        for j in range(4):
            at, i = base + 96 + 4 * c + j, 4 * chip + 4 + j
            next_o[at : at + 1, :] = pick(up, bw[c, i, 9:10, :], bw[c, i, 6:7, :])
    for j in range(10):
        e_o[j] = ew[2 * g + j]
        w_o[j] = wt[2 * g + j]
        for c in range(4):
            y_o[c, j] = y1[c, 2 * g + j]
            b_o[c, j] = bw[c, 2 * g + j]


def up_all(groups, devs, idx, low, by1, by2, swapped, y_i, b_i, e1, w1, x1, ew, wt, fw, own_edge, far_edge, sol_o, res_o,
           e2, w2, b2, z0, z1, b1, ya, yb, rep, va, vb):
    g, d = idx[0], idx[1]
    core = g % 2
    zero = jnp.zeros((32, 128), F32)
    lane = lax.broadcasted_iota(jnp.int32, (4, 128), 1)
    even = lane % 2 == 0

    for i in (0, 1, groups + 2, groups + 3):
        e2[i] = zero
        for c in range(4):
            z0[c, i] = zero
            z1[c, i] = zero
    for i in range(2, groups + 2):
        e2[i, 0:8, :] = zero[0:8]
        e2[i, 16:32, :] = zero[0:16]
        for c in range(4):
            b2[c, i, 0:8, :] = zero[0:8]
            b2[c, i, 16:32, :] = zero[0:16]
    tall = 20 * (groups // 2)
    by1_rows = tall + 112
    first_core = core == 0

    def from_second(by, offset, at, rows=4):
        a, b = by[at : at + rows, :], swapped[offset + at : offset + at + rows, :]
        return pick(first_core, a, b), pick(first_core, b, a)

    for away in (-2, -1, 0, 1, 2):
        row = 10 + 4 * away
        there = 1.0 if away == 0 else jnp.where((d + away >= 0) & (d + away < devs), 1.0, 0.0)
        for c in range(5):
            for q in range(groups // 2):
                at = 4 * (c * (groups // 2) + q)
                if away == 0:
                    packed = low[at : at + 4, :]
                else:
                    by, offset = (by1, 0) if away in (-1, 1) else (by2, by1_rows)
                    packed = from_second(by, offset, at)[0 if away < 0 else 1]
                first = jnp.where(even, packed, pltpu.roll(packed, 1, 1))
                second = jnp.where(even, pltpu.roll(packed, 127, 1), packed)
                if c == 4:
                    e2[2 * q + 2, row : row + 4, :] = first * there
                    e2[2 * q + 3, row : row + 4, :] = second * there
                else:
                    b2[c, 2 * q + 2, row : row + 4, :] = first
                    b2[c, 2 * q + 3, row : row + 4, :] = second
    for i in range(2, groups + 2):
        for row in (0, 8, 16):
            inside = rows_inside(row, 4 * d - 10, 4 * devs, 128)
            start_chunk(z0, i, row, 2, 4.0, e2, i, w2, i, b2, i, inside)
    here, other = z0, z1
    for k in range(COARSE - 1):
        for i in range(2, groups + 2):
            for row in (4, 12) if k < COARSE - 2 else (8,):
                sweep_chunk(other, here, i, row, 2, 4.0, e2, i, w2, i, b2, i)
        here, other = other, here
    z = here

    low_y, high_y = jnp.where(d > 0, 1.0, 0.0), jnp.where(d < devs - 1, 1.0, 0.0)

    def mid_halo(at, rows):
        a, b = from_second(by1, 0, at, rows), from_second(by1, 0, at + 2 * rows, rows)
        return pick(first_core, a[0], b[0]), pick(first_core, a[1], b[1])

    for c in range(4):
        for k in range(5):
            rows = z[c, g + k, 8:16, :]
            rep[c, k, pl.ds(0, 8, stride=2), :] = rows
            rep[c, k, pl.ds(1, 8, stride=2), :] = rows
    for c in range(4):
        for j in range(10):
            b1[c, j] = b_i[c, j]
            ya[c, j] = y_i[c, j]
        for j in range(2):
            before, after = mid_halo(tall + 96 + 4 * c + j, 1)
            b1[c, 4 + j, 1:2, :] = before
            b1[c, 4 + j, 14:15, :] = after
        for j in range(6):
            before, after = mid_halo(tall + 3 * (8 * c + j), 3)
            ya[c, 2 + j, 0:3, :] = before * low_y
            ya[c, 2 + j, 13:16, :] = after * high_y
        for j in range(10):
            ya[c, j] = ya[c, j] + rep[c, j // 2]
    for at in range(1, 9):
        for row in (0, 8) if 1 < at < 8 else (4,):
            sweep_chunk(yb, ya, at, row, 1, 2.0, e1, at, w1, at, b1, at)
    for at in range(2, 8):
        for row in (0, 8) if 2 < at < 7 else (4,):
            sweep_chunk(ya, yb, at, row, 1, 2.0, e1, at, w1, at, b1, at)

    low_x, high_x = jnp.where(g > 0, 1.0, 0.0), jnp.where(g < groups - 1, 1.0, 0.0)
    for c in range(4):
        for m in range(6):
            for k in range(2):
                both = spread(ya[c, 2 + m, 8 * k : 8 * k + 8, :])
                rows = slice(16 * k, 16 * k + 16)
                for layer in (2 * m, 2 * m + 1):
                    for n in range(2):
                        if 3 <= layer <= 8:
                            va[c, layer, n, rows, :] = both[n] + x1[c, layer - 2, n, rows, :]
                        elif 1 <= layer <= 10:
                            va[c, layer, n, rows, :] = both[n]
        for j in range(2):
            at = 64 + 18 * (2 * c + j)
            own, far = own_edge[at : at + 18, :], far_edge[at : at + 18, :]
            before = jnp.where(core == 0, far, own) * low_x
            after = jnp.where(core == 0, own, far) * high_x
            put(va, (c, 1 + j), 7, get(va, (c, 1 + j), 7, 18) + before)
            put(va, (c, 9 + j), 7, get(va, (c, 9 + j), 7, 18) + after)
    for at in range(2, 10):
        for row in (4, 12, 20) if 2 < at < 9 else (8, 16):
            sweep_chunk(vb, va, at, row, 1, 1.0, ew, at - 1, wt, at - 2, fw, at - 2)
    for at in range(3, 9):
        for row in (4, 12, 20) if 3 < at < 8 else (8, 16):
            sweep_chunk(va, vb, at, row, 1, 1.0, ew, at - 1, wt, at - 2, fw, at - 2)
    for i in range(4):
        for row in (8, 16):
            out = residual_chunk(va, i + 4, row, 1, 1.0, ew, i + 3, fw, i + 2)
            for c in range(4):
                sol_o[c, i, row - 8 : row, :] = get(va, (c, i + 4), row)
                res_o[c, i, row - 8 : row, :] = 0.5 * out[c]


def call(kernel, outs, scratch, *args):
    specs = [pl.BlockSpec(memory_space=pltpu.SMEM)] + [pl.BlockSpec(memory_space=pltpu.VMEM)] * (len(args) - 1)
    return pl.pallas_call(
        kernel,
        out_shape=[jax.ShapeDtypeStruct(shape, F32) for shape in outs],
        in_specs=specs,
        out_specs=[pl.BlockSpec(memory_space=pltpu.VMEM)] * len(outs),
        scratch_shapes=[pltpu.VMEM(shape, F32) for shape in scratch],
        compiler_params=pltpu.CompilerParams(vmem_limit_bytes=VMEM_LIMIT),
    )(*args)


def local(forcing, viscosity):
    groups, devs = lax.axis_size("grp"), lax.axis_size("dev")
    idx = jnp.stack([lax.axis_index("grp"), lax.axis_index("dev")]).astype(jnp.int32)
    swap = [(i, i ^ 1) for i in range(groups)]
    beside = [(i, (i + 1) % groups if i % 2 else (i - 1) % groups) for i in range(groups)]
    next_chip = [(i, (i - 2) % groups if i % 2 else (i + 2) % groups) for i in range(groups)]
    far_chip = [(i, (i + 4) % groups) for i in range(groups)]
    even = [(i, i ^ 1) for i in range(devs)]

    def pairs_of(to):
        every = [(g, d) for g in range(groups) for d in range(devs)]
        return [(g * devs + d, to(g, d)[0] * devs + to(g, d)[1]) for g, d in every]

    cross_pairs = pairs_of(lambda g, d: (beside[g][1], d) if 0 < g < groups - 1 else (g, d ^ 1))
    odd_pairs = pairs_of(lambda g, d: (g, d + 1 if d % 2 else d - 1) if 0 < d < devs - 1 else (g ^ 1, d))

    def along(step):
        def to(g, d):
            there = d - step if g % 2 else d + step
            return (g, there) if 0 <= there < devs else (g ^ 1, d)

        return pairs_of(to)

    f_first, f_last, visc = lax.optimization_barrier((forcing[:, 0:2], forcing[:, 2:4], viscosity))
    first = jnp.concatenate([f_first.reshape(8, 16, 256), visc[0:3]], axis=0)
    last = jnp.concatenate([f_last.reshape(8, 16, 256), visc[1:4]], axis=0)
    cross, inner = pick(idx[0] % 2 == 0, first, last), pick(idx[0] % 2 == 0, last, first)
    cross, inner = lax.optimization_barrier((cross, inner))
    cross, inner = lax.ppermute(cross, ("grp", "dev"), cross_pairs), lax.ppermute(inner, "grp", swap)
    to_even, to_odd = call(pack_second, [(SECOND_ROWS, 256)] * 2, [], idx, forcing, viscosity, cross, inner)
    from_odd, from_even = lax.ppermute(to_odd, ("grp", "dev"), odd_pairs), lax.ppermute(to_even, "dev", even)
    mid, pay, x1, ew, wt, fw = call(
        lambda *refs: fine_down(groups, devs, *refs),
        [(64, 256), (208, 256), (4, 8, 2, 32, 128), (10, 2, 32, 128), (8, 2, 32, 128), (4, 8, 2, 32, 128)],
        [(4, 8, 2, 32, 128), (10, 32, 256), (320, 128)],
        idx, forcing, viscosity, cross, inner, from_odd, from_even,
    )

    xco = lax.ppermute(pay, "grp", beside)
    c2 = lax.ppermute(mid, "grp", far_chip)
    cpm = lax.ppermute(mid, "grp", next_chip)
    partner = lax.ppermute(pay, "grp", swap)
    s1 = lax.ppermute(xco[:64], "grp", swap)
    s3 = lax.ppermute(jnp.concatenate([cpm, c2], axis=0), "grp", swap)

    layers = 2 * groups + 8
    tall = 20 * (groups // 2)
    to_next, low, y_w, b_w, e_w, w_w = call(
        lambda *refs: mid_down(groups, devs, *refs),
        [(tall + 112, 128), (tall, 128), (4, 10, 16, 128), (4, 10, 16, 128), (10, 16, 128), (10, 16, 128)],
        [(4, layers, 16, 128), (layers, 16, 128), (layers, 16, 128), (4, layers, 16, 128), (4, layers, 16, 128),
         (groups, 5, 8, 128), (5, groups, 8, 128)],
        idx, mid, partner, xco, cpm, c2, s1, s3,
    )

    by1 = lax.ppermute(to_next, ("grp", "dev"), along(1))
    by2 = lax.ppermute(low, ("grp", "dev"), along(2))
    swapped = lax.ppermute(jnp.concatenate([by1, by2], axis=0), "grp", swap)
    deep = groups + 4
    return tuple(call(
        lambda *refs: up_all(groups, devs, *refs),
        [(4, 4, 16, 256), (4, 4, 16, 256)],
        [(deep, 32, 128), (deep, 32, 128), (4, deep, 32, 128), (4, deep, 32, 128), (4, deep, 32, 128),
         (4, 10, 16, 128), (4, 10, 16, 128), (4, 10, 16, 128), (4, 5, 16, 128),
         (4, 12, 2, 32, 128), (4, 12, 2, 32, 128)],
        idx, low, by1, by2, swapped, y_w, b_w, e_w, w_w, x1, ew, wt, fw, partner, xco,
    ))


def solution(mesh):
    in_specs = (P(None, "grp", "dev", None), P("grp", "dev", None))
    out_specs = (P(None, "grp", "dev", None), P(None, "grp", "dev", None))
    return jax.shard_map(local, mesh=mesh, in_specs=in_specs, out_specs=out_specs, check_vma=False)
```
